32 devices in a mesh: tile: 8 (over z, core), bank: 4 (over y, x).
Axes of the slice: x: 2, y: 2, z: 4, core: 2. Of those that a mesh axis runs over, the one named last changes fastest.
Arguments:
- volume: bfloat16 [512, 256, 128], P('tile', 'bank'), may hold values from -6 to 6
- pick_list: int32 [3, 8, 4, 16], P(None, 'tile', 'bank'), may hold values from 0 to 511, as said below
- box_counts: int32 [8, 4], P('tile', 'bank'), may hold values from 1 to 16, as said below
- orientations: int32 [8, 4, 16, 128], P('tile', 'bank'), may hold values from 0 to 255, all different within a row
- orient_weight: int32 [8, 4, 16, 128], P('tile', 'bank'), may hold values from 1 to 4
- reference_bank: bfloat16 [256, 20, 4096], P('bank'), may hold values from -6 to 6
Outputs:
- class_sums: float32 [256, 20, 4096], P('bank')
- weight_sums: float32 [256, 20], P('bank')
The draws below stay inside these ranges and needn't reach their ends.
Inputs may be any that keep to these rules, and one draw needn't show every extreme that they name: pick_list[0, t, b, s] lies in [t * 64, (t + 1) * 64), pick_list[1, t, b, s] in [b * 64, (b + 1) * 64), and pick_list[2, t, b, s] in [0, 32]. `box_counts`: every device has at least one live slot and some device has all 16. The 128 orientations of a slot are distinct.
All inputs are finite; a program needn't handle non-finite values.
Results may differ from the reference program's by a relative error of at most 0.012.
Values may be sent and summed in bfloat16 or wider, within the bound.
No kernel may reach another device: no remote copies, remote signals or barrier semaphores. Data moves between devices by JAX's collectives and lax.ppermute only.
A program may use at most 128 MiB of HBM per device.

```python
import jax
import jax.numpy as jnp
from jax import lax

CX = 64
CY = 64
Z = 128
MAXB = 16
B = 96
L = 16
C = 20
R = 256
KO = 128
F = 4096
NX = 512
NY = 256
N_TILE = 8
N_BANK = 4


def draw_pick_list(key, part):
    tiles = NX // CX
    banks = NY // CY
    key_x, key_y, key_z = jax.random.split(key, 3)
    grid_shape = (tiles, banks, MAXB)
    pos_x = jax.random.randint(key_x, grid_shape, 0, CX) + (jnp.arange(tiles) * CX)[:, None, None]
    pos_y = jax.random.randint(key_y, grid_shape, 0, CY) + (jnp.arange(banks) * CY)[None, :, None]
    pos_z = jax.random.randint(key_z, grid_shape, 0, Z - B + 1)
    pos_x = pos_x.at[0, 0, 0].set(0).at[tiles - 1, banks - 1, 0].set(NX - 1)
    pos_y = pos_y.at[0, 0, 0].set(0).at[tiles - 1, banks - 1, 0].set(NY - 1)
    pos_z = pos_z.at[0, 0, 0].set(0).at[tiles - 1, banks - 1, 0].set(Z - B)
    return jnp.stack([pos_x, pos_y, pos_z]).astype(jnp.int32)


def draw_box_counts(key, part):
    tiles = NX // CX
    banks = NY // CY
    key_a, key_b = jax.random.split(key, 2)
    drawn = jax.random.randint(key_a, (tiles * banks,), 1, MAXB + 1)
    chosen = jax.random.randint(key_b, (), 0, tiles * banks)
    drawn = jnp.where(jnp.arange(tiles * banks) == chosen, MAXB, drawn)
    return drawn.reshape(tiles, banks).astype(jnp.int32)


def place_ends(array, key, low, largest):
    index_at = [jax.random.randint(jax.random.fold_in(key, axis), (), 0, length) for axis, length in enumerate(array.shape)]
    main_axis = array.shape.index(max(array.shape))
    next_to = index_at[:main_axis] + [(index_at[main_axis] + 1) % array.shape[main_axis]] + index_at[main_axis + 1:]
    return array.at[tuple(index_at)].set(low).at[tuple(next_to)].set(largest)


def level_of(key, shape, cuts, low, largest):
    loudness = 1.0
    for axis_at, parts in cuts:
        draws = jax.random.uniform(jax.random.fold_in(jax.random.fold_in(key, 6), axis_at), (parts,), jnp.float32, low / len(cuts), largest / len(cuts))
        loudness = loudness * jnp.repeat(jnp.exp(draws), shape[axis_at] // parts).reshape((-1,) + (1,) * (len(shape) - 1 - axis_at))
    return loudness


def picks_of(own_key, rows, count, top, lift):
    ranking = jax.random.permutation(jax.random.fold_in(own_key, 1), count)
    boost = ranking
    for power in range(3):
        boost = boost * boost // count
    boost = boost * lift // count
    tickets = jax.random.randint(jax.random.fold_in(own_key, 2), (rows, count), 0, 4096) + boost
    fixed_rows = jax.random.permutation(jax.random.fold_in(own_key, 3), rows)[jnp.arange(count) % rows]
    tickets = jnp.where(jnp.arange(rows)[:, None] == fixed_rows[None, :], 1 << 14, tickets)
    merit = tickets * count + jnp.arange(count)
    return lax.top_k(merit.astype(jnp.int32), top)[1].astype(jnp.int32)


def centred(key, extent, spread, most, shards=(), dtype=jnp.bfloat16):
    result = jax.random.normal(key, extent, jnp.float32) * spread
    if len(shards) > 0:
        result = level_of(key, extent, shards, -0.22, 0.18) * result
    return jnp.clip(result, min=-most, max=most).astype(dtype)


def setup_inputs(seed: int = 0) -> dict:
    key_of = jax.random.split(jax.random.key(seed), 7)
    return {
        "volume": centred(key_of[0], (NX, NY, Z), 1.0, 6.0, ((0, 8), (1, 4))),
        "pick_list": draw_pick_list(jax.random.fold_in(key_of[6], 71), 0),
        "box_counts": draw_box_counts(jax.random.fold_in(key_of[6], 71), 0),
        "orientations": picks_of(key_of[3], N_TILE * N_BANK * MAXB, R, KO, 0).reshape((N_TILE, N_BANK, MAXB, KO)),
        "orient_weight": place_ends(jax.random.randint(key_of[4], (N_TILE, N_BANK, MAXB, KO), 1, 5), jax.random.fold_in(key_of[4], 1), 1, 4).astype(jnp.int32),
        "reference_bank": centred(key_of[5], (R, C, F), 1.0, 6.0, ((0, 4),)),
    }


EPSILON = 1e-06

def fourier_table():
    samples = jnp.arange(B).astype(jnp.float32)
    terms = jnp.arange(L)
    frequency = jnp.where(terms <= L // 2, terms, terms - L // 2).astype(jnp.float32)
    angles = 2.0 * jnp.pi * frequency[:, None] * samples[None, :] / B
    table = jnp.where((terms <= L // 2)[:, None], jnp.cos(angles), jnp.sin(angles)) / jnp.sqrt(jnp.float32(B))
    table_half = table.astype(jnp.bfloat16)
    return (table_half, table_half.astype(jnp.float32))

def box_features(box_cube, table_half, table_full):
    first = jnp.dot(box_cube.reshape(B * B, B), table_half.T, preferred_element_type=jnp.float32).reshape(B, B, L)
    second = jnp.einsum('xyc,by->xbc', first, table_full, precision=lax.Precision.HIGHEST)
    third = jnp.einsum('xbc,ax->abc', second, table_full, precision=lax.Precision.HIGHEST)
    return third.reshape(L * L * L).astype(jnp.bfloat16)

def reference(volume, pick_list, box_counts, orientations, orient_weight, reference_bank):
    table_half, table_full = fourier_table()
    half_box = B // 2
    padded = jnp.pad(volume, ((half_box, half_box), (half_box, half_box), (0, 0)))
    coords = jnp.stack([pick_list[0].reshape(-1), pick_list[1].reshape(-1), pick_list[2].reshape(-1)], axis=1).astype(jnp.int32)

    def extract_one(corner):
        box_cube = lax.dynamic_slice(padded, (corner[0], corner[1], corner[2]), (B, B, B))
        return box_features(box_cube, table_half, table_full)
    features = lax.map(extract_one, coords)
    box_total = coords.shape[0]
    slot_index = jnp.arange(MAXB).astype(jnp.int32)
    live_slots = (slot_index[None, None, :] < box_counts[:, :, None]).reshape(-1)
    orient_rows = orientations.reshape(box_total, KO)
    weight_rows = orient_weight.reshape(box_total, KO).astype(jnp.float32)
    multiplicity = jnp.zeros((box_total, R), jnp.float32).at[jnp.arange(box_total)[:, None], orient_rows].add(weight_rows)
    multiplicity = jnp.where(live_slots[:, None], multiplicity, jnp.float32(0.0)).astype(jnp.bfloat16)
    feature_wide = features.astype(jnp.float32)
    box_norm = jnp.sqrt(lax.optimization_barrier(jnp.mean(feature_wide * feature_wide, axis=1)) + EPSILON)
    bank_wide = reference_bank.astype(jnp.float32)
    ref_norm = jnp.sqrt(lax.optimization_barrier(jnp.mean(bank_wide * bank_wide, axis=2)) + EPSILON)
    scores = jnp.einsum('if,rcf->irc', feature_wide, bank_wide)
    correl = scores / (F * box_norm[:, None, None] * ref_norm[None])
    weights = (multiplicity.astype(jnp.float32)[:, :, None] * jnp.maximum(correl, 0.0)).astype(jnp.bfloat16)
    weight_wide = weights.astype(jnp.float32)
    class_sums = jnp.einsum('irc,if->rcf', weight_wide, feature_wide)
    weight_sums = lax.optimization_barrier(jnp.sum(weight_wide, axis=0))
    return (class_sums, weight_sums)
```

```python
import functools

import jax
import jax.numpy as jnp
import numpy as np
from jax import lax
from jax.experimental import pallas as pl
from jax.experimental.pallas import tpu as pltpu
from jax.sharding import PartitionSpec as P

B = 96
L = 16
R = 256
F = L * L * L
HALF = B // 2
TERMS = L // 2
EPSILON = 1e-06
LIMIT = 60 * 1024 * 1024


def waves(count):
    steps = 2.0 * np.pi * np.outer(np.arange(TERMS + 1), np.arange(count)) / B
    return np.cos(steps) / np.sqrt(B), np.sin(steps) / np.sqrt(B)


def depth_tables(depth):
    cos, sin = waves(depth)
    first = np.concatenate([cos, sin[1:TERMS]], axis=0)
    second = np.concatenate([sin, -cos[1:TERMS]], axis=0)
    repeat = 128 // L
    return (
        np.tile(first.T, (1, repeat)).astype(np.float32),
        np.tile(second.T, (1, repeat)).astype(np.float32),
    )


def plane_table(wide, high):
    cos_x, sin_x = waves(wide)
    cos_y, sin_y = waves(high)
    along_x = np.concatenate([cos_x, sin_x[1:]], axis=0)
    along_y = np.concatenate([cos_y[1:], sin_y[1:]], axis=0)
    main = np.einsum("ax,by->abxy", along_x, along_y).reshape(-1, wide * high)
    order = np.concatenate([along_x[1:], along_x[:1]], axis=0)
    flat = np.einsum("ax,y->axy", order, cos_y[0]).reshape(-1, wide * high)
    rows = np.concatenate([main, flat], axis=0)
    pad = -rows.shape[0] % 16
    return np.concatenate([rows, np.zeros((pad, rows.shape[1]))], axis=0).astype(np.float32)


def spread(corners, lanes):
    boxes = corners.shape[1]
    box = lax.broadcasted_iota(jnp.int32, (boxes, lanes), 0)
    lane = lax.broadcasted_iota(jnp.int32, (boxes, lanes), 1)
    pick = jnp.where(lane // L == box, 1.0, 0.0).astype(jnp.bfloat16)
    return jnp.dot(corners, pick, preferred_element_type=jnp.float32)


def turns(terms, shift):
    turn = (terms * shift).astype(jnp.int32)
    turn = lax.rem(turn, B)
    angle = turn.astype(jnp.float32) * (2.0 * np.pi / B)
    return jnp.cos(angle), jnp.sin(angle)


def prepare(corners_ref, first_ref, second_ref, depth_ref, high_ref):
    depth, lanes = depth_ref.shape
    where = spread(corners_ref[...], lanes)
    start_y, start_z = where[1:2], where[2:3]
    lane = lax.rem(lax.broadcasted_iota(jnp.int32, (1, lanes), 1), L)
    term = jnp.where(lane <= TERMS, lane, lane - TERMS).astype(jnp.float32)
    cos, sin = turns(term, start_z)
    copies = lanes // first_ref.shape[1]
    first = jnp.concatenate([first_ref[...]] * copies, axis=1)
    second = jnp.concatenate([second_ref[...]] * copies, axis=1)
    z = lax.broadcasted_iota(jnp.int32, (depth, lanes), 0).astype(jnp.float32) - start_z
    table = jnp.where((z >= 0) & (z < B), first * cos + second * sin, 0.0)
    depth_ref[...] = table.astype(jnp.bfloat16)
    y = lax.broadcasted_iota(jnp.int32, high_ref.shape, 0).astype(jnp.float32) - start_y
    high_ref[...] = jnp.where((y >= 0) & (y < B), 1.0, 0.0)
    return where[0:1]


def add_rows(voxels, base, start_x, depth_ref, high_ref, part_ref, plane):
    count, high, depth = voxels.shape
    for x in range(0, count, 4):
        rows = voxels[x : x + 4].reshape(4 * high, depth)
        first = jnp.dot(rows, depth_ref[...], preferred_element_type=jnp.float32)
        for i in range(4):
            at = (base + (x + i)).astype(jnp.float32) - start_x
            live = high_ref[...] * jnp.where((at >= 0) & (at < B), 1.0, 0.0)
            kept = first[i * high : (i + 1) * high] * live
            part_ref[pl.ds((x + i) * high, high), :] = kept.astype(jnp.bfloat16)
    return jnp.dot(plane, part_ref[...], preferred_element_type=jnp.float32)


def near_kernel(
    corners_ref, first_ref, second_ref, volume_ref, plane_ref, total_ref,
    depth_ref, high_ref, start_ref, part_ref, *, offset,
):
    step = pl.program_id(0)

    @pl.when(step == 0)
    def _():
        start_ref[...] = prepare(corners_ref, first_ref, second_ref, depth_ref, high_ref)

    base = offset + step * volume_ref.shape[0]
    added = add_rows(
        volume_ref[...], base, start_ref[...], depth_ref, high_ref, part_ref, plane_ref[...]
    )

    @pl.when(step == 0)
    def _():
        total_ref[...] = added

    @pl.when(step > 0)
    def _():
        total_ref[...] += added


def rotate(total, start_x, start_y):
    lanes = total.shape[1]
    term = (lax.broadcasted_iota(jnp.int32, (TERMS, lanes), 0) + 1).astype(jnp.float32)
    cos_x, sin_x = turns(term, start_x)
    cos_y, sin_y = turns(term, start_y)
    blocks = 2 * TERMS + 1
    main = blocks * 2 * TERMS
    flat_cos = total[main : main + TERMS]
    flat_sin = total[main + TERMS : main + 2 * TERMS]
    flat_zero = total[main + 2 * TERMS : main + 2 * TERMS + 1]
    flats = (
        [flat_zero]
        + [flat_cos[j : j + 1] for j in range(TERMS)]
        + [flat_sin[j : j + 1] for j in range(TERMS)]
    )
    last = lax.broadcasted_iota(jnp.int32, (TERMS, lanes), 0) == TERMS - 1
    turned = []
    for a in range(blocks):
        cos = total[a * 2 * TERMS : a * 2 * TERMS + TERMS]
        sin = total[a * 2 * TERMS + TERMS : (a + 1) * 2 * TERMS]
        low = cos * cos_y + sin * sin_y
        high = sin * cos_y - cos * sin_y
        turned.append((low, jnp.where(last, flats[a], high)))
    rows = [None] * (2 * TERMS)
    rows[0] = turned[0]
    for j in range(1, TERMS + 1):
        c, s = cos_x[j - 1 : j], sin_x[j - 1 : j]
        cos, sin = turned[j], turned[TERMS + j]
        rows[j] = tuple(u * c + v * s for u, v in zip(cos, sin))
        if j < TERMS:
            rows[TERMS + j] = tuple(v * c - u * s for u, v in zip(cos, sin))
    return jnp.concatenate([half for pair in rows for half in pair], axis=0)


def far_kernel(
    corners_ref, first_ref, second_ref, low_ref, high_voxels_ref, plane_ref, near_ref,
    left_ref, own_ref, right_ref,
    depth_ref, high_ref, start_ref, part_ref, total_ref, *, half, gap,
):
    step = pl.program_id(0)

    @pl.when(step == 0)
    def _():
        start_ref[...] = prepare(corners_ref, first_ref, second_ref, depth_ref, high_ref)
        total_ref[...] = near_ref[...]

    count = low_ref.shape[0]
    base = step * count + jnp.where(step < half, 0, gap)
    voxels = jnp.where(step < half, low_ref[...], high_voxels_ref[...])
    total_ref[...] += add_rows(
        voxels, base, start_ref[...], depth_ref, high_ref, part_ref, plane_ref[...]
    )

    @pl.when(step == 2 * half - 1)
    def _():
        where = spread(corners_ref[...], total_ref.shape[1])
        rows = rotate(total_ref[...], where[0:1], where[1:2])
        width = left_ref.shape[1]
        left_ref[...] = rows[:, :width].astype(jnp.bfloat16)
        own_ref[...] = rows[:, width : 2 * width]
        right_ref[...] = rows[:, 2 * width :].astype(jnp.bfloat16)


def join_kernel(own_ref, left_ref, right_ref, multiplicity_ref, out_ref, wide_ref):
    total = own_ref[...] + left_ref[...].astype(jnp.float32) + right_ref[...].astype(jnp.float32)
    total = total.astype(jnp.bfloat16)
    rows, lanes = total.shape
    slots = lanes // L
    k = lax.broadcasted_iota(jnp.int32, (lanes, L * L), 0)
    lane = lax.broadcasted_iota(jnp.int32, (lanes, L * L), 1)
    gap = k - lax.rem(lane, L)
    row = lax.rem(lax.broadcasted_iota(jnp.int32, (rows, L * L), 0), L)
    place = jnp.where(row == L - 1, 0, row + 1)
    keep = jnp.where(
        place == lax.broadcasted_iota(jnp.int32, (rows, L * L), 1) // L, 1.0, 0.0
    )
    sums = jnp.where(
        lax.broadcasted_iota(jnp.int32, (L, rows), 1) // L
        == lax.broadcasted_iota(jnp.int32, (L, rows), 0),
        1.0,
        0.0,
    ).astype(jnp.bfloat16)
    for s in range(slots):
        copies = jnp.where(gap == s * L, 1.0, 0.0).astype(jnp.bfloat16)
        spread_rows = jnp.dot(total, copies, preferred_element_type=jnp.float32) * keep
        feature = jnp.dot(
            sums, spread_rows.astype(jnp.bfloat16), preferred_element_type=jnp.float32
        )
        for a in range(L):
            wide_ref[s : s + 1, a * L * L : (a + 1) * L * L] = feature[a : a + 1]
    wide = wide_ref[...]
    norm = jnp.sqrt(jnp.mean(wide * wide, axis=1, keepdims=True) + EPSILON)
    high = norm.astype(jnp.bfloat16).astype(jnp.float32)
    tail = lax.broadcasted_iota(jnp.int32, (slots, 128), 1)
    tail = jnp.where(tail == 0, high, jnp.where(tail == 1, norm - high, 0.0))
    out_ref[:, :F] = wide.astype(jnp.bfloat16)
    out_ref[:, F : F + R] = multiplicity_ref[...]
    out_ref[:, F + R :] = tail.astype(jnp.bfloat16)


def score_kernel(
    rows_ref, multiplicity_ref, norm_ref, bank_ref, out_ref, sums_ref, turned_ref,
):
    step = pl.program_id(0)

    @pl.when(step == 0)
    def _():
        turned_ref[...] = rows_ref[...].T

    count, orients, width = bank_ref.shape
    bank = bank_ref[...].reshape(count * orients, width)
    scores = jnp.dot(bank, turned_ref[...], preferred_element_type=jnp.float32)
    wide = bank.astype(jnp.float32)
    bank_norm = jnp.sqrt(jnp.mean(wide * wide, axis=1, keepdims=True) + EPSILON)
    correl = scores / (F * norm_ref[...] * bank_norm)
    multiplicity = jnp.concatenate([multiplicity_ref[...].astype(jnp.float32)] * count, axis=0)
    weights = (multiplicity * jnp.maximum(correl, 0.0)).astype(jnp.bfloat16)
    total = jnp.dot(weights, rows_ref[...], preferred_element_type=jnp.float32)
    out_ref[...] = total.reshape(out_ref.shape)
    sums = jnp.sum(weights.astype(jnp.float32), axis=1, keepdims=True)
    sums_ref[...] = sums.reshape(sums_ref.shape)


def score_plain(rows, multiplicity, norm, bank):
    scores = jnp.einsum("if,rcf->irc", rows, bank, preferred_element_type=jnp.float32)
    wide = bank.astype(jnp.float32)
    bank_norm = jnp.sqrt(jnp.mean(wide * wide, axis=2) + EPSILON)
    correl = scores / (F * norm[:, None, None] * bank_norm[None])
    weights = (multiplicity.astype(jnp.float32)[:, :, None] * jnp.maximum(correl, 0.0)).astype(
        jnp.bfloat16
    )
    class_sums = jnp.einsum("irc,if->rcf", weights, rows, preferred_element_type=jnp.float32)
    return class_sums, jnp.sum(weights.astype(jnp.float32), axis=0)


def steps_of(axis, by):
    count = lax.axis_size(axis)
    return [(i, i + by) for i in range(count) if 0 <= i + by < count]


def shifted(value, axis, by):
    return lax.ppermute(value, axis, steps_of(axis, by))


def gather_rows(mine):
    tiles, banks = lax.axis_size("tile"), lax.axis_size("bank")
    blocks = [mine]
    if tiles % 2 == 0:
        for by in range(2, tiles, 2):
            blocks.append(
                lax.ppermute(mine, "tile", [(i, (i + by) % tiles) for i in range(tiles)])
            )
    line = jnp.concatenate(blocks, axis=0)
    if banks == 4:
        along_x = lax.ppermute(line, "bank", [(0, 1), (1, 0), (2, 3), (3, 2)])
        along_y = lax.ppermute(line, "bank", [(0, 2), (2, 0), (1, 3), (3, 1)])
        half = line.shape[0] // 2
        across_y = lax.ppermute(along_x[:half], "bank", [(0, 2), (2, 0), (1, 3), (3, 1)])
        across_x = lax.ppermute(along_y[half:], "bank", [(0, 1), (1, 0), (2, 3), (3, 2)])
        line = jnp.concatenate([line, along_x, along_y, across_y, across_x], axis=0)
    else:
        line = lax.all_gather(line, "bank", axis=0, tiled=True)
    if tiles % 2 == 0:
        other = lax.ppermute(line, "tile", [(i, i ^ 1) for i in range(tiles)])
        return jnp.concatenate([line, other], axis=0)
    return lax.all_gather(line, "tile", axis=0, tiled=True)


def score_local(rows, reference_bank):
    local_rows, classes, width = reference_bank.shape
    row_start = lax.axis_index("bank") * local_rows
    multiplicity = lax.dynamic_slice_in_dim(rows, F + row_start, local_rows, 1)
    norm = rows[:, F + R].astype(jnp.float32) + rows[:, F + R + 1].astype(jnp.float32)
    features = rows[:, :F]
    boxes = rows.shape[0]
    if boxes > 1024 or classes % 4:
        return score_plain(features, multiplicity, norm, reference_bank)
    group = 4
    out, sums = pl.pallas_call(
        score_kernel,
        grid=(classes // group,),
        in_specs=[
            pl.BlockSpec((boxes, F), lambda i: (0, 0)),
            pl.BlockSpec((local_rows, boxes), lambda i: (0, 0)),
            pl.BlockSpec((1, boxes), lambda i: (0, 0)),
            pl.BlockSpec((group, local_rows, width), lambda i: (i, 0, 0)),
        ],
        out_specs=[
            pl.BlockSpec((group, local_rows, width), lambda i: (i, 0, 0)),
            pl.BlockSpec((group, local_rows, 1), lambda i: (i, 0, 0)),
        ],
        out_shape=[
            jax.ShapeDtypeStruct((classes, local_rows, width), jnp.float32),
            jax.ShapeDtypeStruct((classes, local_rows, 1), jnp.float32),
        ],
        scratch_shapes=[pltpu.VMEM((F, boxes), jnp.bfloat16)],
        compiler_params=pltpu.CompilerParams(vmem_limit_bytes=LIMIT),
        cost_estimate=pl.CostEstimate(
            flops=4 * boxes * classes * local_rows * width,
            bytes_accessed=6 * classes * local_rows * width,
            transcendentals=0,
        ),
        name="score",
    )(features, multiplicity.T, norm[None], jnp.transpose(reference_bank, (1, 0, 2)))
    return jnp.transpose(out, (1, 0, 2)), jnp.transpose(sums[:, :, 0], (1, 0))


def body(volume, pick_list, box_counts, orientations, orient_weight, reference_bank):
    wide, high, depth = volume.shape
    slots = pick_list.shape[3]
    low = shifted(volume[wide - HALF :], "tile", 1)
    top = shifted(volume[:HALF], "tile", -1)

    corner_x = pick_list[0, 0, 0] - lax.axis_index("tile") * wide
    corner_y = pick_list[1, 0, 0] - lax.axis_index("bank") * high - HALF
    own = jnp.stack([corner_x, corner_y, pick_list[2, 0, 0]])
    before = shifted(own, "bank", 1)
    after = shifted(own, "bank", -1)
    step = jnp.array([0, high, 0], jnp.int32)[:, None]
    corners = jnp.concatenate([before - step, own, after + step], axis=1)
    corners = jnp.pad(corners, ((0, 5), (0, 128 - 3 * slots))).astype(jnp.bfloat16)

    first, second = depth_tables(depth)
    plane = jnp.asarray(plane_table(wide + 2 * HALF, high), jnp.bfloat16)
    modes, lanes = plane.shape[0], 3 * slots * L
    unit = 16
    scratch = [
        pltpu.VMEM((depth, lanes), jnp.bfloat16),
        pltpu.VMEM((high, lanes), jnp.float32),
        pltpu.VMEM((1, lanes), jnp.float32),
        pltpu.VMEM((unit * high, lanes), jnp.bfloat16),
    ]
    whole = [
        pl.BlockSpec((8, 128), lambda i: (0, 0)),
        pl.BlockSpec((depth, 128), lambda i: (0, 0)),
        pl.BlockSpec((depth, 128), lambda i: (0, 0)),
    ]
    params = pltpu.CompilerParams(vmem_limit_bytes=LIMIT)
    near = pl.pallas_call(
        functools.partial(near_kernel, offset=HALF),
        grid=(wide // unit,),
        in_specs=whole
        + [
            pl.BlockSpec((unit, high, depth), lambda i: (i, 0, 0)),
            pl.BlockSpec((modes, unit * high), lambda i: (0, HALF // unit + i)),
        ],
        out_specs=pl.BlockSpec((modes, lanes), lambda i: (0, 0)),
        out_shape=jax.ShapeDtypeStruct((modes, lanes), jnp.float32),
        scratch_shapes=scratch,
        compiler_params=params,
        cost_estimate=pl.CostEstimate(
            flops=2 * wide * high * lanes * (depth + modes), bytes_accessed=8000000, transcendentals=0
        ),
        name="near_rows",
    )(corners, first, second, volume, plane)
    half = HALF // unit
    skip = wide // unit
    left, mid, right = pl.pallas_call(
        functools.partial(far_kernel, half=half, gap=wide),
        grid=(2 * half,),
        in_specs=whole
        + [
            pl.BlockSpec((unit, high, depth), lambda i: (jnp.minimum(i, half - 1), 0, 0)),
            pl.BlockSpec((unit, high, depth), lambda i: (jnp.maximum(i - half, 0), 0, 0)),
            pl.BlockSpec(
                (modes, unit * high), lambda i: (0, jnp.where(i < half, i, i + skip))
            ),
            pl.BlockSpec((modes, lanes), lambda i: (0, 0)),
        ],
        out_specs=[pl.BlockSpec((L * L, slots * L), lambda i: (0, 0))] * 3,
        out_shape=[
            jax.ShapeDtypeStruct((L * L, slots * L), jnp.bfloat16),
            jax.ShapeDtypeStruct((L * L, slots * L), jnp.float32),
            jax.ShapeDtypeStruct((L * L, slots * L), jnp.bfloat16),
        ],
        scratch_shapes=scratch + [pltpu.VMEM((modes, lanes), jnp.float32)],
        compiler_params=params,
        name="far_rows",
    )(corners, first, second, low, top, plane, near)
    from_after = shifted(left, "bank", -1)
    from_before = shifted(right, "bank", 1)

    live_slots = jnp.arange(slots) < box_counts[0, 0]
    matches = orientations[0, 0][:, :, None] == jnp.arange(R)[None, None, :]
    multiplicity = jnp.sum(
        jnp.where(matches, orient_weight[0, 0][:, :, None].astype(jnp.float32), 0.0), axis=1
    )
    multiplicity = jnp.where(live_slots[:, None], multiplicity, 0.0).astype(jnp.bfloat16)
    mine = pl.pallas_call(
        join_kernel,
        out_shape=jax.ShapeDtypeStruct((slots, F + R + 128), jnp.bfloat16),
        scratch_shapes=[pltpu.VMEM((slots, F), jnp.float32)],
        compiler_params=params,
        name="join",
    )(mid, from_after, from_before, multiplicity)
    return score_local(gather_rows(mine), reference_bank)


def solution(mesh):
    in_specs = (
        P("tile", "bank", None),
        P(None, "tile", "bank", None),
        P("tile", "bank"),
        P("tile", "bank", None, None),
        P("tile", "bank", None, None),
        P("bank", None, None),
    )
    out_specs = (P("bank", None, None), P("bank", None))
    return jax.shard_map(body, mesh=mesh, in_specs=in_specs, out_specs=out_specs, check_vma=False)
```

```python
import functools

import jax
import jax.numpy as jnp
import numpy as np
from jax import lax
from jax.experimental import pallas as pl
from jax.experimental.pallas import tpu as pltpu
from jax.sharding import PartitionSpec as P

B = 96
L = 16
R = 256
F = L * L * L
HALF = B // 2
TERMS = L // 2
EPSILON = 1e-06
MIB = 1024 * 1024


def waves(count):
    steps = 2.0 * np.pi * np.outer(np.arange(TERMS + 1), np.arange(count)) / B
    return np.cos(steps) / np.sqrt(B), np.sin(steps) / np.sqrt(B)


def depth_tables(depth):
    cos, sin = waves(depth)
    first = np.concatenate([cos, sin[1:TERMS]], axis=0)
    second = np.concatenate([sin, -cos[1:TERMS]], axis=0)
    repeat = 128 // L
    return (
        np.tile(first.T, (1, repeat)).astype(np.float32),
        np.tile(second.T, (1, repeat)).astype(np.float32),
    )


def plane_table(wide, high):
    cos_x, sin_x = waves(wide)
    cos_y, sin_y = waves(high)
    along_x = np.concatenate([cos_x, sin_x[1:]], axis=0)
    along_y = np.concatenate([cos_y[1:], sin_y[1:]], axis=0)
    main = np.einsum("ax,by->abxy", along_x, along_y).reshape(-1, wide * high)
    order = np.concatenate([along_x[1:], along_x[:1]], axis=0)
    flat = np.einsum("ax,y->axy", order, cos_y[0]).reshape(-1, wide * high)
    rows = np.concatenate([main, flat], axis=0)
    pad = -rows.shape[0] % 16
    return np.concatenate([rows, np.zeros((pad, rows.shape[1]))], axis=0).astype(np.float32)


def spread(corners, lanes):
    boxes = corners.shape[1]
    box = lax.broadcasted_iota(jnp.int32, (boxes, lanes), 0)
    lane = lax.broadcasted_iota(jnp.int32, (boxes, lanes), 1)
    pick = jnp.where(lane // L == box, 1.0, 0.0).astype(jnp.bfloat16)
    return jnp.dot(corners, pick, preferred_element_type=jnp.float32)


def turns(terms, shift):
    turn = (terms * shift).astype(jnp.int32)
    turn = lax.rem(turn, B)
    angle = turn.astype(jnp.float32) * (2.0 * np.pi / B)
    return jnp.cos(angle), jnp.sin(angle)


def prepare(corners_ref, first_ref, second_ref, depth_ref, high_ref):
    depth, lanes = depth_ref.shape
    where = spread(corners_ref[...], lanes)
    start_y, start_z = where[1:2], where[2:3]
    lane = lax.rem(lax.broadcasted_iota(jnp.int32, (1, lanes), 1), L)
    term = jnp.where(lane <= TERMS, lane, lane - TERMS).astype(jnp.float32)
    cos, sin = turns(term, start_z)
    copies = lanes // first_ref.shape[1]
    first = jnp.concatenate([first_ref[...]] * copies, axis=1)
    second = jnp.concatenate([second_ref[...]] * copies, axis=1)
    z = lax.broadcasted_iota(jnp.int32, (depth, lanes), 0).astype(jnp.float32) - start_z
    table = jnp.where((z >= 0) & (z < B), first * cos + second * sin, 0.0)
    depth_ref[...] = table.astype(jnp.bfloat16)
    y = lax.broadcasted_iota(jnp.int32, high_ref.shape, 0).astype(jnp.float32) - start_y
    high_ref[...] = jnp.where((y >= 0) & (y < B), 1.0, 0.0)
    return where[0:1]


def add_rows(voxels, base, start_x, depth_ref, high_ref, part_ref, plane):
    count, high, depth = voxels.shape
    for x in range(0, count, 4):
        rows = voxels[x : x + 4].reshape(4 * high, depth)
        first = jnp.dot(rows, depth_ref[...], preferred_element_type=jnp.float32)
        for i in range(4):
            at = (base + (x + i)).astype(jnp.float32) - start_x
            live = high_ref[...] * jnp.where((at >= 0) & (at < B), 1.0, 0.0)
            kept = first[i * high : (i + 1) * high] * live
            part_ref[pl.ds((x + i) * high, high), :] = kept.astype(jnp.bfloat16)
    return jnp.dot(plane, part_ref[...], preferred_element_type=jnp.float32)


def near_kernel(
    corners_ref, first_ref, second_ref, volume_ref, plane_ref, total_ref,
    depth_ref, high_ref, start_ref, part_ref, *, offset,
):
    step = pl.program_id(0)

    @pl.when(step == 0)
    def _():
        start_ref[...] = prepare(corners_ref, first_ref, second_ref, depth_ref, high_ref)

    base = offset + step * volume_ref.shape[0]
    added = add_rows(
        volume_ref[...], base, start_ref[...], depth_ref, high_ref, part_ref, plane_ref[...]
    )

    @pl.when(step == 0)
    def _():
        total_ref[...] = added

    @pl.when(step > 0)
    def _():
        total_ref[...] += added


def rotate(total, start_x, start_y):
    lanes = total.shape[1]
    term = (lax.broadcasted_iota(jnp.int32, (TERMS, lanes), 0) + 1).astype(jnp.float32)
    cos_x, sin_x = turns(term, start_x)
    cos_y, sin_y = turns(term, start_y)
    blocks = 2 * TERMS + 1
    main = blocks * 2 * TERMS
    flat_cos = total[main : main + TERMS]
    flat_sin = total[main + TERMS : main + 2 * TERMS]
    flat_zero = total[main + 2 * TERMS : main + 2 * TERMS + 1]
    flats = (
        [flat_zero]
        + [flat_cos[j : j + 1] for j in range(TERMS)]
        + [flat_sin[j : j + 1] for j in range(TERMS)]
    )
    last = lax.broadcasted_iota(jnp.int32, (TERMS, lanes), 0) == TERMS - 1
    turned = []
    for a in range(blocks):
        cos = total[a * 2 * TERMS : a * 2 * TERMS + TERMS]
        sin = total[a * 2 * TERMS + TERMS : (a + 1) * 2 * TERMS]
        low = cos * cos_y + sin * sin_y
        high = sin * cos_y - cos * sin_y
        turned.append((low, jnp.where(last, flats[a], high)))
    rows = [None] * (2 * TERMS)
    rows[0] = turned[0]
    for j in range(1, TERMS + 1):
        c, s = cos_x[j - 1 : j], sin_x[j - 1 : j]
        cos, sin = turned[j], turned[TERMS + j]
        rows[j] = tuple(u * c + v * s for u, v in zip(cos, sin))
        if j < TERMS:
            rows[TERMS + j] = tuple(v * c - u * s for u, v in zip(cos, sin))
    return jnp.concatenate([half for pair in rows for half in pair], axis=0)


def far_kernel(
    corners_ref, first_ref, second_ref, low_ref, high_voxels_ref, plane_ref, near_ref,
    left_ref, own_ref, right_ref,
    depth_ref, high_ref, start_ref, part_ref, total_ref, *, half, gap,
):
    step = pl.program_id(0)

    @pl.when(step == 0)
    def _():
        start_ref[...] = prepare(corners_ref, first_ref, second_ref, depth_ref, high_ref)
        total_ref[...] = near_ref[...]

    count = low_ref.shape[0]
    base = step * count + jnp.where(step < half, 0, gap)
    voxels = jnp.where(step < half, low_ref[...], high_voxels_ref[...])
    total_ref[...] += add_rows(
        voxels, base, start_ref[...], depth_ref, high_ref, part_ref, plane_ref[...]
    )

    @pl.when(step == 2 * half - 1)
    def _():
        where = spread(corners_ref[...], total_ref.shape[1])
        rows = rotate(total_ref[...], where[0:1], where[1:2])
        width = left_ref.shape[1]
        left_ref[...] = rows[:, :width].astype(jnp.bfloat16)
        own_ref[...] = rows[:, width : 2 * width]
        right_ref[...] = rows[:, 2 * width :].astype(jnp.bfloat16)


def join_kernel(own_ref, left_ref, right_ref, multiplicity_ref, out_ref, wide_ref):
    total = own_ref[...] + left_ref[...].astype(jnp.float32) + right_ref[...].astype(jnp.float32)
    total = total.astype(jnp.bfloat16)
    rows, lanes = total.shape
    slots = lanes // L
    k = lax.broadcasted_iota(jnp.int32, (lanes, L * L), 0)
    lane = lax.broadcasted_iota(jnp.int32, (lanes, L * L), 1)
    gap = k - lax.rem(lane, L)
    row = lax.rem(lax.broadcasted_iota(jnp.int32, (rows, L * L), 0), L)
    place = jnp.where(row == L - 1, 0, row + 1)
    keep = jnp.where(
        place == lax.broadcasted_iota(jnp.int32, (rows, L * L), 1) // L, 1.0, 0.0
    )
    sums = jnp.where(
        lax.broadcasted_iota(jnp.int32, (L, rows), 1) // L
        == lax.broadcasted_iota(jnp.int32, (L, rows), 0),
        1.0,
        0.0,
    ).astype(jnp.bfloat16)
    for s in range(slots):
        copies = jnp.where(gap == s * L, 1.0, 0.0).astype(jnp.bfloat16)
        spread_rows = jnp.dot(total, copies, preferred_element_type=jnp.float32) * keep
        feature = jnp.dot(
            sums, spread_rows.astype(jnp.bfloat16), preferred_element_type=jnp.float32
        )
        for a in range(L):
            wide_ref[s : s + 1, a * L * L : (a + 1) * L * L] = feature[a : a + 1]
    wide = wide_ref[...]
    norm = jnp.sqrt(jnp.mean(wide * wide, axis=1, keepdims=True) + EPSILON)
    high = norm.astype(jnp.bfloat16).astype(jnp.float32)
    tail = lax.broadcasted_iota(jnp.int32, (slots, 128), 1)
    tail = jnp.where(tail == 0, high, jnp.where(tail == 1, norm - high, 0.0))
    out_ref[:, :F] = wide.astype(jnp.bfloat16)
    out_ref[:, F : F + R] = multiplicity_ref[...]
    out_ref[:, F + R :] = tail.astype(jnp.bfloat16)


def load_blocks(blocks, rows_ref, tail_ref, sems):
    copies, at = [], 0
    for k, block in enumerate(blocks):
        count = block.shape[0]
        place = pl.ds(at, count)
        copies.append(
            pltpu.make_async_copy(block.at[:, pl.ds(0, F)], rows_ref.at[place], sems.at[2 * k])
        )
        copies.append(
            pltpu.make_async_copy(
                block.at[:, pl.ds(F, block.shape[1] - F)], tail_ref.at[place], sems.at[2 * k + 1]
            )
        )
        at += count
    for copy in copies:
        copy.start()
    for copy in copies:
        copy.wait()


def read_tail(bank_ref, tail, tail_ref, multiplicity_ref, norm_ref, orients):
    tail_ref[...] = tail.astype(jnp.float32).T
    start = pl.multiple_of(bank_ref[0] * orients, orients)
    multiplicity_ref[...] = tail_ref[pl.ds(start, orients), :]
    norm_ref[...] = tail_ref[R : R + 1, :] + tail_ref[R + 1 : R + 2, :]


def weigh(bank_rows, rows, multiplicity, norm, count):
    scores = lax.dot_general(
        bank_rows, rows, (((1,), (1,)), ((), ())), preferred_element_type=jnp.float32
    )
    wide = bank_rows.astype(jnp.float32)
    bank_norm = jnp.sqrt(jnp.mean(wide * wide, axis=1, keepdims=True) + EPSILON)
    correl = scores / (F * norm * bank_norm)
    multiplicity = jnp.concatenate([multiplicity] * count, axis=0)
    return (multiplicity * jnp.maximum(correl, 0.0)).astype(jnp.bfloat16)


def weigh_kernel(index_ref, *refs, blocks):
    sources, (bank_ref, out_ref) = refs[:blocks], refs[blocks : blocks + 2]
    rows_ref, tail_ref, turned_ref, multiplicity_ref, norm_ref, sems = refs[blocks + 2 :]
    count, orients, width = bank_ref.shape

    @pl.when(pl.program_id(0) == 0)
    def _():
        load_blocks(sources, rows_ref, tail_ref, sems)
        read_tail(index_ref, tail_ref[...], turned_ref, multiplicity_ref, norm_ref, orients)

    bank = bank_ref[...].reshape(count * orients, width)
    weights = weigh(bank, rows_ref[...], multiplicity_ref[...], norm_ref[...], count)
    out_ref[...] = weights.reshape(out_ref.shape)


def sum_kernel(index_ref, *refs, early, blocks, late):
    parts, sources = refs[:early], refs[early : early + blocks]
    bank_ref, out_ref, sums_ref = refs[early + blocks : early + blocks + 3]
    rows_ref, tail_ref, turned_ref, multiplicity_ref, norm_ref, sems = refs[early + blocks + 3 :]
    count, orients, width = bank_ref.shape
    boxes = rows_ref.shape[0]
    step = pl.program_id(0)

    @pl.when(step == 0)
    def _():
        load_blocks(sources, rows_ref, tail_ref, sems)
        read_tail(
            index_ref, tail_ref[boxes - late :], turned_ref, multiplicity_ref, norm_ref, orients
        )

    bank = bank_ref[...].reshape(count * orients, width)
    weights = weigh(
        bank, rows_ref[boxes - late :, :], multiplicity_ref[...], norm_ref[...], count
    )
    known = [part[...].reshape(count * orients, part.shape[2]) for part in parts]
    weights = jnp.concatenate(known + [weights], axis=1)
    total = jnp.dot(weights, rows_ref[...], preferred_element_type=jnp.float32)
    out_ref[...] = total.reshape(out_ref.shape)
    ones = jnp.ones((8, boxes), jnp.bfloat16)
    sums = lax.dot_general(
        ones, weights, (((1,), (1,)), ((), ())), preferred_element_type=jnp.float32
    )
    for c in range(count):
        sums_ref[pl.ds(step * count + c, 1), :] = sums[:1, c * orients : (c + 1) * orients]


def score_plain(rows, bank):
    local_rows = bank.shape[0]
    start = F + lax.axis_index("bank") * local_rows
    multiplicity = lax.dynamic_slice_in_dim(rows, start, local_rows, 1).astype(jnp.float32)
    norm = rows[:, F + R].astype(jnp.float32) + rows[:, F + R + 1].astype(jnp.float32)
    features = rows[:, :F]
    scores = jnp.einsum("if,rcf->irc", features, bank, preferred_element_type=jnp.float32)
    wide = bank.astype(jnp.float32)
    bank_norm = jnp.sqrt(jnp.mean(wide * wide, axis=2) + EPSILON)
    correl = scores / (F * norm[:, None, None] * bank_norm[None])
    weights = (multiplicity[:, :, None] * jnp.maximum(correl, 0.0)).astype(jnp.bfloat16)
    class_sums = jnp.einsum("irc,if->rcf", weights, features, preferred_element_type=jnp.float32)
    return class_sums, jnp.sum(weights.astype(jnp.float32), axis=0)


def steps_of(axis, by):
    count = lax.axis_size(axis)
    return [(i, i + by) for i in range(count) if 0 <= i + by < count]


def shifted(value, axis, by):
    return lax.ppermute(value, axis, steps_of(axis, by))


def gather_score(mine, reference_bank):
    tiles, banks = lax.axis_size("tile"), lax.axis_size("bank")
    local_rows, classes, width = reference_bank.shape
    if banks != 4 or tiles % 2 or tiles * banks * mine.shape[0] > 1024 or classes % 5:
        return score_plain(
            lax.all_gather(lax.all_gather(mine, "bank", axis=0, tiled=True), "tile", axis=0, tiled=True),
            reference_bank,
        )
    bank = jnp.transpose(reference_bank, (1, 0, 2))

    def along(value, pairs):
        return lax.ppermute(value, "bank", pairs)

    def swap(value):
        return lax.ppermute(value, "tile", [(i, i ^ 1) for i in range(tiles)])

    x_pairs, y_pairs = [(0, 1), (1, 0), (2, 3), (3, 2)], [(0, 2), (2, 0), (1, 3), (3, 1)]
    line = jnp.concatenate(
        [mine]
        + [
            lax.ppermute(mine, "tile", [(i, (i + by) % tiles) for i in range(tiles)])
            for by in range(2, tiles, 2)
        ],
        axis=0,
    )
    half = line.shape[0] // 2
    from_x, from_y = along(line, x_pairs), along(line, y_pairs)
    near = [line, swap(line)]
    first = weigh_blocks(near, bank)
    part_x, part_y, first = lax.optimization_barrier((from_x[:half], from_y[half:], first))
    across_y, across_x = along(part_x, y_pairs), along(part_y, x_pairs)
    middle = [from_x, from_y, swap(from_x), swap(from_y)]
    second = weigh_blocks(middle, bank)
    across_y, across_x, second = lax.optimization_barrier((across_y, across_x, second))
    last = [across_y, across_x, swap(across_y), swap(across_x)]
    out, sums = sum_blocks([first, second], near + middle + last, 2 * line.shape[0], bank)
    return jnp.transpose(out, (1, 0, 2)), jnp.transpose(sums, (1, 0))


def scratch_of(boxes, scored, blocks, orients, tail):
    return [
        pltpu.VMEM((boxes, F), jnp.bfloat16),
        pltpu.VMEM((boxes, tail), jnp.bfloat16),
        pltpu.VMEM((tail, scored), jnp.float32),
        pltpu.VMEM((orients, scored), jnp.float32),
        pltpu.VMEM((1, scored), jnp.float32),
        pltpu.SemaphoreType.DMA((2 * blocks,)),
    ]


CLASSES = 5


def bank_index():
    return lax.axis_index("bank").astype(jnp.int32)[None]


def weigh_blocks(blocks, bank):
    classes, orients, width = bank.shape
    boxes = sum(block.shape[0] for block in blocks)
    tail = blocks[0].shape[1] - F
    return pl.pallas_call(
        functools.partial(weigh_kernel, blocks=len(blocks)),
        grid=(classes // CLASSES,),
        in_specs=[pl.BlockSpec(memory_space=pltpu.SMEM)]
        + [pl.BlockSpec(memory_space=pl.ANY)] * len(blocks)
        + [pl.BlockSpec((CLASSES, orients, width), lambda i: (i, 0, 0))],
        out_specs=pl.BlockSpec((CLASSES, orients, boxes), lambda i: (i, 0, 0)),
        out_shape=jax.ShapeDtypeStruct((classes, orients, boxes), jnp.bfloat16),
        scratch_shapes=scratch_of(boxes, boxes, len(blocks), orients, tail),
        compiler_params=pltpu.CompilerParams(vmem_limit_bytes=18 * MIB),
        cost_estimate=pl.CostEstimate(
            flops=2 * boxes * classes * orients * width,
            bytes_accessed=2 * classes * orients * width,
            transcendentals=0,
        ),
        name="weigh",
    )(bank_index(), *blocks, bank)


def sum_blocks(parts, blocks, late, bank):
    classes, orients, width = bank.shape
    boxes = sum(block.shape[0] for block in blocks)
    tail = blocks[0].shape[1] - F
    return pl.pallas_call(
        functools.partial(sum_kernel, early=len(parts), blocks=len(blocks), late=late),
        grid=(classes // CLASSES,),
        in_specs=[pl.BlockSpec(memory_space=pltpu.SMEM)]
        + [pl.BlockSpec((CLASSES, orients, part.shape[2]), lambda i: (i, 0, 0)) for part in parts]
        + [pl.BlockSpec(memory_space=pl.ANY)] * len(blocks)
        + [pl.BlockSpec((CLASSES, orients, width), lambda i: (i, 0, 0))],
        out_specs=[
            pl.BlockSpec((CLASSES, orients, width), lambda i: (i, 0, 0)),
            pl.BlockSpec((classes, orients), lambda i: (0, 0)),
        ],
        out_shape=[
            jax.ShapeDtypeStruct((classes, orients, width), jnp.float32),
            jax.ShapeDtypeStruct((classes, orients), jnp.float32),
        ],
        scratch_shapes=scratch_of(boxes, late, len(blocks), orients, tail),
        compiler_params=pltpu.CompilerParams(vmem_limit_bytes=36 * MIB),
        cost_estimate=pl.CostEstimate(
            flops=2 * (boxes + late) * classes * orients * width,
            bytes_accessed=6 * classes * orients * width,
            transcendentals=0,
        ),
        name="class_sums",
    )(bank_index(), *parts, *blocks, bank)


def body(volume, pick_list, box_counts, orientations, orient_weight, reference_bank):
    wide, high, depth = volume.shape
    slots = pick_list.shape[3]
    low = shifted(volume[wide - HALF :], "tile", 1)
    top = shifted(volume[:HALF], "tile", -1)

    corner_x = pick_list[0, 0, 0] - lax.axis_index("tile") * wide
    corner_y = pick_list[1, 0, 0] - lax.axis_index("bank") * high - HALF
    own = jnp.stack([corner_x, corner_y, pick_list[2, 0, 0]])
    before = shifted(own, "bank", 1)
    after = shifted(own, "bank", -1)
    step = jnp.array([0, high, 0], jnp.int32)[:, None]
    corners = jnp.concatenate([before - step, own, after + step], axis=1)
    corners = jnp.pad(corners, ((0, 5), (0, 128 - 3 * slots))).astype(jnp.bfloat16)

    first, second = depth_tables(depth)
    plane = jnp.asarray(plane_table(wide + 2 * HALF, high), jnp.bfloat16)
    modes, lanes = plane.shape[0], 3 * slots * L
    unit = 16
    scratch = [
        pltpu.VMEM((depth, lanes), jnp.bfloat16),
        pltpu.VMEM((high, lanes), jnp.float32),
        pltpu.VMEM((1, lanes), jnp.float32),
        pltpu.VMEM((unit * high, lanes), jnp.bfloat16),
    ]
    whole = [
        pl.BlockSpec((8, 128), lambda i: (0, 0)),
        pl.BlockSpec((depth, 128), lambda i: (0, 0)),
        pl.BlockSpec((depth, 128), lambda i: (0, 0)),
    ]
    params = pltpu.CompilerParams(vmem_limit_bytes=16 * MIB)
    near = pl.pallas_call(
        functools.partial(near_kernel, offset=HALF),
        grid=(wide // unit,),
        in_specs=whole
        + [
            pl.BlockSpec((unit, high, depth), lambda i: (i, 0, 0)),
            pl.BlockSpec((modes, unit * high), lambda i: (0, HALF // unit + i)),
        ],
        out_specs=pl.BlockSpec((modes, lanes), lambda i: (0, 0)),
        out_shape=jax.ShapeDtypeStruct((modes, lanes), jnp.float32),
        scratch_shapes=scratch,
        compiler_params=params,
        cost_estimate=pl.CostEstimate(
            flops=2 * wide * high * lanes * (depth + modes), bytes_accessed=8000000, transcendentals=0
        ),
        name="near_rows",
    )(corners, first, second, volume, plane)
    half = HALF // unit
    skip = wide // unit
    left, mid, right = pl.pallas_call(
        functools.partial(far_kernel, half=half, gap=wide),
        grid=(2 * half,),
        in_specs=whole
        + [
            pl.BlockSpec((unit, high, depth), lambda i: (jnp.minimum(i, half - 1), 0, 0)),
            pl.BlockSpec((unit, high, depth), lambda i: (jnp.maximum(i - half, 0), 0, 0)),
            pl.BlockSpec(
                (modes, unit * high), lambda i: (0, jnp.where(i < half, i, i + skip))
            ),
            pl.BlockSpec((modes, lanes), lambda i: (0, 0)),
        ],
        out_specs=[pl.BlockSpec((L * L, slots * L), lambda i: (0, 0))] * 3,
        out_shape=[
            jax.ShapeDtypeStruct((L * L, slots * L), jnp.bfloat16),
            jax.ShapeDtypeStruct((L * L, slots * L), jnp.float32),
            jax.ShapeDtypeStruct((L * L, slots * L), jnp.bfloat16),
        ],
        scratch_shapes=scratch + [pltpu.VMEM((modes, lanes), jnp.float32)],
        compiler_params=params,
        name="far_rows",
    )(corners, first, second, low, top, plane, near)
    from_after = shifted(left, "bank", -1)
    from_before = shifted(right, "bank", 1)

    live_slots = jnp.arange(slots) < box_counts[0, 0]
    matches = orientations[0, 0][:, :, None] == jnp.arange(R)[None, None, :]
    multiplicity = jnp.sum(
        jnp.where(matches, orient_weight[0, 0][:, :, None].astype(jnp.float32), 0.0), axis=1
    )
    multiplicity = jnp.where(live_slots[:, None], multiplicity, 0.0).astype(jnp.bfloat16)
    mine = pl.pallas_call(
        join_kernel,
        out_shape=jax.ShapeDtypeStruct((slots, F + R + 128), jnp.bfloat16),
        scratch_shapes=[pltpu.VMEM((slots, F), jnp.float32)],
        compiler_params=params,
        name="join",
    )(mid, from_after, from_before, multiplicity)
    return gather_score(mine, reference_bank)


def solution(mesh):
    in_specs = (
        P("tile", "bank", None),
        P(None, "tile", "bank", None),
        P("tile", "bank"),
        P("tile", "bank", None, None),
        P("tile", "bank", None, None),
        P("bank", None, None),
    )
    out_specs = (P("bank", None, None), P("bank", None))
    return jax.shard_map(body, mesh=mesh, in_specs=in_specs, out_specs=out_specs, check_vma=False)
```

```python
import functools

import jax
import jax.numpy as jnp
import numpy as np
from jax import lax
from jax.experimental import pallas as pl
from jax.experimental.pallas import tpu as pltpu
from jax.sharding import PartitionSpec as P

B = 96
L = 16
R = 256
F = L * L * L
HALF = B // 2
TERMS = L // 2
EPSILON = 1e-06
MIB = 1024 * 1024


def waves(count):
    steps = 2.0 * np.pi * np.outer(np.arange(TERMS + 1), np.arange(count)) / B
    return np.cos(steps) / np.sqrt(B), np.sin(steps) / np.sqrt(B)


def depth_tables(depth):
    cos, sin = waves(depth)
    first = np.concatenate([cos, sin[1:TERMS]], axis=0)
    second = np.concatenate([sin, -cos[1:TERMS]], axis=0)
    repeat = 128 // L
    return (
        np.tile(first.T, (1, repeat)).astype(np.float32),
        np.tile(second.T, (1, repeat)).astype(np.float32),
    )


def plane_table(wide, high):
    cos_x, sin_x = waves(wide)
    cos_y, sin_y = waves(high)
    along_x = np.concatenate([cos_x, sin_x[1:]], axis=0)
    along_y = np.concatenate([cos_y[1:], sin_y[1:]], axis=0)
    main = np.einsum("ax,by->abxy", along_x, along_y).reshape(-1, wide * high)
    order = np.concatenate([along_x[1:], along_x[:1]], axis=0)
    flat = np.einsum("ax,y->axy", order, cos_y[0]).reshape(-1, wide * high)
    rows = np.concatenate([main, flat], axis=0)
    pad = -rows.shape[0] % 16
    return np.concatenate([rows, np.zeros((pad, rows.shape[1]))], axis=0).astype(np.float32)


def spread(origin_ref, corner_refs, lanes):
    slots = corner_refs[0].shape[3]
    box = lax.broadcasted_iota(jnp.int32, (slots, lanes), 0)
    lane = lax.broadcasted_iota(jnp.int32, (slots, lanes), 1)
    row = lax.broadcasted_iota(jnp.int32, (8, slots), 0)
    origin = jnp.where(row == 0, origin_ref[0], jnp.where(row == 1, origin_ref[1], 0))
    total = jnp.zeros((8, lanes), jnp.float32)
    for k, corner_ref in enumerate(corner_refs):
        corners = jnp.zeros((8, slots), jnp.int32)
        for axis in range(3):
            corners = jnp.where(row == axis, corner_ref[axis, 0], corners)
        corners = (corners - origin).astype(jnp.float32).astype(jnp.bfloat16)
        pick = jnp.where(lane // L == box + k * slots, 1.0, 0.0).astype(jnp.bfloat16)
        total += jnp.dot(corners, pick, preferred_element_type=jnp.float32)
    return total


def turns(terms, shift):
    turn = (terms * shift).astype(jnp.int32)
    turn = lax.rem(turn, B)
    angle = turn.astype(jnp.float32) * (2.0 * np.pi / B)
    return jnp.cos(angle), jnp.sin(angle)


def prepare(origin_ref, corner_refs, first_ref, second_ref, depth_ref, high_ref):
    depth, lanes = depth_ref.shape
    where = spread(origin_ref, corner_refs, lanes)
    start_y, start_z = where[1:2], where[2:3]
    lane = lax.rem(lax.broadcasted_iota(jnp.int32, (1, lanes), 1), L)
    term = jnp.where(lane <= TERMS, lane, lane - TERMS).astype(jnp.float32)
    cos, sin = turns(term, start_z)
    copies = lanes // first_ref.shape[1]
    first = jnp.concatenate([first_ref[...]] * copies, axis=1)
    second = jnp.concatenate([second_ref[...]] * copies, axis=1)
    z = lax.broadcasted_iota(jnp.int32, (depth, lanes), 0).astype(jnp.float32) - start_z
    table = jnp.where((z >= 0) & (z < B), first * cos + second * sin, 0.0)
    depth_ref[...] = table.astype(jnp.bfloat16)
    y = lax.broadcasted_iota(jnp.int32, high_ref.shape, 0).astype(jnp.float32) - start_y
    high_ref[...] = jnp.where((y >= 0) & (y < B), 1.0, 0.0)
    return where[0:1]


def block_modes(voxels, at_x, turn, start_x, depth_ref, high_ref, part_ref, plane_ref):
    count, high, depth = voxels.shape
    offset = at_x - start_x
    for x in range(0, count, 4):
        rows = voxels[x : x + 4].reshape(4 * high, depth)
        first = jnp.dot(rows, depth_ref[...], preferred_element_type=jnp.float32)
        for i in range(4):
            at = offset + float(x + i)
            live = high_ref[...] * jnp.where((at >= 0) & (at < B), 1.0, 0.0)
            kept = first[i * high : (i + 1) * high] * live
            part_ref[pl.ds((x + i) * high, high), :] = kept.astype(jnp.bfloat16)
    length = count * high
    total = jnp.dot(
        plane_ref[:, :length], part_ref[:length], preferred_element_type=jnp.float32
    )
    return total if turn is None else moved(total, turn)


def turn_of(at_x):
    angles = 2.0 * np.pi * np.arange(1, TERMS + 1) * at_x / B
    return [float(c) for c in np.cos(angles)], [float(s) for s in np.sin(angles)]


def either(flag, one, other):
    return tuple([jnp.where(flag, a, b) for a, b in zip(u, v)] for u, v in zip(one, other))


def moved(total, turn):
    group, blocks = 2 * TERMS, 2 * TERMS + 1
    rows = [total[a * group : (a + 1) * group] for a in range(blocks)]
    main = blocks * group
    flat_cos, flat_sin = total[main : main + TERMS], total[main + TERMS : main + group]
    out = list(rows)
    term = lax.broadcasted_iota(jnp.int32, flat_cos.shape, 0)
    flat_c, flat_s = jnp.zeros_like(flat_cos), jnp.zeros_like(flat_cos)
    for j, (c, s) in enumerate(zip(*turn)):
        out[1 + j] = rows[1 + j] * c - rows[1 + TERMS + j] * s
        out[1 + TERMS + j] = rows[1 + j] * s + rows[1 + TERMS + j] * c
        flat_c = jnp.where(term == j, c, flat_c)
        flat_s = jnp.where(term == j, s, flat_s)
    out += [
        flat_cos * flat_c - flat_sin * flat_s,
        flat_cos * flat_s + flat_sin * flat_c,
        total[main + group :],
    ]
    return jnp.concatenate(out, axis=0)


def near_kernel(
    origin_ref, first_pick_ref, pick_ref, second_pick_ref, first_ref, second_ref, volume_ref, plane_ref,
    total_ref, depth_ref, high_ref, part_ref,
):
    corner_refs = (first_pick_ref, pick_ref, second_pick_ref)
    start_x = prepare(origin_ref, corner_refs, first_ref, second_ref, depth_ref, high_ref)
    unit = part_ref.shape[0] // volume_ref.shape[1]
    for x in range(0, volume_ref.shape[0], unit):
        added = block_modes(
            volume_ref[x : x + unit], float(x), turn_of(x) if x else None, start_x,
            depth_ref, high_ref, part_ref, plane_ref,
        )
        total_ref[...] = added if x == 0 else total_ref[...] + added


def rotate(total, start_x, start_y):
    lanes = total.shape[1]
    term = (lax.broadcasted_iota(jnp.int32, (TERMS, lanes), 0) + 1).astype(jnp.float32)
    cos_x, sin_x = turns(term, start_x)
    cos_y, sin_y = turns(term, start_y)
    blocks = 2 * TERMS + 1
    main = blocks * 2 * TERMS
    flat_cos = total[main : main + TERMS]
    flat_sin = total[main + TERMS : main + 2 * TERMS]
    flat_zero = total[main + 2 * TERMS : main + 2 * TERMS + 1]
    flats = (
        [flat_zero]
        + [flat_cos[j : j + 1] for j in range(TERMS)]
        + [flat_sin[j : j + 1] for j in range(TERMS)]
    )
    last = lax.broadcasted_iota(jnp.int32, (TERMS, lanes), 0) == TERMS - 1
    turned = []
    for a in range(blocks):
        cos = total[a * 2 * TERMS : a * 2 * TERMS + TERMS]
        sin = total[a * 2 * TERMS + TERMS : (a + 1) * 2 * TERMS]
        low = cos * cos_y + sin * sin_y
        high = sin * cos_y - cos * sin_y
        turned.append((low, jnp.where(last, flats[a], high)))
    rows = [None] * (2 * TERMS)
    rows[0] = turned[0]
    for j in range(1, TERMS + 1):
        c, s = cos_x[j - 1 : j], sin_x[j - 1 : j]
        cos, sin = turned[j], turned[TERMS + j]
        rows[j] = tuple(u * c + v * s for u, v in zip(cos, sin))
        if j < TERMS:
            rows[TERMS + j] = tuple(v * c - u * s for u, v in zip(cos, sin))
    return jnp.concatenate([half for pair in rows for half in pair], axis=0)


def far_kernel(
    origin_ref, first_pick_ref, pick_ref, second_pick_ref, first_ref, second_ref, first_halo_ref, second_halo_ref, plane_ref,
    near_ref, first_out_ref, own_ref, second_out_ref, depth_ref, high_ref, part_ref, total_ref, *, wide,
):
    corner_refs = (first_pick_ref, pick_ref, second_pick_ref)
    start_x = prepare(origin_ref, corner_refs, first_ref, second_ref, depth_ref, high_ref)
    where = spread(origin_ref, corner_refs, total_ref.shape[1])
    total_ref[...] = near_ref[...]
    even = origin_ref[2] == 0
    below, above = turn_of(-HALF), turn_of(wide)
    sides = (
        (first_halo_ref, jnp.where(even, wide, -HALF), either(even, above, below)),
        (second_halo_ref, jnp.where(even, -HALF, wide), either(even, below, above)),
    )
    for voxels_ref, at_x, turn in sides:
        total_ref[...] += block_modes(
            voxels_ref[...], at_x.astype(jnp.float32), turn, start_x,
            depth_ref, high_ref, part_ref, plane_ref,
        )
    rows = rotate(total_ref[...], start_x, where[1:2])
    width = own_ref.shape[1]
    first_out_ref[...] = rows[:, :width].astype(jnp.bfloat16)
    own_ref[...] = rows[:, width : 2 * width]
    second_out_ref[...] = rows[:, 2 * width :].astype(jnp.bfloat16)


def join_kernel(own_ref, left_ref, right_ref, multiplicity_ref, out_ref, wide_ref):
    total = own_ref[...] + left_ref[...].astype(jnp.float32) + right_ref[...].astype(jnp.float32)
    total = total.astype(jnp.bfloat16)
    rows, lanes = total.shape
    slots = lanes // L
    k = lax.broadcasted_iota(jnp.int32, (lanes, L * L), 0)
    lane = lax.broadcasted_iota(jnp.int32, (lanes, L * L), 1)
    gap = k - lax.rem(lane, L)
    row = lax.rem(lax.broadcasted_iota(jnp.int32, (rows, L * L), 0), L)
    place = jnp.where(row == L - 1, 0, row + 1)
    keep = jnp.where(
        place == lax.broadcasted_iota(jnp.int32, (rows, L * L), 1) // L, 1.0, 0.0
    )
    sums = jnp.where(
        lax.broadcasted_iota(jnp.int32, (L, rows), 1) // L
        == lax.broadcasted_iota(jnp.int32, (L, rows), 0),
        1.0,
        0.0,
    ).astype(jnp.bfloat16)
    for s in range(slots):
        copies = jnp.where(gap == s * L, 1.0, 0.0).astype(jnp.bfloat16)
        spread_rows = jnp.dot(total, copies, preferred_element_type=jnp.float32) * keep
        feature = jnp.dot(
            sums, spread_rows.astype(jnp.bfloat16), preferred_element_type=jnp.float32
        )
        for a in range(L):
            wide_ref[s : s + 1, a * L * L : (a + 1) * L * L] = feature[a : a + 1]
    wide = wide_ref[...]
    norm = jnp.sqrt(jnp.mean(wide * wide, axis=1, keepdims=True) + EPSILON)
    high = norm.astype(jnp.bfloat16).astype(jnp.float32)
    tail = lax.broadcasted_iota(jnp.int32, (slots, 128), 1)
    tail = jnp.where(tail == 0, high, jnp.where(tail == 1, norm - high, 0.0))
    out_ref[:, :F] = wide.astype(jnp.bfloat16)
    out_ref[:, F : F + R] = multiplicity_ref[...]
    out_ref[:, F + R :] = tail.astype(jnp.bfloat16)


def load_blocks(blocks, rows_ref, tail_ref, sems):
    copies, at = [], 0
    for k, block in enumerate(blocks):
        count = block.shape[0]
        place = pl.ds(at, count)
        copies.append(
            pltpu.make_async_copy(block.at[:, pl.ds(0, F)], rows_ref.at[place], sems.at[2 * k])
        )
        copies.append(
            pltpu.make_async_copy(
                block.at[:, pl.ds(F, block.shape[1] - F)], tail_ref.at[place], sems.at[2 * k + 1]
            )
        )
        at += count
    for copy in copies:
        copy.start()
    for copy in copies:
        copy.wait()


def read_tail(bank_ref, tail, tail_ref, multiplicity_ref, norm_ref, orients):
    tail_ref[...] = tail.astype(jnp.float32).T
    start = pl.multiple_of(bank_ref[0] * orients, orients)
    multiplicity_ref[...] = tail_ref[pl.ds(start, orients), :]
    norm_ref[...] = tail_ref[R : R + 1, :] + tail_ref[R + 1 : R + 2, :]


def weigh(bank_rows, rows, multiplicity, norm, count):
    scores = lax.dot_general(
        bank_rows, rows, (((1,), (1,)), ((), ())), preferred_element_type=jnp.float32
    )
    wide = bank_rows.astype(jnp.float32)
    bank_norm = jnp.sqrt(jnp.mean(wide * wide, axis=1, keepdims=True) + EPSILON)
    correl = scores / (F * norm * bank_norm)
    multiplicity = jnp.concatenate([multiplicity] * count, axis=0)
    return (multiplicity * jnp.maximum(correl, 0.0)).astype(jnp.bfloat16)


def weigh_kernel(index_ref, *refs, blocks):
    sources, (bank_ref, out_ref) = refs[:blocks], refs[blocks : blocks + 2]
    rows_ref, tail_ref, turned_ref, multiplicity_ref, norm_ref, sems = refs[blocks + 2 :]
    count, orients, width = bank_ref.shape

    @pl.when(pl.program_id(0) == 0)
    def _():
        load_blocks(sources, rows_ref, tail_ref, sems)
        read_tail(index_ref, tail_ref[...], turned_ref, multiplicity_ref, norm_ref, orients)

    bank = bank_ref[...].reshape(count * orients, width)
    weights = weigh(bank, rows_ref[...], multiplicity_ref[...], norm_ref[...], count)
    out_ref[...] = weights.reshape(out_ref.shape)


def sum_kernel(index_ref, *refs, early, blocks, late):
    parts, sources = refs[:early], refs[early : early + blocks]
    bank_ref, out_ref, sums_ref = refs[early + blocks : early + blocks + 3]
    rows_ref, tail_ref, turned_ref, multiplicity_ref, norm_ref, sems = refs[early + blocks + 3 :]
    count, orients, width = bank_ref.shape
    boxes = rows_ref.shape[0]
    step = pl.program_id(0)

    @pl.when(step == 0)
    def _():
        load_blocks(sources, rows_ref, tail_ref, sems)
        read_tail(
            index_ref, tail_ref[boxes - late :], turned_ref, multiplicity_ref, norm_ref, orients
        )

    bank = bank_ref[...].reshape(count * orients, width)
    weights = weigh(
        bank, rows_ref[boxes - late :, :], multiplicity_ref[...], norm_ref[...], count
    )
    known = [part[...].reshape(count * orients, part.shape[2]) for part in parts]
    weights = jnp.concatenate(known + [weights], axis=1)
    total = jnp.dot(weights, rows_ref[...], preferred_element_type=jnp.float32)
    out_ref[...] = total.reshape(out_ref.shape)
    ones = jnp.ones((8, boxes), jnp.bfloat16)
    sums = lax.dot_general(
        ones, weights, (((1,), (1,)), ((), ())), preferred_element_type=jnp.float32
    )
    for c in range(count):
        sums_ref[pl.ds(step * count + c, 1), :] = sums[:1, c * orients : (c + 1) * orients]


def score_plain(rows, bank):
    local_rows = bank.shape[0]
    start = F + lax.axis_index("bank") * local_rows
    multiplicity = lax.dynamic_slice_in_dim(rows, start, local_rows, 1).astype(jnp.float32)
    norm = rows[:, F + R].astype(jnp.float32) + rows[:, F + R + 1].astype(jnp.float32)
    features = rows[:, :F]
    scores = jnp.einsum("if,rcf->irc", features, bank, preferred_element_type=jnp.float32)
    wide = bank.astype(jnp.float32)
    bank_norm = jnp.sqrt(jnp.mean(wide * wide, axis=2) + EPSILON)
    correl = scores / (F * norm[:, None, None] * bank_norm[None])
    weights = (multiplicity[:, :, None] * jnp.maximum(correl, 0.0)).astype(jnp.bfloat16)
    class_sums = jnp.einsum("irc,if->rcf", weights, features, preferred_element_type=jnp.float32)
    return class_sums, jnp.sum(weights.astype(jnp.float32), axis=0)


def exchange(value, axis, first):
    count = lax.axis_size(axis)
    pairs = []
    for i in range(0 if first else 1, count - 1, 2):
        pairs += [(i, i + 1), (i + 1, i)]
    return lax.ppermute(value, axis, pairs)


def gather_score(mine, reference_bank):
    tiles, banks = lax.axis_size("tile"), lax.axis_size("bank")
    local_rows, classes, width = reference_bank.shape
    if banks != 4 or tiles & (tiles - 1) or tiles < 2 or tiles * banks * mine.shape[0] > 1024 or classes % 5:
        return score_plain(
            lax.all_gather(lax.all_gather(mine, "bank", axis=0, tiled=True), "tile", axis=0, tiled=True),
            reference_bank,
        )
    bank = jnp.transpose(reference_bank, (1, 0, 2))

    def along(value, pairs):
        return lax.ppermute(value, "bank", pairs)

    def swap(value):
        return lax.ppermute(value, "tile", [(i, i ^ 1) for i in range(tiles)])

    x_pairs, y_pairs = [(0, 1), (1, 0), (2, 3), (3, 2)], [(0, 2), (2, 0), (1, 3), (3, 1)]
    line = jnp.concatenate(
        [mine]
        + [
            lax.ppermute(mine, "tile", [(i, i ^ by) for i in range(tiles)])
            for by in range(2, tiles, 2)
        ],
        axis=0,
    )
    half = line.shape[0] // 2
    from_x, from_y = along(line, x_pairs), along(line, y_pairs)
    near = [line, swap(line)]
    first = weigh_blocks(near, bank)
    from_x, from_y, first = lax.optimization_barrier((from_x, from_y, first))
    across_y, across_x = along(from_x[:half], y_pairs), along(from_y[half:], x_pairs)
    middle = [from_x, from_y, swap(from_x), swap(from_y)]
    second = weigh_blocks(middle, bank)
    across_y, across_x, second = lax.optimization_barrier((across_y, across_x, second))
    last = [across_y, across_x, swap(across_y), swap(across_x)]
    out, sums = sum_blocks([first, second], near + middle + last, 2 * line.shape[0], bank)
    return jnp.transpose(out, (1, 0, 2)), jnp.transpose(sums, (1, 0))


def scratch_of(boxes, scored, blocks, orients, tail):
    return [
        pltpu.VMEM((boxes, F), jnp.bfloat16),
        pltpu.VMEM((boxes, tail), jnp.bfloat16),
        pltpu.VMEM((tail, scored), jnp.float32),
        pltpu.VMEM((orients, scored), jnp.float32),
        pltpu.VMEM((1, scored), jnp.float32),
        pltpu.SemaphoreType.DMA((2 * blocks,)),
    ]


CLASSES = 5


def bank_index():
    return lax.axis_index("bank").astype(jnp.int32)[None]


def weigh_blocks(blocks, bank):
    classes, orients, width = bank.shape
    boxes = sum(block.shape[0] for block in blocks)
    tail = blocks[0].shape[1] - F
    return pl.pallas_call(
        functools.partial(weigh_kernel, blocks=len(blocks)),
        grid=(classes // CLASSES,),
        in_specs=[pl.BlockSpec(memory_space=pltpu.SMEM)]
        + [pl.BlockSpec(memory_space=pl.ANY)] * len(blocks)
        + [pl.BlockSpec((CLASSES, orients, width), lambda i: (i, 0, 0))],
        out_specs=pl.BlockSpec((CLASSES, orients, boxes), lambda i: (i, 0, 0)),
        out_shape=jax.ShapeDtypeStruct((classes, orients, boxes), jnp.bfloat16),
        scratch_shapes=scratch_of(boxes, boxes, len(blocks), orients, tail),
        compiler_params=pltpu.CompilerParams(vmem_limit_bytes=18 * MIB),
        cost_estimate=pl.CostEstimate(
            flops=2 * boxes * classes * orients * width,
            bytes_accessed=2 * classes * orients * width,
            transcendentals=0,
        ),
        name="weigh",
    )(bank_index(), *blocks, bank)


def sum_blocks(parts, blocks, late, bank):
    classes, orients, width = bank.shape
    boxes = sum(block.shape[0] for block in blocks)
    tail = blocks[0].shape[1] - F
    return pl.pallas_call(
        functools.partial(sum_kernel, early=len(parts), blocks=len(blocks), late=late),
        grid=(classes // CLASSES,),
        in_specs=[pl.BlockSpec(memory_space=pltpu.SMEM)]
        + [pl.BlockSpec((CLASSES, orients, part.shape[2]), lambda i: (i, 0, 0)) for part in parts]
        + [pl.BlockSpec(memory_space=pl.ANY)] * len(blocks)
        + [pl.BlockSpec((CLASSES, orients, width), lambda i: (i, 0, 0))],
        out_specs=[
            pl.BlockSpec((CLASSES, orients, width), lambda i: (i, 0, 0)),
            pl.BlockSpec((classes, orients), lambda i: (0, 0)),
        ],
        out_shape=[
            jax.ShapeDtypeStruct((classes, orients, width), jnp.float32),
            jax.ShapeDtypeStruct((classes, orients), jnp.float32),
        ],
        scratch_shapes=scratch_of(boxes, late, len(blocks), orients, tail),
        compiler_params=pltpu.CompilerParams(vmem_limit_bytes=36 * MIB),
        cost_estimate=pl.CostEstimate(
            flops=2 * (boxes + late) * classes * orients * width,
            bytes_accessed=6 * classes * orients * width,
            transcendentals=0,
        ),
        name="class_sums",
    )(bank_index(), *parts, *blocks, bank)


def body(volume, pick_list, box_counts, orientations, orient_weight, reference_bank):
    wide, high, depth = volume.shape
    slots = pick_list.shape[3]
    tile, bank = lax.axis_index("tile"), lax.axis_index("bank")
    side = lax.rem(tile, 2)
    upper, lower = volume[wide - HALF :], volume[:HALF]
    to_first = jnp.where(side == 0, upper, lower)
    to_second = jnp.where(side == 0, lower, upper)
    to_first, to_second, picks = lax.optimization_barrier((to_first, to_second, pick_list))
    first_halo = exchange(to_first, "tile", True)
    second_halo = exchange(to_second, "tile", False)
    first_picks, second_picks = exchange(picks, "bank", True), exchange(picks, "bank", False)
    origin = jnp.stack([tile * wide + HALF, bank * high + HALF, side]).astype(jnp.int32)

    first, second = depth_tables(depth)
    plane = jnp.asarray(plane_table(HALF, high), jnp.bfloat16)
    modes, lanes = plane.shape[0], 3 * slots * L
    unit = 32

    def scratch(count):
        return [
            pltpu.VMEM((depth, lanes), jnp.bfloat16),
            pltpu.VMEM((high, lanes), jnp.float32),
            pltpu.VMEM((count * high, lanes), jnp.bfloat16),
        ]

    params = pltpu.CompilerParams(vmem_limit_bytes=24 * MIB)
    vmem = pl.BlockSpec(memory_space=pltpu.VMEM)
    given = [pl.BlockSpec(memory_space=pltpu.SMEM)] + [vmem] * 5
    near = pl.pallas_call(
        near_kernel,
        in_specs=given + [vmem] * 2,
        out_specs=vmem,
        out_shape=jax.ShapeDtypeStruct((modes, lanes), jnp.float32),
        scratch_shapes=scratch(unit),
        compiler_params=params,
        cost_estimate=pl.CostEstimate(
            flops=2 * wide * high * lanes * (depth + modes), bytes_accessed=8000000, transcendentals=0
        ),
        name="near_rows",
    )(origin, first_picks, picks, second_picks, first, second, volume, plane)
    for_first, mid, for_second = pl.pallas_call(
        functools.partial(far_kernel, wide=wide),
        in_specs=given + [vmem] * 4,
        out_specs=[vmem] * 3,
        out_shape=[
            jax.ShapeDtypeStruct((L * L, slots * L), jnp.bfloat16),
            jax.ShapeDtypeStruct((L * L, slots * L), jnp.float32),
            jax.ShapeDtypeStruct((L * L, slots * L), jnp.bfloat16),
        ],
        scratch_shapes=scratch(HALF) + [pltpu.VMEM((modes, lanes), jnp.float32)],
        compiler_params=params,
        name="far_rows",
    )(
        origin, first_picks, picks, second_picks, first, second, first_halo, second_halo, plane, near
    )
    from_first, from_second = exchange(for_first, "bank", True), exchange(for_second, "bank", False)

    live_slots = jnp.arange(slots) < box_counts[0, 0]
    matches = orientations[0, 0][:, :, None] == jnp.arange(R)[None, None, :]
    multiplicity = jnp.sum(
        jnp.where(matches, orient_weight[0, 0][:, :, None].astype(jnp.float32), 0.0), axis=1
    )
    multiplicity = jnp.where(live_slots[:, None], multiplicity, 0.0).astype(jnp.bfloat16)
    mine = pl.pallas_call(
        join_kernel,
        out_shape=jax.ShapeDtypeStruct((slots, F + R + 128), jnp.bfloat16),
        scratch_shapes=[pltpu.VMEM((slots, F), jnp.float32)],
        compiler_params=params,
        name="join",
    )(mid, from_first, from_second, multiplicity)
    return gather_score(mine, reference_bank)


def solution(mesh):
    in_specs = (
        P("tile", "bank", None),
        P(None, "tile", "bank", None),
        P("tile", "bank"),
        P("tile", "bank", None, None),
        P("tile", "bank", None, None),
        P("bank", None, None),
    )
    out_specs = (P("bank", None, None), P("bank", None))
    return jax.shard_map(body, mesh=mesh, in_specs=in_specs, out_specs=out_specs, check_vma=False)
```

```python
import functools

import jax
import jax.numpy as jnp
import numpy as np
from jax import lax
from jax.experimental import pallas as pl
from jax.experimental.pallas import tpu as pltpu
from jax.sharding import PartitionSpec as P

B = 96
L = 16
R = 256
F = L * L * L
HALF = B // 2
TERMS = L // 2
EPSILON = 1e-06
MIB = 1024 * 1024


def waves(count):
    steps = 2.0 * np.pi * np.outer(np.arange(TERMS + 1), np.arange(count)) / B
    return np.cos(steps) / np.sqrt(B), np.sin(steps) / np.sqrt(B)


def depth_tables(depth):
    cos, sin = waves(depth)
    first = np.concatenate([cos, sin[1:TERMS]], axis=0)
    second = np.concatenate([sin, -cos[1:TERMS]], axis=0)
    repeat = 128 // L
    return (
        np.tile(first.T, (1, repeat)).astype(np.float32),
        np.tile(second.T, (1, repeat)).astype(np.float32),
    )


def plane_table(wide, high):
    cos_x, sin_x = waves(wide)
    cos_y, sin_y = waves(high)
    along_x = np.concatenate([cos_x, sin_x[1:]], axis=0)
    along_y = np.concatenate([cos_y[1:], sin_y[1:]], axis=0)
    main = np.einsum("ax,by->abxy", along_x, along_y).reshape(-1, wide * high)
    order = np.concatenate([along_x[1:], along_x[:1]], axis=0)
    flat = np.einsum("ax,y->axy", order, cos_y[0]).reshape(-1, wide * high)
    rows = np.concatenate([main, flat], axis=0)
    pad = -rows.shape[0] % 16
    return np.concatenate([rows, np.zeros((pad, rows.shape[1]))], axis=0).astype(np.float32)


def spread(origin_ref, corner_refs, lanes):
    slots = corner_refs[0].shape[3]
    box = lax.broadcasted_iota(jnp.int32, (slots, lanes), 0)
    lane = lax.broadcasted_iota(jnp.int32, (slots, lanes), 1)
    row = lax.broadcasted_iota(jnp.int32, (8, slots), 0)
    origin = jnp.where(row == 0, origin_ref[0], jnp.where(row == 1, origin_ref[1], 0))
    total = jnp.zeros((8, lanes), jnp.float32)
    for k, corner_ref in enumerate(corner_refs):
        corners = jnp.zeros((8, slots), jnp.int32)
        for axis in range(3):
            corners = jnp.where(row == axis, corner_ref[axis, 0], corners)
        corners = (corners - origin).astype(jnp.float32).astype(jnp.bfloat16)
        pick = jnp.where(lane // L == box + k * slots, 1.0, 0.0).astype(jnp.bfloat16)
        total += jnp.dot(corners, pick, preferred_element_type=jnp.float32)
    return total


def turns(terms, shift):
    turn = (terms * shift).astype(jnp.int32)
    turn = lax.rem(turn, B)
    angle = turn.astype(jnp.float32) * (2.0 * np.pi / B)
    return jnp.cos(angle), jnp.sin(angle)


def prepare(origin_ref, corner_refs, first_ref, second_ref, depth_ref, high_ref):
    depth, lanes = depth_ref.shape
    where = spread(origin_ref, corner_refs, lanes)
    start_y, start_z = where[1:2], where[2:3]
    lane = lax.rem(lax.broadcasted_iota(jnp.int32, (1, lanes), 1), L)
    term = jnp.where(lane <= TERMS, lane, lane - TERMS).astype(jnp.float32)
    cos, sin = turns(term, start_z)
    copies = lanes // first_ref.shape[1]
    first = jnp.concatenate([first_ref[...]] * copies, axis=1)
    second = jnp.concatenate([second_ref[...]] * copies, axis=1)
    z = lax.broadcasted_iota(jnp.int32, (depth, lanes), 0).astype(jnp.float32) - start_z
    table = jnp.where((z >= 0) & (z < B), first * cos + second * sin, 0.0)
    depth_ref[...] = table.astype(jnp.bfloat16)
    y = lax.broadcasted_iota(jnp.int32, high_ref.shape, 0).astype(jnp.float32) - start_y
    high_ref[...] = jnp.where((y >= 0) & (y < B), 1.0, 0.0)
    return where[0:1]


def block_modes(voxels, at_x, turn, start_x, depth_ref, high_ref, part_ref, plane_ref):
    count, high, depth = voxels.shape
    offset = at_x - start_x
    for x in range(0, count, 4):
        rows = voxels[x : x + 4].reshape(4 * high, depth)
        first = jnp.dot(rows, depth_ref[...], preferred_element_type=jnp.float32)
        for i in range(4):
            at = offset + float(x + i)
            live = high_ref[...] * jnp.where((at >= 0) & (at < B), 1.0, 0.0)
            kept = first[i * high : (i + 1) * high] * live
            part_ref[pl.ds((x + i) * high, high), :] = kept.astype(jnp.bfloat16)
    length = count * high
    total = jnp.dot(
        plane_ref[:, :length], part_ref[:length], preferred_element_type=jnp.float32
    )
    return total if turn is None else moved(total, turn)


def turn_of(at_x):
    angles = 2.0 * np.pi * np.arange(1, TERMS + 1) * at_x / B
    return [float(c) for c in np.cos(angles)], [float(s) for s in np.sin(angles)]


def either(flag, one, other):
    return tuple([jnp.where(flag, a, b) for a, b in zip(u, v)] for u, v in zip(one, other))


def moved(total, turn):
    group, blocks = 2 * TERMS, 2 * TERMS + 1
    rows = [total[a * group : (a + 1) * group] for a in range(blocks)]
    main = blocks * group
    flat_cos, flat_sin = total[main : main + TERMS], total[main + TERMS : main + group]
    out = list(rows)
    term = lax.broadcasted_iota(jnp.int32, flat_cos.shape, 0)
    flat_c, flat_s = jnp.zeros_like(flat_cos), jnp.zeros_like(flat_cos)
    for j, (c, s) in enumerate(zip(*turn)):
        out[1 + j] = rows[1 + j] * c - rows[1 + TERMS + j] * s
        out[1 + TERMS + j] = rows[1 + j] * s + rows[1 + TERMS + j] * c
        flat_c = jnp.where(term == j, c, flat_c)
        flat_s = jnp.where(term == j, s, flat_s)
    out += [
        flat_cos * flat_c - flat_sin * flat_s,
        flat_cos * flat_s + flat_sin * flat_c,
        total[main + group :],
    ]
    return jnp.concatenate(out, axis=0)


def near_kernel(
    origin_ref, first_pick_ref, pick_ref, second_pick_ref, first_ref, second_ref, volume_ref, plane_ref,
    total_ref, depth_ref, high_ref, part_ref,
):
    corner_refs = (first_pick_ref, pick_ref, second_pick_ref)
    start_x = prepare(origin_ref, corner_refs, first_ref, second_ref, depth_ref, high_ref)
    unit = part_ref.shape[0] // volume_ref.shape[1]
    for x in range(0, volume_ref.shape[0], unit):
        added = block_modes(
            volume_ref[x : x + unit], float(x), turn_of(x) if x else None, start_x,
            depth_ref, high_ref, part_ref, plane_ref,
        )
        total_ref[...] = added if x == 0 else total_ref[...] + added


def rotate(total, start_x, start_y):
    lanes = total.shape[1]
    term = (lax.broadcasted_iota(jnp.int32, (TERMS, lanes), 0) + 1).astype(jnp.float32)
    cos_x, sin_x = turns(term, start_x)
    cos_y, sin_y = turns(term, start_y)
    blocks = 2 * TERMS + 1
    main = blocks * 2 * TERMS
    flat_cos = total[main : main + TERMS]
    flat_sin = total[main + TERMS : main + 2 * TERMS]
    flat_zero = total[main + 2 * TERMS : main + 2 * TERMS + 1]
    flats = (
        [flat_zero]
        + [flat_cos[j : j + 1] for j in range(TERMS)]
        + [flat_sin[j : j + 1] for j in range(TERMS)]
    )
    last = lax.broadcasted_iota(jnp.int32, (TERMS, lanes), 0) == TERMS - 1
    turned = []
    for a in range(blocks):
        cos = total[a * 2 * TERMS : a * 2 * TERMS + TERMS]
        sin = total[a * 2 * TERMS + TERMS : (a + 1) * 2 * TERMS]
        low = cos * cos_y + sin * sin_y
        high = sin * cos_y - cos * sin_y
        turned.append((low, jnp.where(last, flats[a], high)))
    rows = [None] * (2 * TERMS)
    rows[0] = turned[0]
    for j in range(1, TERMS + 1):
        c, s = cos_x[j - 1 : j], sin_x[j - 1 : j]
        cos, sin = turned[j], turned[TERMS + j]
        rows[j] = tuple(u * c + v * s for u, v in zip(cos, sin))
        if j < TERMS:
            rows[TERMS + j] = tuple(v * c - u * s for u, v in zip(cos, sin))
    return jnp.concatenate([half for pair in rows for half in pair], axis=0)


def far_kernel(
    origin_ref, first_pick_ref, pick_ref, second_pick_ref, first_ref, second_ref, first_halo_ref, second_halo_ref, plane_ref,
    near_ref, first_out_ref, own_ref, second_out_ref, depth_ref, high_ref, part_ref, total_ref, *, wide,
):
    corner_refs = (first_pick_ref, pick_ref, second_pick_ref)
    start_x = prepare(origin_ref, corner_refs, first_ref, second_ref, depth_ref, high_ref)
    where = spread(origin_ref, corner_refs, total_ref.shape[1])
    total_ref[...] = near_ref[...]
    even = origin_ref[2] == 0
    below, above = turn_of(-HALF), turn_of(wide)
    sides = (
        (first_halo_ref, jnp.where(even, wide, -HALF), either(even, above, below)),
        (second_halo_ref, jnp.where(even, -HALF, wide), either(even, below, above)),
    )
    for voxels_ref, at_x, turn in sides:
        total_ref[...] += block_modes(
            voxels_ref[...], at_x.astype(jnp.float32), turn, start_x,
            depth_ref, high_ref, part_ref, plane_ref,
        )
    rows = rotate(total_ref[...], start_x, where[1:2])
    width = own_ref.shape[1]
    first_out_ref[...] = rows[:, :width].astype(jnp.bfloat16)
    own_ref[...] = rows[:, width : 2 * width]
    second_out_ref[...] = rows[:, 2 * width :].astype(jnp.bfloat16)


def join_kernel(own_ref, left_ref, right_ref, multiplicity_ref, *refs):
    outs, wide_ref = refs[:-1], refs[-1]
    total = own_ref[...] + left_ref[...].astype(jnp.float32) + right_ref[...].astype(jnp.float32)
    total = total.astype(jnp.bfloat16)
    rows, lanes = total.shape
    slots = lanes // L
    k = lax.broadcasted_iota(jnp.int32, (lanes, L * L), 0)
    lane = lax.broadcasted_iota(jnp.int32, (lanes, L * L), 1)
    gap = k - lax.rem(lane, L)
    row = lax.rem(lax.broadcasted_iota(jnp.int32, (rows, L * L), 0), L)
    place = jnp.where(row == L - 1, 0, row + 1)
    keep = jnp.where(
        place == lax.broadcasted_iota(jnp.int32, (rows, L * L), 1) // L, 1.0, 0.0
    )
    sums = jnp.where(
        lax.broadcasted_iota(jnp.int32, (L, rows), 1) // L
        == lax.broadcasted_iota(jnp.int32, (L, rows), 0),
        1.0,
        0.0,
    ).astype(jnp.bfloat16)
    for s in range(slots):
        copies = jnp.where(gap == s * L, 1.0, 0.0).astype(jnp.bfloat16)
        spread_rows = jnp.dot(total, copies, preferred_element_type=jnp.float32) * keep
        feature = jnp.dot(
            sums, spread_rows.astype(jnp.bfloat16), preferred_element_type=jnp.float32
        )
        for a in range(L):
            wide_ref[s : s + 1, a * L * L : (a + 1) * L * L] = feature[a : a + 1]
    wide = wide_ref[...]
    norm = jnp.sqrt(jnp.mean(wide * wide, axis=1, keepdims=True) + EPSILON)
    high = norm.astype(jnp.bfloat16).astype(jnp.float32)
    tail = lax.broadcasted_iota(jnp.int32, (slots, 128), 1)
    tail = jnp.where(tail == 0, high, jnp.where(tail == 1, norm - high, 0.0))
    row = jnp.concatenate(
        [wide.astype(jnp.bfloat16), multiplicity_ref[...], tail.astype(jnp.bfloat16)], axis=1
    )
    for k, out_ref in enumerate(outs):
        count = out_ref.shape[0]
        out_ref[...] = row[k * count : (k + 1) * count]


def load_blocks(blocks, rows_ref, tail_ref, sems):
    copies, at = [], 0
    for k, block in enumerate(blocks):
        count = block.shape[0]
        place = pl.ds(at, count)
        copies.append(
            pltpu.make_async_copy(block.at[:, pl.ds(0, F)], rows_ref.at[place], sems.at[2 * k])
        )
        if tail_ref is not None:
            copies.append(
                pltpu.make_async_copy(
                    block.at[:, pl.ds(F, block.shape[1] - F)], tail_ref.at[place], sems.at[2 * k + 1]
                )
            )
        at += count
    for copy in copies:
        copy.start()
    for copy in copies:
        copy.wait()


def read_tail(bank_ref, tail, tail_ref, multiplicity_ref, norm_ref, orients):
    tail_ref[...] = tail.astype(jnp.float32).T
    start = pl.multiple_of(bank_ref[0] * orients, orients)
    multiplicity_ref[...] = tail_ref[pl.ds(start, orients), :]
    norm_ref[...] = tail_ref[R : R + 1, :] + tail_ref[R + 1 : R + 2, :]


def weigh(bank_rows, rows, multiplicity, norm, count):
    scores = lax.dot_general(
        bank_rows, rows, (((1,), (1,)), ((), ())), preferred_element_type=jnp.float32
    )
    wide = bank_rows.astype(jnp.float32)
    bank_norm = jnp.sqrt(jnp.mean(wide * wide, axis=1, keepdims=True) + EPSILON)
    correl = scores / (F * norm * bank_norm)
    multiplicity = jnp.concatenate([multiplicity] * count, axis=0)
    return (multiplicity * jnp.maximum(correl, 0.0)).astype(jnp.bfloat16)


def weigh_kernel(index_ref, *refs, blocks):
    sources, (bank_ref, out_ref) = refs[:blocks], refs[blocks : blocks + 2]
    rows_ref, tail_ref, turned_ref, multiplicity_ref, norm_ref, sems = refs[blocks + 2 :]
    count, orients, width = bank_ref.shape

    @pl.when(pl.program_id(0) == 0)
    def _():
        load_blocks(sources, rows_ref, tail_ref, sems)
        read_tail(index_ref, tail_ref[...], turned_ref, multiplicity_ref, norm_ref, orients)

    bank = bank_ref[...].reshape(count * orients, width)
    weights = weigh(bank, rows_ref[...], multiplicity_ref[...], norm_ref[...], count)
    out_ref[...] = weights.reshape(out_ref.shape)


def sum_kernel(*refs, early, blocks):
    parts, sources = refs[:early], refs[early : early + blocks]
    out_ref, sums_ref, rows_ref, sems = refs[early + blocks :]
    count, orients, width = out_ref.shape
    boxes = rows_ref.shape[0]
    step = pl.program_id(0)

    @pl.when(step == 0)
    def _():
        load_blocks(sources, rows_ref, None, sems)

    weights = jnp.concatenate(
        [part[...].reshape(count * orients, part.shape[2]) for part in parts], axis=1
    )
    total = jnp.dot(weights, rows_ref[...], preferred_element_type=jnp.float32)
    out_ref[...] = total.reshape(out_ref.shape)
    ones = jnp.ones((8, boxes), jnp.bfloat16)
    sums = lax.dot_general(
        ones, weights, (((1,), (1,)), ((), ())), preferred_element_type=jnp.float32
    )
    for c in range(count):
        sums_ref[pl.ds(step * count + c, 1), :] = sums[:1, c * orients : (c + 1) * orients]


def score_plain(rows, bank):
    local_rows = bank.shape[0]
    start = F + lax.axis_index("bank") * local_rows
    multiplicity = lax.dynamic_slice_in_dim(rows, start, local_rows, 1).astype(jnp.float32)
    norm = rows[:, F + R].astype(jnp.float32) + rows[:, F + R + 1].astype(jnp.float32)
    features = rows[:, :F]
    scores = jnp.einsum("if,rcf->irc", features, bank, preferred_element_type=jnp.float32)
    wide = bank.astype(jnp.float32)
    bank_norm = jnp.sqrt(jnp.mean(wide * wide, axis=2) + EPSILON)
    correl = scores / (F * norm[:, None, None] * bank_norm[None])
    weights = (multiplicity[:, :, None] * jnp.maximum(correl, 0.0)).astype(jnp.bfloat16)
    class_sums = jnp.einsum("irc,if->rcf", weights, features, preferred_element_type=jnp.float32)
    return class_sums, jnp.sum(weights.astype(jnp.float32), axis=0)


def exchange(value, axis, first):
    count = lax.axis_size(axis)
    pairs = []
    for i in range(0 if first else 1, count - 1, 2):
        pairs += [(i, i + 1), (i + 1, i)]
    return lax.ppermute(value, axis, pairs)


def gather_score(mine, reference_bank):
    tiles, banks = lax.axis_size("tile"), lax.axis_size("bank")
    local_rows, classes, width = reference_bank.shape
    boxes = tiles * banks * sum(part.shape[0] for part in mine)
    if banks != 4 or tiles & (tiles - 1) or tiles < 4 or boxes > 1024 or classes % 5:
        rows = jnp.concatenate(mine, axis=0)
        for axis in ("bank", "tile"):
            rows = lax.all_gather(rows, axis, axis=0, tiled=True)
        return score_plain(rows, reference_bank)
    bank = jnp.transpose(reference_bank, (1, 0, 2))
    early, late = mine

    def along_x(value):
        return lax.ppermute(value, "bank", [(0, 1), (1, 0), (2, 3), (3, 2)])

    def along_y(value):
        return lax.ppermute(value, "bank", [(0, 2), (2, 0), (1, 3), (3, 1)])

    def swap(*values):
        return [lax.ppermute(value, "tile", [(i, i ^ 1) for i in range(tiles)]) for value in values]

    def line_of(part):
        others = [
            lax.ppermute(part, "tile", [(i, i ^ by) for i in range(tiles)])
            for by in range(2, tiles, 2)
        ]
        return jnp.concatenate([part] + others, axis=0)

    def with_swap(*values):
        joined = jnp.concatenate(values, axis=0) if len(values) > 1 else values[0]
        return [*values, *swap(joined)]

    early_line = line_of(early)
    late, early_line = lax.optimization_barrier((late, early_line))
    from_x, from_y = along_x(early_line), along_y(early_line)
    late_line = line_of(late)
    half = early_line.shape[0] // 2
    to_x = jnp.concatenate([from_y[half:], late_line], axis=0)
    to_y = jnp.concatenate([from_x[:half], late_line], axis=0)
    blocks = [with_swap(early_line, from_x, from_y)]
    next_x, next_y = along_x(to_x), along_y(to_y)
    first = weigh_blocks(blocks[0], bank)
    first, next_x, next_y = lax.optimization_barrier((first, next_x, next_y))
    last_x, last_y = along_x(next_y[half + half :]), along_y(next_x[half : half + half])
    blocks.append(with_swap(late_line, next_x, next_y))
    second = weigh_blocks(blocks[1], bank)
    second, last_x, last_y = lax.optimization_barrier((second, last_x, last_y))
    blocks.append(with_swap(last_x, last_y))
    third = weigh_blocks(blocks[2], bank)
    out, sums = sum_blocks([first, second, third], sum(blocks, []), bank)
    return jnp.transpose(out, (1, 0, 2)), jnp.transpose(sums, (1, 0))


CLASSES = 5


def bank_index():
    return lax.axis_index("bank").astype(jnp.int32)[None]


def weigh_blocks(blocks, bank):
    classes, orients, width = bank.shape
    boxes = sum(block.shape[0] for block in blocks)
    tail = blocks[0].shape[1] - F
    return pl.pallas_call(
        functools.partial(weigh_kernel, blocks=len(blocks)),
        grid=(classes // CLASSES,),
        in_specs=[pl.BlockSpec(memory_space=pltpu.SMEM)]
        + [pl.BlockSpec(memory_space=pl.ANY)] * len(blocks)
        + [pl.BlockSpec((CLASSES, orients, width), lambda i: (i, 0, 0))],
        out_specs=pl.BlockSpec((CLASSES, orients, boxes), lambda i: (i, 0, 0)),
        out_shape=jax.ShapeDtypeStruct((classes, orients, boxes), jnp.bfloat16),
        scratch_shapes=[
            pltpu.VMEM((boxes, F), jnp.bfloat16),
            pltpu.VMEM((boxes, tail), jnp.bfloat16),
            pltpu.VMEM((tail, boxes), jnp.float32),
            pltpu.VMEM((orients, boxes), jnp.float32),
            pltpu.VMEM((1, boxes), jnp.float32),
            pltpu.SemaphoreType.DMA((2 * len(blocks),)),
        ],
        compiler_params=pltpu.CompilerParams(vmem_limit_bytes=18 * MIB),
        cost_estimate=pl.CostEstimate(
            flops=2 * boxes * classes * orients * width,
            bytes_accessed=2 * classes * orients * width,
            transcendentals=0,
        ),
        name="weigh",
    )(bank_index(), *blocks, bank)


def sum_blocks(parts, blocks, bank):
    classes, orients, width = bank.shape
    boxes = sum(block.shape[0] for block in blocks)
    return pl.pallas_call(
        functools.partial(sum_kernel, early=len(parts), blocks=len(blocks)),
        grid=(classes // CLASSES,),
        in_specs=[
            pl.BlockSpec((CLASSES, orients, part.shape[2]), lambda i: (i, 0, 0)) for part in parts
        ]
        + [pl.BlockSpec(memory_space=pl.ANY)] * len(blocks),
        out_specs=[
            pl.BlockSpec((CLASSES, orients, width), lambda i: (i, 0, 0)),
            pl.BlockSpec((classes, orients), lambda i: (0, 0)),
        ],
        out_shape=[
            jax.ShapeDtypeStruct((classes, orients, width), jnp.float32),
            jax.ShapeDtypeStruct((classes, orients), jnp.float32),
        ],
        scratch_shapes=[
            pltpu.VMEM((boxes, F), jnp.bfloat16),
            pltpu.SemaphoreType.DMA((2 * len(blocks),)),
        ],
        compiler_params=pltpu.CompilerParams(vmem_limit_bytes=36 * MIB),
        cost_estimate=pl.CostEstimate(
            flops=2 * boxes * classes * orients * width,
            bytes_accessed=4 * classes * orients * width,
            transcendentals=0,
        ),
        name="class_sums",
    )(*parts, *blocks)


def body(volume, pick_list, box_counts, orientations, orient_weight, reference_bank):
    wide, high, depth = volume.shape
    slots = pick_list.shape[3]
    tile, bank = lax.axis_index("tile"), lax.axis_index("bank")
    side = lax.rem(tile, 2)
    rest = wide - HALF
    to_first = lax.dynamic_slice_in_dim(volume, jnp.where(side == 0, rest, 0), HALF, 0)
    to_second = lax.dynamic_slice_in_dim(volume, jnp.where(side == 0, 0, rest), HALF, 0)
    first_halo = exchange(to_first, "tile", True)
    second_halo = exchange(to_second, "tile", False)
    picks, first_halo = lax.optimization_barrier((pick_list, first_halo))
    first_picks, second_picks = exchange(picks, "bank", True), exchange(picks, "bank", False)
    origin = jnp.stack([tile * wide + HALF, bank * high + HALF, side]).astype(jnp.int32)

    first, second = depth_tables(depth)
    plane = jnp.asarray(plane_table(HALF, high), jnp.bfloat16)
    modes, lanes = plane.shape[0], 3 * slots * L
    unit = 32

    def scratch(count):
        return [
            pltpu.VMEM((depth, lanes), jnp.bfloat16),
            pltpu.VMEM((high, lanes), jnp.float32),
            pltpu.VMEM((count * high, lanes), jnp.bfloat16),
        ]

    params = pltpu.CompilerParams(vmem_limit_bytes=24 * MIB)
    vmem = pl.BlockSpec(memory_space=pltpu.VMEM)
    given = [pl.BlockSpec(memory_space=pltpu.SMEM)] + [vmem] * 5
    near = pl.pallas_call(
        near_kernel,
        in_specs=given + [vmem] * 2,
        out_specs=vmem,
        out_shape=jax.ShapeDtypeStruct((modes, lanes), jnp.float32),
        scratch_shapes=scratch(unit),
        compiler_params=params,
        cost_estimate=pl.CostEstimate(
            flops=2 * wide * high * lanes * (depth + modes), bytes_accessed=8000000, transcendentals=0
        ),
        name="near_rows",
    )(origin, first_picks, picks, second_picks, first, second, volume, plane)
    for_first, mid, for_second = pl.pallas_call(
        functools.partial(far_kernel, wide=wide),
        in_specs=given + [vmem] * 4,
        out_specs=[vmem] * 3,
        out_shape=[
            jax.ShapeDtypeStruct((L * L, slots * L), jnp.bfloat16),
            jax.ShapeDtypeStruct((L * L, slots * L), jnp.float32),
            jax.ShapeDtypeStruct((L * L, slots * L), jnp.bfloat16),
        ],
        scratch_shapes=scratch(HALF) + [pltpu.VMEM((modes, lanes), jnp.float32)],
        compiler_params=params,
        name="far_rows",
    )(
        origin, first_picks, picks, second_picks, first, second, first_halo, second_halo, plane, near
    )
    from_first, from_second = exchange(for_first, "bank", True), exchange(for_second, "bank", False)

    live_slots = jnp.arange(slots) < box_counts[0, 0]
    matches = orientations[0, 0][:, :, None] == jnp.arange(R)[None, None, :]
    multiplicity = jnp.sum(
        jnp.where(matches, orient_weight[0, 0][:, :, None].astype(jnp.float32), 0.0), axis=1
    )
    multiplicity = jnp.where(live_slots[:, None], multiplicity, 0.0).astype(jnp.bfloat16)
    parts = 2
    mine = pl.pallas_call(
        join_kernel,
        out_shape=[jax.ShapeDtypeStruct((slots // parts, F + R + 128), jnp.bfloat16)] * parts,
        scratch_shapes=[pltpu.VMEM((slots, F), jnp.float32)],
        compiler_params=params,
        name="join",
    )(mid, from_first, from_second, multiplicity)
    return gather_score(mine, reference_bank)


def solution(mesh):
    in_specs = (
        P("tile", "bank", None),
        P(None, "tile", "bank", None),
        P("tile", "bank"),
        P("tile", "bank", None, None),
        P("tile", "bank", None, None),
        P("bank", None, None),
    )
    out_specs = (P("bank", None, None), P("bank", None))
    return jax.shard_map(body, mesh=mesh, in_specs=in_specs, out_specs=out_specs, check_vma=False)
```

```python
import functools

import jax
import jax.numpy as jnp
import numpy as np
from jax import lax
from jax.experimental import pallas as pl
from jax.experimental.pallas import tpu as pltpu
from jax.sharding import PartitionSpec as P

B = 96
L = 16
R = 256
F = L * L * L
HALF = B // 2
TERMS = L // 2
EPSILON = 1e-06
MIB = 1024 * 1024


def waves(count):
    steps = 2.0 * np.pi * np.outer(np.arange(TERMS + 1), np.arange(count)) / B
    return np.cos(steps) / np.sqrt(B), np.sin(steps) / np.sqrt(B)


def depth_tables(depth):
    cos, sin = waves(depth)
    first = np.concatenate([cos, sin[1:TERMS]], axis=0)
    second = np.concatenate([sin, -cos[1:TERMS]], axis=0)
    repeat = 128 // L
    return (
        np.tile(first.T, (1, repeat)).astype(np.float32),
        np.tile(second.T, (1, repeat)).astype(np.float32),
    )


def plane_table(wide, high):
    cos_x, sin_x = waves(wide)
    cos_y, sin_y = waves(high)
    along_x = np.concatenate([cos_x, sin_x[1:]], axis=0)
    along_y = np.concatenate([cos_y[1:], sin_y[1:]], axis=0)
    main = np.einsum("ax,by->abxy", along_x, along_y).reshape(-1, wide * high)
    order = np.concatenate([along_x[1:], along_x[:1]], axis=0)
    flat = np.einsum("ax,y->axy", order, cos_y[0]).reshape(-1, wide * high)
    rows = np.concatenate([main, flat], axis=0)
    pad = -rows.shape[0] % 16
    return np.concatenate([rows, np.zeros((pad, rows.shape[1]))], axis=0).astype(np.float32)


def spread(origin_ref, corner_refs, lanes):
    slots = corner_refs[0].shape[3]
    box = lax.broadcasted_iota(jnp.int32, (slots, lanes), 0)
    lane = lax.broadcasted_iota(jnp.int32, (slots, lanes), 1)
    row = lax.broadcasted_iota(jnp.int32, (8, slots), 0)
    origin = jnp.where(row == 0, origin_ref[0], jnp.where(row == 1, origin_ref[1], 0))
    total = jnp.zeros((8, lanes), jnp.float32)
    for k, corner_ref in enumerate(corner_refs):
        corners = jnp.zeros((8, slots), jnp.int32)
        for axis in range(3):
            corners = jnp.where(row == axis, corner_ref[axis, 0], corners)
        corners = (corners - origin).astype(jnp.float32).astype(jnp.bfloat16)
        pick = jnp.where(lane // L == box + k * slots, 1.0, 0.0).astype(jnp.bfloat16)
        total += jnp.dot(corners, pick, preferred_element_type=jnp.float32)
    return total


def turns(terms, shift):
    turn = (terms * shift).astype(jnp.int32)
    turn = lax.rem(turn, B)
    angle = turn.astype(jnp.float32) * (2.0 * np.pi / B)
    return jnp.cos(angle), jnp.sin(angle)


def prepare(origin_ref, corner_refs, first_ref, second_ref, depth_ref, high_ref):
    depth, lanes = depth_ref.shape
    where = spread(origin_ref, corner_refs, lanes)
    start_y, start_z = where[1:2], where[2:3]
    lane = lax.rem(lax.broadcasted_iota(jnp.int32, (1, lanes), 1), L)
    term = jnp.where(lane <= TERMS, lane, lane - TERMS).astype(jnp.float32)
    cos, sin = turns(term, start_z)
    copies = lanes // first_ref.shape[1]
    first = jnp.concatenate([first_ref[...]] * copies, axis=1)
    second = jnp.concatenate([second_ref[...]] * copies, axis=1)
    z = lax.broadcasted_iota(jnp.int32, (depth, lanes), 0).astype(jnp.float32) - start_z
    table = jnp.where((z >= 0) & (z < B), first * cos + second * sin, 0.0)
    depth_ref[...] = table.astype(jnp.bfloat16)
    y = lax.broadcasted_iota(jnp.int32, high_ref.shape, 0).astype(jnp.float32) - start_y
    high_ref[...] = jnp.where((y >= 0) & (y < B), 1.0, 0.0)
    return where[0:1]


def block_modes(voxels, at_x, turn, start_x, depth_ref, high_ref, part_ref, plane_ref):
    count, high, depth = voxels.shape
    offset = at_x - start_x
    for x in range(0, count, 4):
        rows = voxels[x : x + 4].reshape(4 * high, depth)
        first = jnp.dot(rows, depth_ref[...], preferred_element_type=jnp.float32)
        for i in range(4):
            at = offset + float(x + i)
            live = high_ref[...] * jnp.where((at >= 0) & (at < B), 1.0, 0.0)
            kept = first[i * high : (i + 1) * high] * live
            part_ref[pl.ds((x + i) * high, high), :] = kept.astype(jnp.bfloat16)
    length = count * high
    total = jnp.dot(
        plane_ref[:, :length], part_ref[:length], preferred_element_type=jnp.float32
    )
    return total if turn is None else moved(total, turn)


def turn_of(at_x):
    angles = 2.0 * np.pi * np.arange(1, TERMS + 1) * at_x / B
    return [float(c) for c in np.cos(angles)], [float(s) for s in np.sin(angles)]


def either(flag, one, other):
    return tuple([jnp.where(flag, a, b) for a, b in zip(u, v)] for u, v in zip(one, other))


def moved(total, turn):
    group, blocks = 2 * TERMS, 2 * TERMS + 1
    rows = [total[a * group : (a + 1) * group] for a in range(blocks)]
    main = blocks * group
    flat_cos, flat_sin = total[main : main + TERMS], total[main + TERMS : main + group]
    out = list(rows)
    term = lax.broadcasted_iota(jnp.int32, flat_cos.shape, 0)
    flat_c, flat_s = jnp.zeros_like(flat_cos), jnp.zeros_like(flat_cos)
    for j, (c, s) in enumerate(zip(*turn)):
        out[1 + j] = rows[1 + j] * c - rows[1 + TERMS + j] * s
        out[1 + TERMS + j] = rows[1 + j] * s + rows[1 + TERMS + j] * c
        flat_c = jnp.where(term == j, c, flat_c)
        flat_s = jnp.where(term == j, s, flat_s)
    out += [
        flat_cos * flat_c - flat_sin * flat_s,
        flat_cos * flat_s + flat_sin * flat_c,
        total[main + group :],
    ]
    return jnp.concatenate(out, axis=0)


def near_kernel(
    origin_ref, first_pick_ref, pick_ref, second_pick_ref, first_ref, second_ref, volume_ref, plane_ref,
    total_ref, depth_ref, high_ref, part_ref,
):
    corner_refs = (first_pick_ref, pick_ref, second_pick_ref)
    start_x = prepare(origin_ref, corner_refs, first_ref, second_ref, depth_ref, high_ref)
    unit = part_ref.shape[0] // volume_ref.shape[1]
    for x in range(0, volume_ref.shape[0], unit):
        added = block_modes(
            volume_ref[x : x + unit], float(x), turn_of(x) if x else None, start_x,
            depth_ref, high_ref, part_ref, plane_ref,
        )
        total_ref[...] = added if x == 0 else total_ref[...] + added


def rotate(total, start_x, start_y):
    lanes = total.shape[1]
    term = (lax.broadcasted_iota(jnp.int32, (TERMS, lanes), 0) + 1).astype(jnp.float32)
    cos_x, sin_x = turns(term, start_x)
    cos_y, sin_y = turns(term, start_y)
    blocks = 2 * TERMS + 1
    main = blocks * 2 * TERMS
    flat_cos = total[main : main + TERMS]
    flat_sin = total[main + TERMS : main + 2 * TERMS]
    flat_zero = total[main + 2 * TERMS : main + 2 * TERMS + 1]
    flats = (
        [flat_zero]
        + [flat_cos[j : j + 1] for j in range(TERMS)]
        + [flat_sin[j : j + 1] for j in range(TERMS)]
    )
    last = lax.broadcasted_iota(jnp.int32, (TERMS, lanes), 0) == TERMS - 1
    turned = []
    for a in range(blocks):
        cos = total[a * 2 * TERMS : a * 2 * TERMS + TERMS]
        sin = total[a * 2 * TERMS + TERMS : (a + 1) * 2 * TERMS]
        low = cos * cos_y + sin * sin_y
        high = sin * cos_y - cos * sin_y
        turned.append((low, jnp.where(last, flats[a], high)))
    rows = [None] * (2 * TERMS)
    rows[0] = turned[0]
    for j in range(1, TERMS + 1):
        c, s = cos_x[j - 1 : j], sin_x[j - 1 : j]
        cos, sin = turned[j], turned[TERMS + j]
        rows[j] = tuple(u * c + v * s for u, v in zip(cos, sin))
        if j < TERMS:
            rows[TERMS + j] = tuple(v * c - u * s for u, v in zip(cos, sin))
    return jnp.concatenate([half for pair in rows for half in pair], axis=0)


def far_kernel(
    origin_ref, first_pick_ref, pick_ref, second_pick_ref, first_ref, second_ref, first_halo_ref, second_halo_ref, plane_ref,
    near_ref, first_out_ref, own_ref, second_out_ref, depth_ref, high_ref, part_ref, total_ref, *, wide,
):
    corner_refs = (first_pick_ref, pick_ref, second_pick_ref)
    start_x = prepare(origin_ref, corner_refs, first_ref, second_ref, depth_ref, high_ref)
    where = spread(origin_ref, corner_refs, total_ref.shape[1])
    total_ref[...] = near_ref[...]
    even = origin_ref[2] == 0
    below, above = turn_of(-HALF), turn_of(wide)
    sides = (
        (first_halo_ref, jnp.where(even, wide, -HALF), either(even, above, below)),
        (second_halo_ref, jnp.where(even, -HALF, wide), either(even, below, above)),
    )
    for voxels_ref, at_x, turn in sides:
        total_ref[...] += block_modes(
            voxels_ref[...], at_x.astype(jnp.float32), turn, start_x,
            depth_ref, high_ref, part_ref, plane_ref,
        )
    rows = rotate(total_ref[...], start_x, where[1:2])
    width = own_ref.shape[1]
    first_out_ref[...] = rows[:, :width].astype(jnp.bfloat16)
    own_ref[...] = rows[:, width : 2 * width]
    second_out_ref[...] = rows[:, 2 * width :].astype(jnp.bfloat16)


def join_kernel(own_ref, left_ref, right_ref, multiplicity_ref, *refs):
    outs, wide_ref = refs[:-1], refs[-1]
    total = own_ref[...] + left_ref[...].astype(jnp.float32) + right_ref[...].astype(jnp.float32)
    total = total.astype(jnp.bfloat16)
    rows, lanes = total.shape
    slots = lanes // L
    k = lax.broadcasted_iota(jnp.int32, (lanes, L * L), 0)
    lane = lax.broadcasted_iota(jnp.int32, (lanes, L * L), 1)
    gap = k - lax.rem(lane, L)
    row = lax.rem(lax.broadcasted_iota(jnp.int32, (rows, L * L), 0), L)
    place = jnp.where(row == L - 1, 0, row + 1)
    keep = jnp.where(
        place == lax.broadcasted_iota(jnp.int32, (rows, L * L), 1) // L, 1.0, 0.0
    )
    sums = jnp.where(
        lax.broadcasted_iota(jnp.int32, (L, rows), 1) // L
        == lax.broadcasted_iota(jnp.int32, (L, rows), 0),
        1.0,
        0.0,
    ).astype(jnp.bfloat16)
    for s in range(slots):
        copies = jnp.where(gap == s * L, 1.0, 0.0).astype(jnp.bfloat16)
        spread_rows = jnp.dot(total, copies, preferred_element_type=jnp.float32) * keep
        feature = jnp.dot(
            sums, spread_rows.astype(jnp.bfloat16), preferred_element_type=jnp.float32
        )
        for a in range(L):
            wide_ref[s : s + 1, a * L * L : (a + 1) * L * L] = feature[a : a + 1]
    wide = wide_ref[...]
    norm = jnp.sqrt(jnp.mean(wide * wide, axis=1, keepdims=True) + EPSILON)
    high = norm.astype(jnp.bfloat16).astype(jnp.float32)
    tail = lax.broadcasted_iota(jnp.int32, (slots, 128), 1)
    tail = jnp.where(tail == 0, high, jnp.where(tail == 1, norm - high, 0.0))
    row = jnp.concatenate(
        [wide.astype(jnp.bfloat16), multiplicity_ref[...], tail.astype(jnp.bfloat16)], axis=1
    )
    for k, out_ref in enumerate(outs):
        count = out_ref.shape[0]
        out_ref[...] = row[k * count : (k + 1) * count]


def block_copies(blocks, rows_ref, tail_ref, sems):
    copies, at = [], 0
    for k, block in enumerate(blocks):
        count = block.shape[0]
        place = pl.ds(at, count)
        copies.append(
            pltpu.make_async_copy(block.at[:, pl.ds(0, F)], rows_ref.at[place], sems.at[2 * k])
        )
        if tail_ref is not None:
            copies.append(
                pltpu.make_async_copy(
                    block.at[:, pl.ds(F, block.shape[1] - F)], tail_ref.at[place], sems.at[2 * k + 1]
                )
            )
        at += count
    return copies


def read_tail(bank_ref, tail, tail_ref, multiplicity_ref, orients):
    tail_ref[...] = tail.astype(jnp.float32).T
    start = pl.multiple_of(bank_ref[0] * orients, orients)
    norm = tail_ref[R : R + 1, :] + tail_ref[R + 1 : R + 2, :]
    multiplicity_ref[...] = tail_ref[pl.ds(start, orients), :] / (F * norm)


def inverse_norms(bank_rows):
    wide = bank_rows.astype(jnp.float32)
    return 1.0 / jnp.sqrt(jnp.mean(wide * wide, axis=1, keepdims=True) + EPSILON)


def weigh(bank_rows, inverse, rows, multiplicity, count):
    scores = lax.dot_general(
        bank_rows, rows, (((1,), (1,)), ((), ())), preferred_element_type=jnp.float32
    )
    multiplicity = jnp.concatenate([multiplicity] * count, axis=0)
    return (multiplicity * jnp.maximum(scores * inverse, 0.0)).astype(jnp.bfloat16)


def weigh_kernel(index_ref, *refs, blocks, known):
    sources, bank_ref = refs[:blocks], refs[blocks]
    if known:
        norms_ref, out_ref = refs[blocks + 1 : blocks + 3]
    else:
        out_ref, norms_ref = refs[blocks + 1 : blocks + 3]
    rows_ref, tail_ref, turned_ref, multiplicity_ref, sems = refs[blocks + 3 :]
    count, orients, width = bank_ref.shape

    @pl.when(pl.program_id(0) == 0)
    def _():
        copies = block_copies(sources, rows_ref, tail_ref, sems)
        for copy in copies:
            copy.start()
        for copy in copies:
            copy.wait()
        read_tail(index_ref, tail_ref[...], turned_ref, multiplicity_ref, orients)

    bank = bank_ref[...].reshape(count * orients, width)
    if known:
        inverse = norms_ref[...].reshape(count * orients, norms_ref.shape[2])[:, :1]
    else:
        inverse = inverse_norms(bank)
        norms_ref[...] = jnp.broadcast_to(inverse, (count * orients, norms_ref.shape[2])).reshape(
            norms_ref.shape
        )
    weights = weigh(bank, inverse, rows_ref[...], multiplicity_ref[...], count)
    out_ref[...] = weights.reshape(out_ref.shape)


def sum_kernel(index_ref, *refs, early, blocks, late, group):
    parts, sources = refs[:early], refs[early : early + blocks]
    norms_ref, bank_ref, out_ref, sums_ref = refs[early + blocks : early + blocks + 4]
    rows_ref, last_ref, tail_ref, turned_ref, multiplicity_ref, weights_ref, sems, last_sems = refs[
        early + blocks + 4 :
    ]
    count, orients, width = out_ref.shape
    boxes, last = rows_ref.shape[0], last_ref.shape[0]
    step = pl.program_id(0)

    @pl.when(step == 0)
    def _():
        copies = block_copies(sources, rows_ref, None, sems)
        urgent = block_copies(sources[blocks - late :], last_ref, tail_ref, last_sems)
        for copy in urgent + copies:
            copy.start()
        for copy in urgent:
            copy.wait()
        read_tail(index_ref, tail_ref[...], turned_ref, multiplicity_ref, orients)
        for c in range(0, bank_ref.shape[0], group):
            bank = bank_ref[c : c + group].reshape(group * orients, width)
            inverse = norms_ref[c : c + group].reshape(group * orients, norms_ref.shape[2])[:, :1]
            weights = weigh(bank, inverse, last_ref[...], multiplicity_ref[...], group)
            weights_ref[c : c + group] = weights.reshape(group, orients, last)
        for copy in copies:
            copy.wait()

    known = [part[...].reshape(count * orients, part.shape[2]) for part in parts]
    at = pl.multiple_of(step * count, count)
    known.append(weights_ref[pl.ds(at, count)].reshape(count * orients, last))
    weights = jnp.concatenate(known, axis=1)
    total = jnp.dot(weights, rows_ref[...], preferred_element_type=jnp.float32)
    out_ref[...] = total.reshape(out_ref.shape)
    ones = jnp.ones((8, boxes), jnp.bfloat16)
    sums = lax.dot_general(
        ones, weights, (((1,), (1,)), ((), ())), preferred_element_type=jnp.float32
    )
    for c in range(count):
        sums_ref[pl.ds(step * count + c, 1), :] = sums[:1, c * orients : (c + 1) * orients]


def score_plain(rows, bank):
    local_rows = bank.shape[0]
    start = F + lax.axis_index("bank") * local_rows
    multiplicity = lax.dynamic_slice_in_dim(rows, start, local_rows, 1).astype(jnp.float32)
    norm = rows[:, F + R].astype(jnp.float32) + rows[:, F + R + 1].astype(jnp.float32)
    features = rows[:, :F]
    scores = jnp.einsum("if,rcf->irc", features, bank, preferred_element_type=jnp.float32)
    wide = bank.astype(jnp.float32)
    bank_norm = jnp.sqrt(jnp.mean(wide * wide, axis=2) + EPSILON)
    correl = scores / (F * norm[:, None, None] * bank_norm[None])
    weights = (multiplicity[:, :, None] * jnp.maximum(correl, 0.0)).astype(jnp.bfloat16)
    class_sums = jnp.einsum("irc,if->rcf", weights, features, preferred_element_type=jnp.float32)
    return class_sums, jnp.sum(weights.astype(jnp.float32), axis=0)


def exchange(value, axis, first):
    count = lax.axis_size(axis)
    pairs = []
    for i in range(0 if first else 1, count - 1, 2):
        pairs += [(i, i + 1), (i + 1, i)]
    return lax.ppermute(value, axis, pairs)


def gather_score(mine, reference_bank):
    tiles, banks = lax.axis_size("tile"), lax.axis_size("bank")
    local_rows, classes, width = reference_bank.shape
    boxes = tiles * banks * sum(part.shape[0] for part in mine)
    if banks != 4 or tiles & (tiles - 1) or tiles < 4 or boxes > 1024 or classes % 5:
        rows = jnp.concatenate(mine, axis=0)
        for axis in ("bank", "tile"):
            rows = lax.all_gather(rows, axis, axis=0, tiled=True)
        return score_plain(rows, reference_bank)
    bank = jnp.transpose(reference_bank, (1, 0, 2))
    early, late = mine

    def along_x(value):
        return lax.ppermute(value, "bank", [(0, 1), (1, 0), (2, 3), (3, 2)])

    def along_y(value):
        return lax.ppermute(value, "bank", [(0, 2), (2, 0), (1, 3), (3, 1)])

    def swap(*values):
        return [lax.ppermute(value, "tile", [(i, i ^ 1) for i in range(tiles)]) for value in values]

    def line_of(part):
        others = [
            lax.ppermute(part, "tile", [(i, i ^ by) for i in range(tiles)])
            for by in range(2, tiles, 2)
        ]
        return jnp.concatenate([part] + others, axis=0)

    def with_swap(*values):
        joined = jnp.concatenate(values, axis=0) if len(values) > 1 else values[0]
        return [*values, *swap(joined)]

    early_line = line_of(early)
    late, early_line = lax.optimization_barrier((late, early_line))
    from_x, from_y = along_x(early_line), along_y(early_line)
    late_line = line_of(late)
    half = early_line.shape[0] // 2
    to_x = jnp.concatenate([from_y[half:], late_line], axis=0)
    to_y = jnp.concatenate([from_x[:half], late_line], axis=0)
    blocks = [with_swap(early_line, from_x, from_y)]
    next_x, next_y = along_x(to_x), along_y(to_y)
    first, norms = weigh_blocks(blocks[0], bank)
    first, next_x, next_y = lax.optimization_barrier((first, next_x, next_y))
    last_x, last_y = along_x(next_y[half + half :]), along_y(next_x[half : half + half])
    blocks.append(with_swap(late_line, next_x, next_y))
    second = weigh_blocks(blocks[1], bank, norms)
    second, last_x, last_y = lax.optimization_barrier((second, last_x, last_y))
    last = with_swap(last_x, last_y)
    out, sums = sum_blocks([first, second], sum(blocks, []), last, norms, bank)
    return jnp.transpose(out, (1, 0, 2)), jnp.transpose(sums, (1, 0))


CLASSES = 5


def bank_index():
    return lax.axis_index("bank").astype(jnp.int32)[None]


def weigh_blocks(blocks, bank, norms=None):
    classes, orients, width = bank.shape
    boxes = sum(block.shape[0] for block in blocks)
    tail = blocks[0].shape[1] - F
    known = norms is not None
    norm_spec = pl.BlockSpec((CLASSES, orients, 128), lambda i: (i, 0, 0))
    out_spec = pl.BlockSpec((CLASSES, orients, boxes), lambda i: (i, 0, 0))
    out_shape = jax.ShapeDtypeStruct((classes, orients, boxes), jnp.bfloat16)
    norm_shape = jax.ShapeDtypeStruct((classes, orients, 128), jnp.float32)
    return pl.pallas_call(
        functools.partial(weigh_kernel, blocks=len(blocks), known=known),
        grid=(classes // CLASSES,),
        in_specs=[pl.BlockSpec(memory_space=pltpu.SMEM)]
        + [pl.BlockSpec(memory_space=pl.ANY)] * len(blocks)
        + [pl.BlockSpec((CLASSES, orients, width), lambda i: (i, 0, 0))]
        + ([norm_spec] if known else []),
        out_specs=out_spec if known else [out_spec, norm_spec],
        out_shape=out_shape if known else [out_shape, norm_shape],
        scratch_shapes=[
            pltpu.VMEM((boxes, F), jnp.bfloat16),
            pltpu.VMEM((boxes, tail), jnp.bfloat16),
            pltpu.VMEM((tail, boxes), jnp.float32),
            pltpu.VMEM((orients, boxes), jnp.float32),
            pltpu.SemaphoreType.DMA((2 * len(blocks),)),
        ],
        compiler_params=pltpu.CompilerParams(vmem_limit_bytes=18 * MIB),
        cost_estimate=pl.CostEstimate(
            flops=2 * boxes * classes * orients * width,
            bytes_accessed=2 * classes * orients * width,
            transcendentals=0,
        ),
        name="weigh",
    )(bank_index(), *blocks, bank, *([norms] if known else []))


def sum_blocks(parts, blocks, late, norms, bank):
    classes, orients, width = bank.shape
    blocks = blocks + late
    boxes = sum(block.shape[0] for block in blocks)
    last = sum(block.shape[0] for block in late)
    tail = blocks[0].shape[1] - F
    vmem = pl.BlockSpec(memory_space=pltpu.VMEM)
    return pl.pallas_call(
        functools.partial(
            sum_kernel, early=len(parts), blocks=len(blocks), late=len(late), group=CLASSES
        ),
        grid=(classes // CLASSES,),
        in_specs=[pl.BlockSpec(memory_space=pltpu.SMEM)]
        + [pl.BlockSpec((CLASSES, orients, part.shape[2]), lambda i: (i, 0, 0)) for part in parts]
        + [pl.BlockSpec(memory_space=pl.ANY)] * len(blocks)
        + [vmem, vmem],
        out_specs=[
            pl.BlockSpec((CLASSES, orients, width), lambda i: (i, 0, 0)),
            pl.BlockSpec((classes, orients), lambda i: (0, 0)),
        ],
        out_shape=[
            jax.ShapeDtypeStruct((classes, orients, width), jnp.float32),
            jax.ShapeDtypeStruct((classes, orients), jnp.float32),
        ],
        scratch_shapes=[
            pltpu.VMEM((boxes, F), jnp.bfloat16),
            pltpu.VMEM((last, F), jnp.bfloat16),
            pltpu.VMEM((last, tail), jnp.bfloat16),
            pltpu.VMEM((tail, last), jnp.float32),
            pltpu.VMEM((orients, last), jnp.float32),
            pltpu.VMEM((classes, orients, last), jnp.bfloat16),
            pltpu.SemaphoreType.DMA((2 * len(blocks),)),
            pltpu.SemaphoreType.DMA((2 * len(late),)),
        ],
        compiler_params=pltpu.CompilerParams(vmem_limit_bytes=34 * MIB),
        cost_estimate=pl.CostEstimate(
            flops=2 * boxes * classes * orients * width,
            bytes_accessed=4 * classes * orients * width,
            transcendentals=0,
        ),
        name="class_sums",
    )(bank_index(), *parts, *blocks, norms, bank)


def body(volume, pick_list, box_counts, orientations, orient_weight, reference_bank):
    wide, high, depth = volume.shape
    slots = pick_list.shape[3]
    tile, bank = lax.axis_index("tile"), lax.axis_index("bank")
    side = lax.rem(tile, 2)
    rest = wide - HALF
    to_first = lax.dynamic_slice_in_dim(volume, jnp.where(side == 0, rest, 0), HALF, 0)
    to_second = lax.dynamic_slice_in_dim(volume, jnp.where(side == 0, 0, rest), HALF, 0)
    first_halo = exchange(to_first, "tile", True)
    second_halo = exchange(to_second, "tile", False)
    picks, first_halo = lax.optimization_barrier((pick_list, first_halo))
    first_picks, second_picks = exchange(picks, "bank", True), exchange(picks, "bank", False)
    origin = jnp.stack([tile * wide + HALF, bank * high + HALF, side]).astype(jnp.int32)

    first, second = depth_tables(depth)
    plane = jnp.asarray(plane_table(HALF, high), jnp.bfloat16)
    modes, lanes = plane.shape[0], 3 * slots * L
    unit = 32

    def scratch(count):
        return [
            pltpu.VMEM((depth, lanes), jnp.bfloat16),
            pltpu.VMEM((high, lanes), jnp.float32),
            pltpu.VMEM((count * high, lanes), jnp.bfloat16),
        ]

    params = pltpu.CompilerParams(vmem_limit_bytes=24 * MIB)
    vmem = pl.BlockSpec(memory_space=pltpu.VMEM)
    given = [pl.BlockSpec(memory_space=pltpu.SMEM)] + [vmem] * 5
    near = pl.pallas_call(
        near_kernel,
        in_specs=given + [vmem] * 2,
        out_specs=vmem,
        out_shape=jax.ShapeDtypeStruct((modes, lanes), jnp.float32),
        scratch_shapes=scratch(unit),
        compiler_params=params,
        cost_estimate=pl.CostEstimate(
            flops=2 * wide * high * lanes * (depth + modes), bytes_accessed=8000000, transcendentals=0
        ),
        name="near_rows",
    )(origin, first_picks, picks, second_picks, first, second, volume, plane)
    for_first, mid, for_second = pl.pallas_call(
        functools.partial(far_kernel, wide=wide),
        in_specs=given + [vmem] * 4,
        out_specs=[vmem] * 3,
        out_shape=[
            jax.ShapeDtypeStruct((L * L, slots * L), jnp.bfloat16),
            jax.ShapeDtypeStruct((L * L, slots * L), jnp.float32),
            jax.ShapeDtypeStruct((L * L, slots * L), jnp.bfloat16),
        ],
        scratch_shapes=scratch(HALF) + [pltpu.VMEM((modes, lanes), jnp.float32)],
        compiler_params=params,
        name="far_rows",
    )(
        origin, first_picks, picks, second_picks, first, second, first_halo, second_halo, plane, near
    )
    from_first, from_second = exchange(for_first, "bank", True), exchange(for_second, "bank", False)

    live_slots = jnp.arange(slots) < box_counts[0, 0]
    matches = orientations[0, 0][:, :, None] == jnp.arange(R)[None, None, :]
    multiplicity = jnp.sum(
        jnp.where(matches, orient_weight[0, 0][:, :, None].astype(jnp.float32), 0.0), axis=1
    )
    multiplicity = jnp.where(live_slots[:, None], multiplicity, 0.0).astype(jnp.bfloat16)
    parts = 2
    mine = pl.pallas_call(
        join_kernel,
        out_shape=[jax.ShapeDtypeStruct((slots // parts, F + R + 128), jnp.bfloat16)] * parts,
        scratch_shapes=[pltpu.VMEM((slots, F), jnp.float32)],
        compiler_params=params,
        name="join",
    )(mid, from_first, from_second, multiplicity)
    return gather_score(mine, reference_bank)


def solution(mesh):
    in_specs = (
        P("tile", "bank", None),
        P(None, "tile", "bank", None),
        P("tile", "bank"),
        P("tile", "bank", None, None),
        P("tile", "bank", None, None),
        P("bank", None, None),
    )
    out_specs = (P("bank", None, None), P("bank", None))
    return jax.shard_map(body, mesh=mesh, in_specs=in_specs, out_specs=out_specs, check_vma=False)
```

```python
import functools

import jax
import jax.numpy as jnp
import numpy as np
from jax import lax
from jax.experimental import pallas as pl
from jax.experimental.pallas import tpu as pltpu
from jax.sharding import PartitionSpec as P

B = 96
L = 16
R = 256
F = L * L * L
HALF = B // 2
TERMS = L // 2
EPSILON = 1e-06
MIB = 1024 * 1024


def waves(count):
    steps = 2.0 * np.pi * np.outer(np.arange(TERMS + 1), np.arange(count)) / B
    return np.cos(steps) / np.sqrt(B), np.sin(steps) / np.sqrt(B)


def depth_tables(depth):
    cos, sin = waves(depth)
    first = np.concatenate([cos, sin[1:TERMS]], axis=0)
    second = np.concatenate([sin, -cos[1:TERMS]], axis=0)
    repeat = 128 // L
    return (
        np.tile(first.T, (1, repeat)).astype(np.float32),
        np.tile(second.T, (1, repeat)).astype(np.float32),
    )


def plane_table(wide, high):
    cos_x, sin_x = waves(wide)
    cos_y, sin_y = waves(high)
    along_x = np.concatenate([cos_x, sin_x[1:]], axis=0)
    along_y = np.concatenate([cos_y[1:], sin_y[1:]], axis=0)
    main = np.einsum("ax,by->abxy", along_x, along_y).reshape(-1, wide * high)
    order = np.concatenate([along_x[1:], along_x[:1]], axis=0)
    flat = np.einsum("ax,y->axy", order, cos_y[0]).reshape(-1, wide * high)
    rows = np.concatenate([main, flat], axis=0)
    pad = -rows.shape[0] % 16
    return np.concatenate([rows, np.zeros((pad, rows.shape[1]))], axis=0).astype(np.float32)


def spread(origin_ref, corner_refs, lanes):
    slots = corner_refs[0].shape[3]
    box = lax.broadcasted_iota(jnp.int32, (slots, lanes), 0)
    lane = lax.broadcasted_iota(jnp.int32, (slots, lanes), 1)
    row = lax.broadcasted_iota(jnp.int32, (8, slots), 0)
    origin = jnp.where(row == 0, origin_ref[0], jnp.where(row == 1, origin_ref[1], 0))
    total = jnp.zeros((8, lanes), jnp.float32)
    for k, corner_ref in enumerate(corner_refs):
        corners = jnp.zeros((8, slots), jnp.int32)
        for axis in range(3):
            corners = jnp.where(row == axis, corner_ref[axis, 0], corners)
        corners = (corners - origin).astype(jnp.float32).astype(jnp.bfloat16)
        pick = jnp.where(lane // L == box + k * slots, 1.0, 0.0).astype(jnp.bfloat16)
        total += jnp.dot(corners, pick, preferred_element_type=jnp.float32)
    return total


def turns(terms, shift):
    turn = (terms * shift).astype(jnp.int32)
    turn = lax.rem(turn, B)
    angle = turn.astype(jnp.float32) * (2.0 * np.pi / B)
    return jnp.cos(angle), jnp.sin(angle)


def prepare(origin_ref, corner_refs, first_ref, second_ref, depth_ref, high_ref, where_ref):
    depth, lanes = depth_ref.shape
    where = spread(origin_ref, corner_refs, lanes)
    where_ref[...] = where
    start_y, start_z = where[1:2], where[2:3]
    lane = lax.rem(lax.broadcasted_iota(jnp.int32, (1, lanes), 1), L)
    term = jnp.where(lane <= TERMS, lane, lane - TERMS).astype(jnp.float32)
    cos, sin = turns(term, start_z)
    copies = lanes // first_ref.shape[1]
    first = jnp.concatenate([first_ref[...]] * copies, axis=1)
    second = jnp.concatenate([second_ref[...]] * copies, axis=1)
    z = lax.broadcasted_iota(jnp.int32, (depth, lanes), 0).astype(jnp.float32) - start_z
    table = jnp.where((z >= 0) & (z < B), first * cos + second * sin, 0.0)
    depth_ref[...] = table.astype(jnp.bfloat16)
    y = lax.broadcasted_iota(jnp.int32, high_ref.shape, 0).astype(jnp.float32) - start_y
    high_ref[...] = jnp.where((y >= 0) & (y < B), 1.0, 0.0)


def block_modes(voxels, at_x, turn, start_x, depth_ref, high_ref, part_ref, plane_ref):
    count, high, depth = voxels.shape
    offset = at_x - start_x
    rows = voxels.reshape(count * high, depth)
    first = jnp.dot(rows, depth_ref[...], preferred_element_type=jnp.float32)
    for x in range(count):
        at = offset + float(x)
        live = high_ref[...] * jnp.where((at >= 0) & (at < B), 1.0, 0.0)
        kept = first[x * high : (x + 1) * high] * live
        part_ref[pl.ds(x * high, high), :] = kept.astype(jnp.bfloat16)
    length = count * high
    total = jnp.dot(
        plane_ref[:, :length], part_ref[:length], preferred_element_type=jnp.float32
    )
    return total if turn is None else moved(total, turn)


def turn_of(at_x):
    angles = 2.0 * np.pi * np.arange(1, TERMS + 1) * at_x / B
    return [float(c) for c in np.cos(angles)], [float(s) for s in np.sin(angles)]


def either(flag, one, other):
    return tuple([jnp.where(flag, a, b) for a, b in zip(u, v)] for u, v in zip(one, other))


def moved(total, turn):
    group, blocks = 2 * TERMS, 2 * TERMS + 1
    rows = [total[a * group : (a + 1) * group] for a in range(blocks)]
    main = blocks * group
    flat_cos, flat_sin = total[main : main + TERMS], total[main + TERMS : main + group]
    out = list(rows)
    term = lax.broadcasted_iota(jnp.int32, flat_cos.shape, 0)
    flat_c, flat_s = jnp.zeros_like(flat_cos), jnp.zeros_like(flat_cos)
    for j, (c, s) in enumerate(zip(*turn)):
        out[1 + j] = rows[1 + j] * c - rows[1 + TERMS + j] * s
        out[1 + TERMS + j] = rows[1 + j] * s + rows[1 + TERMS + j] * c
        flat_c = jnp.where(term == j, c, flat_c)
        flat_s = jnp.where(term == j, s, flat_s)
    out += [
        flat_cos * flat_c - flat_sin * flat_s,
        flat_cos * flat_s + flat_sin * flat_c,
        total[main + group :],
    ]
    return jnp.concatenate(out, axis=0)


def near_kernel(
    origin_ref, first_pick_ref, pick_ref, second_pick_ref, first_ref, second_ref, volume_ref, plane_ref,
    total_ref, depth_ref, high_ref, where_ref, part_ref,
):
    corner_refs = (first_pick_ref, pick_ref, second_pick_ref)
    prepare(origin_ref, corner_refs, first_ref, second_ref, depth_ref, high_ref, where_ref)
    start_x = where_ref[0:1]
    unit = part_ref.shape[0] // volume_ref.shape[1]
    for x in range(0, volume_ref.shape[0], unit):
        added = block_modes(
            volume_ref[x : x + unit], float(x), turn_of(x) if x else None, start_x,
            depth_ref, high_ref, part_ref, plane_ref,
        )
        total_ref[...] = added if x == 0 else total_ref[...] + added


def rotate(total, start_x, start_y):
    lanes = total.shape[1]
    term = (lax.broadcasted_iota(jnp.int32, (TERMS, lanes), 0) + 1).astype(jnp.float32)
    cos_x, sin_x = turns(term, start_x)
    cos_y, sin_y = turns(term, start_y)
    blocks = 2 * TERMS + 1
    main = blocks * 2 * TERMS
    flat_cos = total[main : main + TERMS]
    flat_sin = total[main + TERMS : main + 2 * TERMS]
    flat_zero = total[main + 2 * TERMS : main + 2 * TERMS + 1]
    flats = (
        [flat_zero]
        + [flat_cos[j : j + 1] for j in range(TERMS)]
        + [flat_sin[j : j + 1] for j in range(TERMS)]
    )
    last = lax.broadcasted_iota(jnp.int32, (TERMS, lanes), 0) == TERMS - 1
    turned = []
    for a in range(blocks):
        cos = total[a * 2 * TERMS : a * 2 * TERMS + TERMS]
        sin = total[a * 2 * TERMS + TERMS : (a + 1) * 2 * TERMS]
        low = cos * cos_y + sin * sin_y
        high = sin * cos_y - cos * sin_y
        turned.append((low, jnp.where(last, flats[a], high)))
    rows = [None] * (2 * TERMS)
    rows[0] = turned[0]
    for j in range(1, TERMS + 1):
        c, s = cos_x[j - 1 : j], sin_x[j - 1 : j]
        cos, sin = turned[j], turned[TERMS + j]
        rows[j] = tuple(u * c + v * s for u, v in zip(cos, sin))
        if j < TERMS:
            rows[TERMS + j] = tuple(v * c - u * s for u, v in zip(cos, sin))
    return jnp.concatenate([half for pair in rows for half in pair], axis=0)


def far_kernel(
    side_ref, depth_ref, high_ref, where_ref, first_halo_ref, second_halo_ref, plane_ref, near_ref,
    first_out_ref, own_ref, second_out_ref, part_ref, total_ref, *, wide,
):
    start_x = where_ref[0:1]
    total_ref[...] = near_ref[...]
    even = side_ref[0] == 0
    below, above = turn_of(-HALF), turn_of(wide)
    sides = (
        (first_halo_ref, jnp.where(even, wide, -HALF), either(even, above, below)),
        (second_halo_ref, jnp.where(even, -HALF, wide), either(even, below, above)),
    )
    for voxels_ref, at_x, turn in sides:
        total_ref[...] += block_modes(
            voxels_ref[...], at_x.astype(jnp.float32), turn, start_x,
            depth_ref, high_ref, part_ref, plane_ref,
        )
    rows = rotate(total_ref[...], start_x, where_ref[1:2])
    width = own_ref.shape[1]
    first_out_ref[...] = rows[:, :width].astype(jnp.bfloat16)
    own_ref[...] = rows[:, width : 2 * width]
    second_out_ref[...] = rows[:, 2 * width :].astype(jnp.bfloat16)


def join_kernel(own_ref, left_ref, right_ref, multiplicity_ref, *refs):
    outs, wide_ref = refs[:-1], refs[-1]
    total = own_ref[...] + left_ref[...].astype(jnp.float32) + right_ref[...].astype(jnp.float32)
    total = total.astype(jnp.bfloat16)
    rows, lanes = total.shape
    slots, group = lanes // L, rows // L

    def grid_of(shape, axis):
        return lax.broadcasted_iota(jnp.int32, shape, axis)

    def ones_where(flag):
        return jnp.where(flag, 1.0, 0.0).astype(jnp.bfloat16)

    square = (slots * group, lanes)
    mine = ones_where(grid_of(square, 0) // group == grid_of(square, 1) // L)
    square = (lanes, L * L)
    tiled = ones_where(lax.rem(grid_of(square, 0), L) == lax.rem(grid_of(square, 1), L))
    square = (slots * group, L * L)
    place = lax.rem(grid_of(square, 0), group) + 1
    place = jnp.where(place == group, 0, place)
    keep = ones_where(place == grid_of(square, 1) // L)
    square = (slots, slots * group)
    sums = ones_where(grid_of(square, 1) // group == grid_of(square, 0))
    copies = jnp.concatenate(
        [
            jnp.concatenate([total[a * group : (a + 1) * group]] * slots, axis=0) * mine
            for a in range(L)
        ],
        axis=0,
    )
    placed = jnp.dot(copies, tiled, preferred_element_type=jnp.float32).astype(jnp.bfloat16)
    flat = jnp.concatenate(
        [placed[a * rows : (a + 1) * rows] * keep for a in range(L)], axis=1
    )
    wide_ref[...] = jnp.dot(sums, flat, preferred_element_type=jnp.float32)
    wide = wide_ref[...]
    norm = jnp.sqrt(jnp.mean(wide * wide, axis=1, keepdims=True) + EPSILON)
    high = norm.astype(jnp.bfloat16).astype(jnp.float32)
    tail = lax.broadcasted_iota(jnp.int32, (slots, 128), 1)
    tail = jnp.where(tail == 0, high, jnp.where(tail == 1, norm - high, 0.0))
    row = jnp.concatenate(
        [wide.astype(jnp.bfloat16), multiplicity_ref[...], tail.astype(jnp.bfloat16)], axis=1
    )
    for k, out_ref in enumerate(outs):
        count = out_ref.shape[0]
        out_ref[...] = row[k * count : (k + 1) * count]


def block_copies(blocks, rows_ref, tail_ref, sems):
    copies, at = [], 0
    for k, block in enumerate(blocks):
        count = block.shape[0]
        place = pl.ds(at, count)
        copies.append(
            pltpu.make_async_copy(block.at[:, pl.ds(0, F)], rows_ref.at[place], sems.at[2 * k])
        )
        if tail_ref is not None:
            copies.append(
                pltpu.make_async_copy(
                    block.at[:, pl.ds(F, block.shape[1] - F)], tail_ref.at[place], sems.at[2 * k + 1]
                )
            )
        at += count
    return copies


def read_tail(bank_ref, tail, tail_ref, multiplicity_ref, orients):
    tail_ref[...] = tail.astype(jnp.float32).T
    start = pl.multiple_of(bank_ref[0] * orients, orients)
    norm = tail_ref[R : R + 1, :] + tail_ref[R + 1 : R + 2, :]
    multiplicity_ref[...] = tail_ref[pl.ds(start, orients), :] / (F * norm)


def inverse_norms(bank_rows):
    wide = bank_rows.astype(jnp.float32)
    return 1.0 / jnp.sqrt(jnp.mean(wide * wide, axis=1, keepdims=True) + EPSILON)


def weigh(bank_rows, inverse, rows, multiplicity, count):
    scores = lax.dot_general(
        bank_rows, rows, (((1,), (1,)), ((), ())), preferred_element_type=jnp.float32
    )
    multiplicity = jnp.concatenate([multiplicity] * count, axis=0)
    return (multiplicity * jnp.maximum(scores * inverse, 0.0)).astype(jnp.bfloat16)


def weigh_kernel(index_ref, *refs, blocks, known):
    sources, bank_ref = refs[:blocks], refs[blocks]
    if known:
        norms_ref, out_ref = refs[blocks + 1 : blocks + 3]
    else:
        out_ref, norms_ref = refs[blocks + 1 : blocks + 3]
    rows_ref, tail_ref, turned_ref, multiplicity_ref, sems = refs[blocks + 3 :]
    count, orients, width = bank_ref.shape

    @pl.when(pl.program_id(0) == 0)
    def _():
        copies = block_copies(sources, rows_ref, tail_ref, sems)
        for copy in copies:
            copy.start()
        for copy in copies:
            copy.wait()
        read_tail(index_ref, tail_ref[...], turned_ref, multiplicity_ref, orients)

    bank = bank_ref[...].reshape(count * orients, width)
    if known:
        inverse = norms_ref[...].reshape(count * orients, norms_ref.shape[2])[:, :1]
    else:
        inverse = inverse_norms(bank)
        norms_ref[...] = jnp.broadcast_to(inverse, (count * orients, norms_ref.shape[2])).reshape(
            norms_ref.shape
        )
    weights = weigh(bank, inverse, rows_ref[...], multiplicity_ref[...], count)
    out_ref[...] = weights.reshape(out_ref.shape)


def sum_kernel(index_ref, *refs, early, blocks, late, group):
    parts, sources = refs[:early], refs[early : early + blocks]
    norms_ref, bank_ref, out_ref, sums_ref = refs[early + blocks : early + blocks + 4]
    rows_ref, last_ref, tail_ref, turned_ref, multiplicity_ref, weights_ref, sems, last_sems = refs[
        early + blocks + 4 :
    ]
    count, orients, width = out_ref.shape
    boxes, last = rows_ref.shape[0], last_ref.shape[0]
    step = pl.program_id(0)

    @pl.when(step == 0)
    def _():
        copies = block_copies(sources, rows_ref, None, sems)
        urgent = block_copies(sources[blocks - late :], last_ref, tail_ref, last_sems)
        for copy in urgent + copies:
            copy.start()
        for copy in urgent:
            copy.wait()
        read_tail(index_ref, tail_ref[...], turned_ref, multiplicity_ref, orients)
        for c in range(0, bank_ref.shape[0], group):
            bank = bank_ref[c : c + group].reshape(group * orients, width)
            inverse = norms_ref[c : c + group].reshape(group * orients, norms_ref.shape[2])[:, :1]
            weights = weigh(bank, inverse, last_ref[...], multiplicity_ref[...], group)
            weights_ref[c : c + group] = weights.reshape(group, orients, last)
        for copy in copies:
            copy.wait()

    known = [part[...].reshape(count * orients, part.shape[2]) for part in parts]
    at = pl.multiple_of(step * count, count)
    known.append(weights_ref[pl.ds(at, count)].reshape(count * orients, last))
    weights = jnp.concatenate(known, axis=1)
    total = jnp.dot(weights, rows_ref[...], preferred_element_type=jnp.float32)
    out_ref[...] = total.reshape(out_ref.shape)
    ones = jnp.ones((8, boxes), jnp.bfloat16)
    sums = lax.dot_general(
        ones, weights, (((1,), (1,)), ((), ())), preferred_element_type=jnp.float32
    )
    for c in range(count):
        sums_ref[pl.ds(step * count + c, 1), :] = sums[:1, c * orients : (c + 1) * orients]


def score_plain(rows, bank):
    local_rows = bank.shape[0]
    start = F + lax.axis_index("bank") * local_rows
    multiplicity = lax.dynamic_slice_in_dim(rows, start, local_rows, 1).astype(jnp.float32)
    norm = rows[:, F + R].astype(jnp.float32) + rows[:, F + R + 1].astype(jnp.float32)
    features = rows[:, :F]
    scores = jnp.einsum("if,rcf->irc", features, bank, preferred_element_type=jnp.float32)
    wide = bank.astype(jnp.float32)
    bank_norm = jnp.sqrt(jnp.mean(wide * wide, axis=2) + EPSILON)
    correl = scores / (F * norm[:, None, None] * bank_norm[None])
    weights = (multiplicity[:, :, None] * jnp.maximum(correl, 0.0)).astype(jnp.bfloat16)
    class_sums = jnp.einsum("irc,if->rcf", weights, features, preferred_element_type=jnp.float32)
    return class_sums, jnp.sum(weights.astype(jnp.float32), axis=0)


def exchange(value, axis, first):
    count = lax.axis_size(axis)
    pairs = []
    for i in range(0 if first else 1, count - 1, 2):
        pairs += [(i, i + 1), (i + 1, i)]
    return lax.ppermute(value, axis, pairs)


def gather_score(mine, reference_bank):
    tiles, banks = lax.axis_size("tile"), lax.axis_size("bank")
    local_rows, classes, width = reference_bank.shape
    boxes = tiles * banks * sum(part.shape[0] for part in mine)
    if banks != 4 or tiles & (tiles - 1) or tiles < 4 or boxes > 1024 or classes % 5:
        rows = jnp.concatenate(mine, axis=0)
        for axis in ("bank", "tile"):
            rows = lax.all_gather(rows, axis, axis=0, tiled=True)
        return score_plain(rows, reference_bank)
    bank = jnp.transpose(reference_bank, (1, 0, 2))
    early, late = mine

    def along_x(value):
        return lax.ppermute(value, "bank", [(0, 1), (1, 0), (2, 3), (3, 2)])

    def along_y(value):
        return lax.ppermute(value, "bank", [(0, 2), (2, 0), (1, 3), (3, 1)])

    def swap(*values):
        return [lax.ppermute(value, "tile", [(i, i ^ 1) for i in range(tiles)]) for value in values]

    def line_of(part):
        others = [
            lax.ppermute(part, "tile", [(i, i ^ by) for i in range(tiles)])
            for by in range(2, tiles, 2)
        ]
        return jnp.concatenate([part] + others, axis=0)

    def with_swap(*values):
        joined = jnp.concatenate(values, axis=0) if len(values) > 1 else values[0]
        return [*values, *swap(joined)]

    early_line = line_of(early)
    late, early_line = lax.optimization_barrier((late, early_line))
    from_x, from_y = along_x(early_line), along_y(early_line)
    late_line = line_of(late)
    half = early_line.shape[0] // 2
    to_x = jnp.concatenate([from_y[half:], late_line], axis=0)
    to_y = jnp.concatenate([from_x[:half], late_line], axis=0)
    blocks = [with_swap(early_line, from_x, from_y)]
    next_x, next_y = along_x(to_x), along_y(to_y)
    first, norms = weigh_blocks(blocks[0], bank)
    first, next_x, next_y = lax.optimization_barrier((first, next_x, next_y))
    last_x, last_y = along_x(next_y[half + half :]), along_y(next_x[half : half + half])
    blocks.append(with_swap(late_line, next_x, next_y))
    second = weigh_blocks(blocks[1], bank, norms)
    second, last_x, last_y = lax.optimization_barrier((second, last_x, last_y))
    last = with_swap(last_x, last_y)
    out, sums = sum_blocks([first, second], sum(blocks, []), last, norms, bank)
    return jnp.transpose(out, (1, 0, 2)), jnp.transpose(sums, (1, 0))


CLASSES = 5


def bank_index():
    return lax.axis_index("bank").astype(jnp.int32)[None]


def weigh_blocks(blocks, bank, norms=None):
    classes, orients, width = bank.shape
    boxes = sum(block.shape[0] for block in blocks)
    tail = blocks[0].shape[1] - F
    known = norms is not None
    norm_spec = pl.BlockSpec((CLASSES, orients, 128), lambda i: (i, 0, 0))
    out_spec = pl.BlockSpec((CLASSES, orients, boxes), lambda i: (i, 0, 0))
    out_shape = jax.ShapeDtypeStruct((classes, orients, boxes), jnp.bfloat16)
    norm_shape = jax.ShapeDtypeStruct((classes, orients, 128), jnp.float32)
    return pl.pallas_call(
        functools.partial(weigh_kernel, blocks=len(blocks), known=known),
        grid=(classes // CLASSES,),
        in_specs=[pl.BlockSpec(memory_space=pltpu.SMEM)]
        + [pl.BlockSpec(memory_space=pl.ANY)] * len(blocks)
        + [pl.BlockSpec((CLASSES, orients, width), lambda i: (i, 0, 0))]
        + ([norm_spec] if known else []),
        out_specs=out_spec if known else [out_spec, norm_spec],
        out_shape=out_shape if known else [out_shape, norm_shape],
        scratch_shapes=[
            pltpu.VMEM((boxes, F), jnp.bfloat16),
            pltpu.VMEM((boxes, tail), jnp.bfloat16),
            pltpu.VMEM((tail, boxes), jnp.float32),
            pltpu.VMEM((orients, boxes), jnp.float32),
            pltpu.SemaphoreType.DMA((2 * len(blocks),)),
        ],
        compiler_params=pltpu.CompilerParams(vmem_limit_bytes=18 * MIB),
        cost_estimate=pl.CostEstimate(
            flops=2 * boxes * classes * orients * width,
            bytes_accessed=2 * classes * orients * width,
            transcendentals=0,
        ),
        name="weigh",
    )(bank_index(), *blocks, bank, *([norms] if known else []))


def sum_blocks(parts, blocks, late, norms, bank):
    classes, orients, width = bank.shape
    blocks = blocks + late
    boxes = sum(block.shape[0] for block in blocks)
    last = sum(block.shape[0] for block in late)
    tail = blocks[0].shape[1] - F
    vmem = pl.BlockSpec(memory_space=pltpu.VMEM)
    return pl.pallas_call(
        functools.partial(
            sum_kernel, early=len(parts), blocks=len(blocks), late=len(late), group=CLASSES
        ),
        grid=(classes // CLASSES,),
        in_specs=[pl.BlockSpec(memory_space=pltpu.SMEM)]
        + [pl.BlockSpec((CLASSES, orients, part.shape[2]), lambda i: (i, 0, 0)) for part in parts]
        + [pl.BlockSpec(memory_space=pl.ANY)] * len(blocks)
        + [vmem, vmem],
        out_specs=[
            pl.BlockSpec((CLASSES, orients, width), lambda i: (i, 0, 0)),
            pl.BlockSpec((classes, orients), lambda i: (0, 0)),
        ],
        out_shape=[
            jax.ShapeDtypeStruct((classes, orients, width), jnp.float32),
            jax.ShapeDtypeStruct((classes, orients), jnp.float32),
        ],
        scratch_shapes=[
            pltpu.VMEM((boxes, F), jnp.bfloat16),
            pltpu.VMEM((last, F), jnp.bfloat16),
            pltpu.VMEM((last, tail), jnp.bfloat16),
            pltpu.VMEM((tail, last), jnp.float32),
            pltpu.VMEM((orients, last), jnp.float32),
            pltpu.VMEM((classes, orients, last), jnp.bfloat16),
            pltpu.SemaphoreType.DMA((2 * len(blocks),)),
            pltpu.SemaphoreType.DMA((2 * len(late),)),
        ],
        compiler_params=pltpu.CompilerParams(vmem_limit_bytes=34 * MIB),
        cost_estimate=pl.CostEstimate(
            flops=2 * boxes * classes * orients * width,
            bytes_accessed=4 * classes * orients * width,
            transcendentals=0,
        ),
        name="class_sums",
    )(bank_index(), *parts, *blocks, norms, bank)


def body(volume, pick_list, box_counts, orientations, orient_weight, reference_bank):
    wide, high, depth = volume.shape
    slots = pick_list.shape[3]
    tile, bank = lax.axis_index("tile"), lax.axis_index("bank")
    side = lax.rem(tile, 2).astype(jnp.int32)
    rest = wide - HALF
    to_first = lax.dynamic_slice_in_dim(volume, jnp.where(side == 0, rest, 0), HALF, 0)
    to_second = lax.dynamic_slice_in_dim(volume, jnp.where(side == 0, 0, rest), HALF, 0)
    first_halo = exchange(to_first, "tile", True)
    second_halo = exchange(to_second, "tile", False)
    picks, first_halo = lax.optimization_barrier((pick_list, first_halo))
    first_picks, second_picks = exchange(picks, "bank", True), exchange(picks, "bank", False)
    origin = jnp.stack([tile * wide + HALF, bank * high + HALF]).astype(jnp.int32)

    first, second = depth_tables(depth)
    plane = jnp.asarray(plane_table(HALF, high), jnp.bfloat16)
    modes, lanes = plane.shape[0], 3 * slots * L
    unit = 32

    params = pltpu.CompilerParams(vmem_limit_bytes=32 * MIB)
    vmem = pl.BlockSpec(memory_space=pltpu.VMEM)
    smem = pl.BlockSpec(memory_space=pltpu.SMEM)
    near, *tables = pl.pallas_call(
        near_kernel,
        in_specs=[smem] + [vmem] * 7,
        out_specs=[vmem] * 4,
        out_shape=[
            jax.ShapeDtypeStruct((modes, lanes), jnp.float32),
            jax.ShapeDtypeStruct((depth, lanes), jnp.bfloat16),
            jax.ShapeDtypeStruct((high, lanes), jnp.float32),
            jax.ShapeDtypeStruct((8, lanes), jnp.float32),
        ],
        scratch_shapes=[pltpu.VMEM((unit * high, lanes), jnp.bfloat16)],
        compiler_params=params,
        cost_estimate=pl.CostEstimate(
            flops=2 * wide * high * lanes * (depth + modes), bytes_accessed=8000000, transcendentals=0
        ),
        name="near_rows",
    )(origin, first_picks, picks, second_picks, first, second, volume, plane)
    for_first, mid, for_second = pl.pallas_call(
        functools.partial(far_kernel, wide=wide),
        in_specs=[smem] + [vmem] * 7,
        out_specs=[vmem] * 3,
        out_shape=[
            jax.ShapeDtypeStruct((L * L, slots * L), jnp.bfloat16),
            jax.ShapeDtypeStruct((L * L, slots * L), jnp.float32),
            jax.ShapeDtypeStruct((L * L, slots * L), jnp.bfloat16),
        ],
        scratch_shapes=[
            pltpu.VMEM((HALF * high, lanes), jnp.bfloat16),
            pltpu.VMEM((modes, lanes), jnp.float32),
        ],
        compiler_params=params,
        name="far_rows",
    )(side[None], *tables, first_halo, second_halo, plane, near)
    from_first, from_second = exchange(for_first, "bank", True), exchange(for_second, "bank", False)

    live_slots = jnp.arange(slots) < box_counts[0, 0]
    matches = orientations[0, 0][:, :, None] == jnp.arange(R)[None, None, :]
    multiplicity = jnp.sum(
        jnp.where(matches, orient_weight[0, 0][:, :, None].astype(jnp.float32), 0.0), axis=1
    )
    multiplicity = jnp.where(live_slots[:, None], multiplicity, 0.0).astype(jnp.bfloat16)
    parts = 2
    mine = pl.pallas_call(
        join_kernel,
        out_shape=[jax.ShapeDtypeStruct((slots // parts, F + R + 128), jnp.bfloat16)] * parts,
        scratch_shapes=[pltpu.VMEM((slots, F), jnp.float32)],
        compiler_params=params,
        name="join",
    )(mid, from_first, from_second, multiplicity)
    return gather_score(mine, reference_bank)


def solution(mesh):
    in_specs = (
        P("tile", "bank", None),
        P(None, "tile", "bank", None),
        P("tile", "bank"),
        P("tile", "bank", None, None),
        P("tile", "bank", None, None),
        P("bank", None, None),
    )
    out_specs = (P("bank", None, None), P("bank", None))
    return jax.shard_map(body, mesh=mesh, in_specs=in_specs, out_specs=out_specs, check_vma=False)
```

```python
import functools

import jax
import jax.numpy as jnp
import numpy as np
from jax import lax
from jax.experimental import pallas as pl
from jax.experimental.pallas import tpu as pltpu
from jax.sharding import PartitionSpec as P

B = 96
L = 16
R = 256
F = L * L * L
HALF = B // 2
TERMS = L // 2
EPSILON = 1e-06
MIB = 1024 * 1024


def waves(count):
    steps = 2.0 * np.pi * np.outer(np.arange(TERMS + 1), np.arange(count)) / B
    return np.cos(steps) / np.sqrt(B), np.sin(steps) / np.sqrt(B)


def depth_tables(depth):
    cos, sin = waves(depth)
    first = np.concatenate([cos, sin[1:TERMS]], axis=0)
    second = np.concatenate([sin, -cos[1:TERMS]], axis=0)
    repeat = 128 // L
    return (
        np.tile(first.T, (1, repeat)).astype(np.float32),
        np.tile(second.T, (1, repeat)).astype(np.float32),
    )


def plane_table(wide, high):
    cos_x, sin_x = waves(wide)
    cos_y, sin_y = waves(high)
    along_x = np.concatenate([cos_x, sin_x[1:]], axis=0)
    along_y = np.concatenate([cos_y[1:], sin_y[1:]], axis=0)
    main = np.einsum("ax,by->abxy", along_x, along_y).reshape(-1, wide * high)
    order = np.concatenate([along_x[1:], along_x[:1]], axis=0)
    flat = np.einsum("ax,y->axy", order, cos_y[0]).reshape(-1, wide * high)
    rows = np.concatenate([main, flat], axis=0)
    pad = -rows.shape[0] % 16
    return np.concatenate([rows, np.zeros((pad, rows.shape[1]))], axis=0).astype(np.float32)


def spread(origin_ref, corner_refs, lanes):
    slots = corner_refs[0].shape[3]
    box = lax.broadcasted_iota(jnp.int32, (slots, lanes), 0)
    lane = lax.broadcasted_iota(jnp.int32, (slots, lanes), 1)
    row = lax.broadcasted_iota(jnp.int32, (8, slots), 0)
    origin = jnp.where(row == 0, origin_ref[0], jnp.where(row == 1, origin_ref[1], 0))
    total = jnp.zeros((8, lanes), jnp.float32)
    for k, corner_ref in enumerate(corner_refs):
        corners = jnp.zeros((8, slots), jnp.int32)
        for axis in range(3):
            corners = jnp.where(row == axis, corner_ref[axis, 0], corners)
        corners = (corners - origin).astype(jnp.float32).astype(jnp.bfloat16)
        pick = jnp.where(lane // L == box + k * slots, 1.0, 0.0).astype(jnp.bfloat16)
        total += jnp.dot(corners, pick, preferred_element_type=jnp.float32)
    return total


def turns(terms, shift):
    turn = (terms * shift).astype(jnp.int32)
    turn = lax.rem(turn, B)
    angle = turn.astype(jnp.float32) * (2.0 * np.pi / B)
    return jnp.cos(angle), jnp.sin(angle)


def prepare(origin_ref, corner_refs, first_ref, second_ref, depth_ref, high_ref, where_ref):
    depth, lanes = depth_ref.shape
    where = spread(origin_ref, corner_refs, lanes)
    where_ref[...] = where
    start_y, start_z = where[1:2], where[2:3]
    lane = lax.rem(lax.broadcasted_iota(jnp.int32, (1, lanes), 1), L)
    term = jnp.where(lane <= TERMS, lane, lane - TERMS).astype(jnp.float32)
    cos, sin = turns(term, start_z)
    copies = lanes // first_ref.shape[1]
    first = jnp.concatenate([first_ref[...]] * copies, axis=1)
    second = jnp.concatenate([second_ref[...]] * copies, axis=1)
    z = lax.broadcasted_iota(jnp.int32, (depth, lanes), 0).astype(jnp.float32) - start_z
    table = jnp.where((z >= 0) & (z < B), first * cos + second * sin, 0.0)
    depth_ref[...] = table.astype(jnp.bfloat16)
    y = lax.broadcasted_iota(jnp.int32, high_ref.shape, 0).astype(jnp.float32) - start_y
    high_ref[...] = jnp.where((y >= 0) & (y < B), 1.0, 0.0)


def block_modes(voxels, at_x, turn, start_x, depth_ref, high_ref, part_ref, plane_ref):
    count, high, depth = voxels.shape
    offset = at_x - start_x
    rows = voxels.reshape(count * high, depth)
    first = jnp.dot(rows, depth_ref[...], preferred_element_type=jnp.float32)
    for x in range(count):
        at = offset + float(x)
        live = high_ref[...] * jnp.where((at >= 0) & (at < B), 1.0, 0.0)
        kept = first[x * high : (x + 1) * high] * live
        part_ref[pl.ds(x * high, high), :] = kept.astype(jnp.bfloat16)
    length = count * high
    total = jnp.dot(
        plane_ref[:, :length], part_ref[:length], preferred_element_type=jnp.float32
    )
    return total if turn is None else moved(total, turn)


def turn_of(at_x):
    angles = 2.0 * np.pi * np.arange(1, TERMS + 1) * at_x / B
    return [float(c) for c in np.cos(angles)], [float(s) for s in np.sin(angles)]


def either(flag, one, other):
    return tuple([jnp.where(flag, a, b) for a, b in zip(u, v)] for u, v in zip(one, other))


def moved(total, turn):
    group, blocks = 2 * TERMS, 2 * TERMS + 1
    rows = [total[a * group : (a + 1) * group] for a in range(blocks)]
    main = blocks * group
    flat_cos, flat_sin = total[main : main + TERMS], total[main + TERMS : main + group]
    out = list(rows)
    term = lax.broadcasted_iota(jnp.int32, flat_cos.shape, 0)
    flat_c, flat_s = jnp.zeros_like(flat_cos), jnp.zeros_like(flat_cos)
    for j, (c, s) in enumerate(zip(*turn)):
        out[1 + j] = rows[1 + j] * c - rows[1 + TERMS + j] * s
        out[1 + TERMS + j] = rows[1 + j] * s + rows[1 + TERMS + j] * c
        flat_c = jnp.where(term == j, c, flat_c)
        flat_s = jnp.where(term == j, s, flat_s)
    out += [
        flat_cos * flat_c - flat_sin * flat_s,
        flat_cos * flat_s + flat_sin * flat_c,
        total[main + group :],
    ]
    return jnp.concatenate(out, axis=0)


def near_kernel(
    origin_ref, first_pick_ref, pick_ref, second_pick_ref, first_ref, second_ref, volume_ref, plane_ref,
    total_ref, depth_ref, high_ref, where_ref, part_ref,
):
    corner_refs = (first_pick_ref, pick_ref, second_pick_ref)
    prepare(origin_ref, corner_refs, first_ref, second_ref, depth_ref, high_ref, where_ref)
    start_x = where_ref[0:1]
    unit = part_ref.shape[0] // volume_ref.shape[1]
    for x in range(0, volume_ref.shape[0], unit):
        added = block_modes(
            volume_ref[x : x + unit], float(x), turn_of(x) if x else None, start_x,
            depth_ref, high_ref, part_ref, plane_ref,
        )
        total_ref[...] = added if x == 0 else total_ref[...] + added


def rotate(total, start_x, start_y):
    lanes = total.shape[1]
    term = (lax.broadcasted_iota(jnp.int32, (TERMS, lanes), 0) + 1).astype(jnp.float32)
    cos_x, sin_x = turns(term, start_x)
    cos_y, sin_y = turns(term, start_y)
    blocks = 2 * TERMS + 1
    main = blocks * 2 * TERMS
    flat_cos = total[main : main + TERMS]
    flat_sin = total[main + TERMS : main + 2 * TERMS]
    flat_zero = total[main + 2 * TERMS : main + 2 * TERMS + 1]
    flats = (
        [flat_zero]
        + [flat_cos[j : j + 1] for j in range(TERMS)]
        + [flat_sin[j : j + 1] for j in range(TERMS)]
    )
    last = lax.broadcasted_iota(jnp.int32, (TERMS, lanes), 0) == TERMS - 1
    turned = []
    for a in range(blocks):
        cos = total[a * 2 * TERMS : a * 2 * TERMS + TERMS]
        sin = total[a * 2 * TERMS + TERMS : (a + 1) * 2 * TERMS]
        low = cos * cos_y + sin * sin_y
        high = sin * cos_y - cos * sin_y
        turned.append((low, jnp.where(last, flats[a], high)))
    rows = [None] * (2 * TERMS)
    rows[0] = turned[0]
    for j in range(1, TERMS + 1):
        c, s = cos_x[j - 1 : j], sin_x[j - 1 : j]
        cos, sin = turned[j], turned[TERMS + j]
        rows[j] = tuple(u * c + v * s for u, v in zip(cos, sin))
        if j < TERMS:
            rows[TERMS + j] = tuple(v * c - u * s for u, v in zip(cos, sin))
    return jnp.concatenate([half for pair in rows for half in pair], axis=0)


def far_kernel(
    side_ref, depth_ref, high_ref, where_ref, first_halo_ref, second_halo_ref, plane_ref, near_ref,
    first_out_ref, own_ref, second_out_ref, part_ref, total_ref, *, wide,
):
    start_x = where_ref[0:1]
    total_ref[...] = near_ref[...]
    even = side_ref[0] == 0
    below, above = turn_of(-HALF), turn_of(wide)
    sides = (
        (first_halo_ref, jnp.where(even, wide, -HALF), either(even, above, below)),
        (second_halo_ref, jnp.where(even, -HALF, wide), either(even, below, above)),
    )
    for voxels_ref, at_x, turn in sides:
        total_ref[...] += block_modes(
            voxels_ref[...], at_x.astype(jnp.float32), turn, start_x,
            depth_ref, high_ref, part_ref, plane_ref,
        )
    rows = rotate(total_ref[...], start_x, where_ref[1:2])
    width = own_ref.shape[1]
    first_out_ref[...] = rows[:, :width].astype(jnp.bfloat16)
    own_ref[...] = rows[:, width : 2 * width]
    second_out_ref[...] = rows[:, 2 * width :].astype(jnp.bfloat16)


def join_kernel(own_ref, left_ref, right_ref, multiplicity_ref, *refs):
    outs, wide_ref = refs[:-1], refs[-1]
    total = own_ref[...] + left_ref[...].astype(jnp.float32) + right_ref[...].astype(jnp.float32)
    total = total.astype(jnp.bfloat16)
    rows, lanes = total.shape
    slots, group = lanes // L, rows // L

    def grid_of(shape, axis):
        return lax.broadcasted_iota(jnp.int32, shape, axis)

    def ones_where(flag):
        return jnp.where(flag, 1.0, 0.0).astype(jnp.bfloat16)

    square = (slots * group, lanes)
    mine = ones_where(grid_of(square, 0) // group == grid_of(square, 1) // L)
    square = (lanes, L * L)
    tiled = ones_where(lax.rem(grid_of(square, 0), L) == lax.rem(grid_of(square, 1), L))
    square = (slots * group, L * L)
    place = lax.rem(grid_of(square, 0), group) + 1
    place = jnp.where(place == group, 0, place)
    keep = ones_where(place == grid_of(square, 1) // L)
    square = (slots, slots * group)
    sums = ones_where(grid_of(square, 1) // group == grid_of(square, 0))
    copies = jnp.concatenate(
        [
            jnp.concatenate([total[a * group : (a + 1) * group]] * slots, axis=0) * mine
            for a in range(L)
        ],
        axis=0,
    )
    placed = jnp.dot(copies, tiled, preferred_element_type=jnp.float32).astype(jnp.bfloat16)
    flat = jnp.concatenate(
        [placed[a * rows : (a + 1) * rows] * keep for a in range(L)], axis=1
    )
    wide_ref[...] = jnp.dot(sums, flat, preferred_element_type=jnp.float32)
    wide = wide_ref[...]
    norm = jnp.sqrt(jnp.mean(wide * wide, axis=1, keepdims=True) + EPSILON)
    high = norm.astype(jnp.bfloat16).astype(jnp.float32)
    tail = lax.broadcasted_iota(jnp.int32, (slots, 128), 1)
    tail = jnp.where(tail == 0, high, jnp.where(tail == 1, norm - high, 0.0))
    row = jnp.concatenate(
        [wide.astype(jnp.bfloat16), multiplicity_ref[...], tail.astype(jnp.bfloat16)], axis=1
    )
    for k, out_ref in enumerate(outs):
        count = out_ref.shape[0]
        out_ref[...] = row[k * count : (k + 1) * count]


def block_copies(blocks, rows_ref, tail_ref, sems):
    copies, at = [], 0
    for k, block in enumerate(blocks):
        count = block.shape[0]
        place = pl.ds(at, count)
        copies.append(
            pltpu.make_async_copy(block.at[:, pl.ds(0, F)], rows_ref.at[place], sems.at[2 * k])
        )
        if tail_ref is not None:
            copies.append(
                pltpu.make_async_copy(
                    block.at[:, pl.ds(F, block.shape[1] - F)], tail_ref.at[place], sems.at[2 * k + 1]
                )
            )
        at += count
    return copies


def read_tail(bank_ref, tail, tail_ref, multiplicity_ref, orients):
    tail_ref[...] = tail.astype(jnp.float32).T
    start = pl.multiple_of(bank_ref[0] * orients, orients)
    norm = tail_ref[R : R + 1, :] + tail_ref[R + 1 : R + 2, :]
    multiplicity_ref[...] = tail_ref[pl.ds(start, orients), :] / (F * norm)


def inverse_norms(bank_rows):
    wide = bank_rows.astype(jnp.float32)
    return 1.0 / jnp.sqrt(jnp.mean(wide * wide, axis=1, keepdims=True) + EPSILON)


def weigh(bank_rows, inverse, rows, multiplicity, count):
    scores = lax.dot_general(
        bank_rows, rows, (((1,), (1,)), ((), ())), preferred_element_type=jnp.float32
    )
    multiplicity = jnp.concatenate([multiplicity] * count, axis=0)
    return (multiplicity * jnp.maximum(scores * inverse, 0.0)).astype(jnp.bfloat16)


def weigh_kernel(index_ref, *refs, blocks, known):
    sources, bank_ref = refs[:blocks], refs[blocks]
    if known:
        norms_ref, out_ref = refs[blocks + 1 : blocks + 3]
    else:
        out_ref, norms_ref = refs[blocks + 1 : blocks + 3]
    rows_ref, tail_ref, turned_ref, multiplicity_ref, sems = refs[blocks + 3 :]
    count, orients, width = bank_ref.shape

    @pl.when(pl.program_id(0) == 0)
    def _():
        copies = block_copies(sources, rows_ref, tail_ref, sems)
        for copy in copies:
            copy.start()
        for copy in copies:
            copy.wait()
        read_tail(index_ref, tail_ref[...], turned_ref, multiplicity_ref, orients)

    bank = bank_ref[...].reshape(count * orients, width)
    if known:
        inverse = norms_ref[...].reshape(count * orients, norms_ref.shape[2])[:, :1]
    else:
        inverse = inverse_norms(bank)
        norms_ref[...] = jnp.broadcast_to(inverse, (count * orients, norms_ref.shape[2])).reshape(
            norms_ref.shape
        )
    weights = weigh(bank, inverse, rows_ref[...], multiplicity_ref[...], count)
    out_ref[...] = weights.reshape(out_ref.shape)


def sum_kernel(index_ref, *refs, early, blocks, late, group):
    parts, sources = refs[:early], refs[early : early + blocks]
    norms_ref, bank_ref, out_ref, sums_ref = refs[early + blocks : early + blocks + 4]
    rows_ref, last_ref, tail_ref, turned_ref, multiplicity_ref, weights_ref, sems, last_sems = refs[
        early + blocks + 4 :
    ]
    count, orients, width = out_ref.shape
    boxes, last = rows_ref.shape[0], last_ref.shape[0]
    step = pl.program_id(0)

    @pl.when(step == 0)
    def _():
        copies = block_copies(sources, rows_ref, None, sems)
        urgent = block_copies(sources[blocks - late :], last_ref, tail_ref, last_sems)
        for copy in urgent + copies:
            copy.start()
        for copy in urgent:
            copy.wait()
        read_tail(index_ref, tail_ref[...], turned_ref, multiplicity_ref, orients)
        for c in range(0, bank_ref.shape[0], group):
            bank = bank_ref[c : c + group].reshape(group * orients, width)
            inverse = norms_ref[c : c + group].reshape(group * orients, norms_ref.shape[2])[:, :1]
            weights = weigh(bank, inverse, last_ref[...], multiplicity_ref[...], group)
            weights_ref[c : c + group] = weights.reshape(group, orients, last)
        for copy in copies:
            copy.wait()

    known = [part[...].reshape(count * orients, part.shape[2]) for part in parts]
    at = pl.multiple_of(step * count, count)
    known.append(weights_ref[pl.ds(at, count)].reshape(count * orients, last))
    weights = jnp.concatenate(known, axis=1)
    total = jnp.dot(weights, rows_ref[...], preferred_element_type=jnp.float32)
    out_ref[...] = total.reshape(out_ref.shape)
    ones = jnp.ones((8, boxes), jnp.bfloat16)
    sums = lax.dot_general(
        ones, weights, (((1,), (1,)), ((), ())), preferred_element_type=jnp.float32
    )
    for c in range(count):
        sums_ref[pl.ds(step * count + c, 1), :] = sums[:1, c * orients : (c + 1) * orients]


def score_plain(rows, bank):
    local_rows = bank.shape[0]
    start = F + lax.axis_index("bank") * local_rows
    multiplicity = lax.dynamic_slice_in_dim(rows, start, local_rows, 1).astype(jnp.float32)
    norm = rows[:, F + R].astype(jnp.float32) + rows[:, F + R + 1].astype(jnp.float32)
    features = rows[:, :F]
    scores = jnp.einsum("if,rcf->irc", features, bank, preferred_element_type=jnp.float32)
    wide = bank.astype(jnp.float32)
    bank_norm = jnp.sqrt(jnp.mean(wide * wide, axis=2) + EPSILON)
    correl = scores / (F * norm[:, None, None] * bank_norm[None])
    weights = (multiplicity[:, :, None] * jnp.maximum(correl, 0.0)).astype(jnp.bfloat16)
    class_sums = jnp.einsum("irc,if->rcf", weights, features, preferred_element_type=jnp.float32)
    return class_sums, jnp.sum(weights.astype(jnp.float32), axis=0)


def exchange(value, axis, first):
    count = lax.axis_size(axis)
    pairs = []
    for i in range(0 if first else 1, count - 1, 2):
        pairs += [(i, i + 1), (i + 1, i)]
    return lax.ppermute(value, axis, pairs)


def gather_score(mine, reference_bank):
    tiles, banks = lax.axis_size("tile"), lax.axis_size("bank")
    local_rows, classes, width = reference_bank.shape
    boxes = tiles * banks * sum(part.shape[0] for part in mine)
    if banks != 4 or tiles & (tiles - 1) or tiles < 4 or boxes > 1024 or classes % 5:
        rows = jnp.concatenate(mine, axis=0)
        for axis in ("bank", "tile"):
            rows = lax.all_gather(rows, axis, axis=0, tiled=True)
        return score_plain(rows, reference_bank)
    bank = jnp.transpose(reference_bank, (1, 0, 2))
    early, late = mine

    def along_x(value):
        return lax.ppermute(value, "bank", [(0, 1), (1, 0), (2, 3), (3, 2)])

    def along_y(value):
        return lax.ppermute(value, "bank", [(0, 2), (2, 0), (1, 3), (3, 1)])

    def swap(*values):
        return [lax.ppermute(value, "tile", [(i, i ^ 1) for i in range(tiles)]) for value in values]

    def line_of(part):
        others = [
            lax.ppermute(part, "tile", [(i, i ^ by) for i in range(tiles)])
            for by in range(2, tiles, 2)
        ]
        return jnp.concatenate([part] + others, axis=0)

    def with_swap(*values):
        joined = jnp.concatenate(values, axis=0) if len(values) > 1 else values[0]
        return [*values, *swap(joined)]

    early_line = line_of(early)
    late, early_line = lax.optimization_barrier((late, early_line))
    from_x, from_y = along_x(early_line), along_y(early_line)
    late_line = line_of(late)
    half = early_line.shape[0] // 2
    to_x = jnp.concatenate([from_y[half:], late_line], axis=0)
    to_y = jnp.concatenate([from_x[:half], late_line], axis=0)
    known = with_swap(early_line, from_x, from_y)
    to_x, to_y = lax.optimization_barrier((to_x, to_y))
    next_x, next_y = along_x(to_x), along_y(to_y)
    known += with_swap(to_x[half:])
    first, norms = weigh_blocks(known, bank)
    first, next_x, next_y = lax.optimization_barrier((first, next_x, next_y))
    last_x, last_y = along_x(next_y[half + half :]), along_y(next_x[half : half + half])
    late = with_swap(next_x, next_y) + with_swap(last_x, last_y)
    out, sums = sum_blocks([first], known, late, norms, bank)
    return jnp.transpose(out, (1, 0, 2)), jnp.transpose(sums, (1, 0))


CLASSES = 5


def bank_index():
    return lax.axis_index("bank").astype(jnp.int32)[None]


def weigh_blocks(blocks, bank, norms=None):
    classes, orients, width = bank.shape
    boxes = sum(block.shape[0] for block in blocks)
    tail = blocks[0].shape[1] - F
    known = norms is not None
    norm_spec = pl.BlockSpec((CLASSES, orients, 128), lambda i: (i, 0, 0))
    out_spec = pl.BlockSpec((CLASSES, orients, boxes), lambda i: (i, 0, 0))
    out_shape = jax.ShapeDtypeStruct((classes, orients, boxes), jnp.bfloat16)
    norm_shape = jax.ShapeDtypeStruct((classes, orients, 128), jnp.float32)
    return pl.pallas_call(
        functools.partial(weigh_kernel, blocks=len(blocks), known=known),
        grid=(classes // CLASSES,),
        in_specs=[pl.BlockSpec(memory_space=pltpu.SMEM)]
        + [pl.BlockSpec(memory_space=pl.ANY)] * len(blocks)
        + [pl.BlockSpec((CLASSES, orients, width), lambda i: (i, 0, 0))]
        + ([norm_spec] if known else []),
        out_specs=out_spec if known else [out_spec, norm_spec],
        out_shape=out_shape if known else [out_shape, norm_shape],
        scratch_shapes=[
            pltpu.VMEM((boxes, F), jnp.bfloat16),
            pltpu.VMEM((boxes, tail), jnp.bfloat16),
            pltpu.VMEM((tail, boxes), jnp.float32),
            pltpu.VMEM((orients, boxes), jnp.float32),
            pltpu.SemaphoreType.DMA((2 * len(blocks),)),
        ],
        compiler_params=pltpu.CompilerParams(vmem_limit_bytes=18 * MIB),
        cost_estimate=pl.CostEstimate(
            flops=boxes * classes * orients * width // 8,
            bytes_accessed=classes * orients * width // 8,
            transcendentals=0,
        ),
        name="weigh",
    )(bank_index(), *blocks, bank, *([norms] if known else []))


def sum_blocks(parts, blocks, late, norms, bank):
    classes, orients, width = bank.shape
    blocks = blocks + late
    boxes = sum(block.shape[0] for block in blocks)
    last = sum(block.shape[0] for block in late)
    tail = blocks[0].shape[1] - F
    vmem = pl.BlockSpec(memory_space=pltpu.VMEM)
    return pl.pallas_call(
        functools.partial(
            sum_kernel, early=len(parts), blocks=len(blocks), late=len(late), group=CLASSES
        ),
        grid=(classes // CLASSES,),
        in_specs=[pl.BlockSpec(memory_space=pltpu.SMEM)]
        + [pl.BlockSpec((CLASSES, orients, part.shape[2]), lambda i: (i, 0, 0)) for part in parts]
        + [pl.BlockSpec(memory_space=pl.ANY)] * len(blocks)
        + [vmem, vmem],
        out_specs=[
            pl.BlockSpec((CLASSES, orients, width), lambda i: (i, 0, 0)),
            pl.BlockSpec((classes, orients), lambda i: (0, 0)),
        ],
        out_shape=[
            jax.ShapeDtypeStruct((classes, orients, width), jnp.float32),
            jax.ShapeDtypeStruct((classes, orients), jnp.float32),
        ],
        scratch_shapes=[
            pltpu.VMEM((boxes, F), jnp.bfloat16),
            pltpu.VMEM((last, F), jnp.bfloat16),
            pltpu.VMEM((last, tail), jnp.bfloat16),
            pltpu.VMEM((tail, last), jnp.float32),
            pltpu.VMEM((orients, last), jnp.float32),
            pltpu.VMEM((classes, orients, last), jnp.bfloat16),
            pltpu.SemaphoreType.DMA((2 * len(blocks),)),
            pltpu.SemaphoreType.DMA((2 * len(late),)),
        ],
        compiler_params=pltpu.CompilerParams(vmem_limit_bytes=34 * MIB),
        cost_estimate=pl.CostEstimate(
            flops=2 * boxes * classes * orients * width,
            bytes_accessed=4 * classes * orients * width,
            transcendentals=0,
        ),
        name="class_sums",
    )(bank_index(), *parts, *blocks, norms, bank)


def body(volume, pick_list, box_counts, orientations, orient_weight, reference_bank):
    wide, high, depth = volume.shape
    slots = pick_list.shape[3]
    tile, bank = lax.axis_index("tile"), lax.axis_index("bank")
    side = lax.rem(tile, 2).astype(jnp.int32)
    rest = wide - HALF
    to_first = lax.dynamic_slice_in_dim(volume, jnp.where(side == 0, rest, 0), HALF, 0)
    to_second = lax.dynamic_slice_in_dim(volume, jnp.where(side == 0, 0, rest), HALF, 0)
    first_halo = exchange(to_first, "tile", True)
    second_halo = exchange(to_second, "tile", False)
    picks, first_halo = lax.optimization_barrier((pick_list, first_halo))
    first_picks, second_picks = exchange(picks, "bank", True), exchange(picks, "bank", False)
    origin = jnp.stack([tile * wide + HALF, bank * high + HALF]).astype(jnp.int32)

    first, second = depth_tables(depth)
    plane = jnp.asarray(plane_table(HALF, high), jnp.bfloat16)
    modes, lanes = plane.shape[0], 3 * slots * L
    unit = 32

    params = pltpu.CompilerParams(vmem_limit_bytes=32 * MIB)
    vmem = pl.BlockSpec(memory_space=pltpu.VMEM)
    smem = pl.BlockSpec(memory_space=pltpu.SMEM)
    near, *tables = pl.pallas_call(
        near_kernel,
        in_specs=[smem] + [vmem] * 7,
        out_specs=[vmem] * 4,
        out_shape=[
            jax.ShapeDtypeStruct((modes, lanes), jnp.float32),
            jax.ShapeDtypeStruct((depth, lanes), jnp.bfloat16),
            jax.ShapeDtypeStruct((high, lanes), jnp.float32),
            jax.ShapeDtypeStruct((8, lanes), jnp.float32),
        ],
        scratch_shapes=[pltpu.VMEM((unit * high, lanes), jnp.bfloat16)],
        compiler_params=params,
        cost_estimate=pl.CostEstimate(
            flops=2 * wide * high * lanes * (depth + modes), bytes_accessed=8000000, transcendentals=0
        ),
        name="near_rows",
    )(origin, first_picks, picks, second_picks, first, second, volume, plane)
    for_first, mid, for_second = pl.pallas_call(
        functools.partial(far_kernel, wide=wide),
        in_specs=[smem] + [vmem] * 7,
        out_specs=[vmem] * 3,
        out_shape=[
            jax.ShapeDtypeStruct((L * L, slots * L), jnp.bfloat16),
            jax.ShapeDtypeStruct((L * L, slots * L), jnp.float32),
            jax.ShapeDtypeStruct((L * L, slots * L), jnp.bfloat16),
        ],
        scratch_shapes=[
            pltpu.VMEM((HALF * high, lanes), jnp.bfloat16),
            pltpu.VMEM((modes, lanes), jnp.float32),
        ],
        compiler_params=params,
        name="far_rows",
    )(side[None], *tables, first_halo, second_halo, plane, near)
    from_first, from_second = exchange(for_first, "bank", True), exchange(for_second, "bank", False)

    live_slots = jnp.arange(slots) < box_counts[0, 0]
    matches = orientations[0, 0][:, :, None] == jnp.arange(R)[None, None, :]
    multiplicity = jnp.sum(
        jnp.where(matches, orient_weight[0, 0][:, :, None].astype(jnp.float32), 0.0), axis=1
    )
    multiplicity = jnp.where(live_slots[:, None], multiplicity, 0.0).astype(jnp.bfloat16)
    parts = 2
    mine = pl.pallas_call(
        join_kernel,
        out_shape=[jax.ShapeDtypeStruct((slots // parts, F + R + 128), jnp.bfloat16)] * parts,
        scratch_shapes=[pltpu.VMEM((slots, F), jnp.float32)],
        compiler_params=params,
        name="join",
    )(mid, from_first, from_second, multiplicity)
    return gather_score(mine, reference_bank)


def solution(mesh):
    in_specs = (
        P("tile", "bank", None),
        P(None, "tile", "bank", None),
        P("tile", "bank"),
        P("tile", "bank", None, None),
        P("tile", "bank", None, None),
        P("bank", None, None),
    )
    out_specs = (P("bank", None, None), P("bank", None))
    return jax.shard_map(body, mesh=mesh, in_specs=in_specs, out_specs=out_specs, check_vma=False)
```

```python
import functools

import jax
import jax.numpy as jnp
import numpy as np
from jax import lax
from jax.experimental import pallas as pl
from jax.experimental.pallas import tpu as pltpu
from jax.sharding import PartitionSpec as P

B = 96
L = 16
R = 256
F = L * L * L
HALF = B // 2
TERMS = L // 2
EPSILON = 1e-06
MIB = 1024 * 1024


def waves(count):
    steps = 2.0 * np.pi * np.outer(np.arange(TERMS + 1), np.arange(count)) / B
    return np.cos(steps) / np.sqrt(B), np.sin(steps) / np.sqrt(B)


def depth_tables(depth):
    cos, sin = waves(depth)
    first = np.concatenate([cos, sin[1:TERMS]], axis=0)
    second = np.concatenate([sin, -cos[1:TERMS]], axis=0)
    repeat = 128 // L
    return (
        np.tile(first.T, (1, repeat)).astype(np.float32),
        np.tile(second.T, (1, repeat)).astype(np.float32),
    )


def plane_table(wide, high):
    cos_x, sin_x = waves(wide)
    cos_y, sin_y = waves(high)
    along_x = np.concatenate([cos_x, sin_x[1:]], axis=0)
    along_y = np.concatenate([cos_y[1:], sin_y[1:]], axis=0)
    main = np.einsum("ax,by->abxy", along_x, along_y).reshape(-1, wide * high)
    order = np.concatenate([along_x[1:], along_x[:1]], axis=0)
    flat = np.einsum("ax,y->axy", order, cos_y[0]).reshape(-1, wide * high)
    rows = np.concatenate([main, flat], axis=0)
    pad = -rows.shape[0] % 16
    return np.concatenate([rows, np.zeros((pad, rows.shape[1]))], axis=0).astype(np.float32)


def spread(origin_ref, corner_refs, lanes):
    slots = corner_refs[0].shape[3]
    box = lax.broadcasted_iota(jnp.int32, (slots, lanes), 0)
    lane = lax.broadcasted_iota(jnp.int32, (slots, lanes), 1)
    row = lax.broadcasted_iota(jnp.int32, (8, slots), 0)
    origin = jnp.where(row == 0, origin_ref[0], jnp.where(row == 1, origin_ref[1], 0))
    total = jnp.zeros((8, lanes), jnp.float32)
    for k, corner_ref in enumerate(corner_refs):
        corners = jnp.zeros((8, slots), jnp.int32)
        for axis in range(3):
            corners = jnp.where(row == axis, corner_ref[axis, 0], corners)
        corners = (corners - origin).astype(jnp.float32).astype(jnp.bfloat16)
        pick = jnp.where(lane // L == box + k * slots, 1.0, 0.0).astype(jnp.bfloat16)
        total += jnp.dot(corners, pick, preferred_element_type=jnp.float32)
    return total


def turns(terms, shift):
    turn = (terms * shift).astype(jnp.int32)
    turn = lax.rem(turn, B)
    angle = turn.astype(jnp.float32) * (2.0 * np.pi / B)
    return jnp.cos(angle), jnp.sin(angle)


def prepare(origin_ref, corner_refs, first_ref, second_ref, depth_ref, high_ref, where_ref):
    depth, lanes = depth_ref.shape
    where = spread(origin_ref, corner_refs, lanes)
    where_ref[...] = where
    start_y, start_z = where[1:2], where[2:3]
    lane = lax.rem(lax.broadcasted_iota(jnp.int32, (1, lanes), 1), L)
    term = jnp.where(lane <= TERMS, lane, lane - TERMS).astype(jnp.float32)
    cos, sin = turns(term, start_z)
    copies = lanes // first_ref.shape[1]
    first = jnp.concatenate([first_ref[...]] * copies, axis=1)
    second = jnp.concatenate([second_ref[...]] * copies, axis=1)
    z = lax.broadcasted_iota(jnp.int32, (depth, lanes), 0).astype(jnp.float32) - start_z
    table = jnp.where((z >= 0) & (z < B), first * cos + second * sin, 0.0)
    depth_ref[...] = table.astype(jnp.bfloat16)
    y = lax.broadcasted_iota(jnp.int32, high_ref.shape, 0).astype(jnp.float32) - start_y
    high_ref[...] = jnp.where((y >= 0) & (y < B), 1.0, 0.0)


def block_modes(voxels, at_x, turn, start_x, depth_ref, high_ref, part_ref, plane_ref):
    count, high, depth = voxels.shape
    offset = at_x - start_x
    rows = voxels.reshape(count * high, depth)
    first = jnp.dot(rows, depth_ref[...], preferred_element_type=jnp.float32)
    for x in range(count):
        at = offset + float(x)
        live = high_ref[...] * jnp.where((at >= 0) & (at < B), 1.0, 0.0)
        kept = first[x * high : (x + 1) * high] * live
        part_ref[pl.ds(x * high, high), :] = kept.astype(jnp.bfloat16)
    length = count * high
    total = jnp.dot(
        plane_ref[:, :length], part_ref[:length], preferred_element_type=jnp.float32
    )
    return total if turn is None else moved(total, turn)


def turn_of(at_x):
    angles = 2.0 * np.pi * np.arange(1, TERMS + 1) * at_x / B
    return [float(c) for c in np.cos(angles)], [float(s) for s in np.sin(angles)]


def either(flag, one, other):
    return tuple([jnp.where(flag, a, b) for a, b in zip(u, v)] for u, v in zip(one, other))


def moved(total, turn):
    group, blocks = 2 * TERMS, 2 * TERMS + 1
    rows = [total[a * group : (a + 1) * group] for a in range(blocks)]
    main = blocks * group
    flat_cos, flat_sin = total[main : main + TERMS], total[main + TERMS : main + group]
    out = list(rows)
    term = lax.broadcasted_iota(jnp.int32, flat_cos.shape, 0)
    flat_c, flat_s = jnp.zeros_like(flat_cos), jnp.zeros_like(flat_cos)
    for j, (c, s) in enumerate(zip(*turn)):
        out[1 + j] = rows[1 + j] * c - rows[1 + TERMS + j] * s
        out[1 + TERMS + j] = rows[1 + j] * s + rows[1 + TERMS + j] * c
        flat_c = jnp.where(term == j, c, flat_c)
        flat_s = jnp.where(term == j, s, flat_s)
    out += [
        flat_cos * flat_c - flat_sin * flat_s,
        flat_cos * flat_s + flat_sin * flat_c,
        total[main + group :],
    ]
    return jnp.concatenate(out, axis=0)


def near_kernel(
    origin_ref, first_pick_ref, pick_ref, second_pick_ref, first_ref, second_ref, volume_ref, plane_ref,
    total_ref, depth_ref, high_ref, where_ref, part_ref,
):
    corner_refs = (first_pick_ref, pick_ref, second_pick_ref)
    prepare(origin_ref, corner_refs, first_ref, second_ref, depth_ref, high_ref, where_ref)
    start_x = where_ref[0:1]
    unit = part_ref.shape[0] // volume_ref.shape[1]
    for x in range(0, volume_ref.shape[0], unit):
        added = block_modes(
            volume_ref[x : x + unit], float(x), turn_of(x) if x else None, start_x,
            depth_ref, high_ref, part_ref, plane_ref,
        )
        total_ref[...] = added if x == 0 else total_ref[...] + added


def rotate(total, start_x, start_y):
    lanes = total.shape[1]
    term = (lax.broadcasted_iota(jnp.int32, (TERMS, lanes), 0) + 1).astype(jnp.float32)
    cos_x, sin_x = turns(term, start_x)
    cos_y, sin_y = turns(term, start_y)
    blocks = 2 * TERMS + 1
    main = blocks * 2 * TERMS
    flat_cos = total[main : main + TERMS]
    flat_sin = total[main + TERMS : main + 2 * TERMS]
    flat_zero = total[main + 2 * TERMS : main + 2 * TERMS + 1]
    flats = (
        [flat_zero]
        + [flat_cos[j : j + 1] for j in range(TERMS)]
        + [flat_sin[j : j + 1] for j in range(TERMS)]
    )
    last = lax.broadcasted_iota(jnp.int32, (TERMS, lanes), 0) == TERMS - 1
    turned = []
    for a in range(blocks):
        cos = total[a * 2 * TERMS : a * 2 * TERMS + TERMS]
        sin = total[a * 2 * TERMS + TERMS : (a + 1) * 2 * TERMS]
        low = cos * cos_y + sin * sin_y
        high = sin * cos_y - cos * sin_y
        turned.append((low, jnp.where(last, flats[a], high)))
    rows = [None] * (2 * TERMS)
    rows[0] = turned[0]
    for j in range(1, TERMS + 1):
        c, s = cos_x[j - 1 : j], sin_x[j - 1 : j]
        cos, sin = turned[j], turned[TERMS + j]
        rows[j] = tuple(u * c + v * s for u, v in zip(cos, sin))
        if j < TERMS:
            rows[TERMS + j] = tuple(v * c - u * s for u, v in zip(cos, sin))
    return jnp.concatenate([half for pair in rows for half in pair], axis=0)


def far_kernel(
    side_ref, depth_ref, high_ref, where_ref, first_halo_ref, second_halo_ref, plane_ref, near_ref,
    first_out_ref, own_ref, second_out_ref, part_ref, total_ref, *, wide,
):
    start_x = where_ref[0:1]
    total_ref[...] = near_ref[...]
    even = side_ref[0] == 0
    below, above = turn_of(-HALF), turn_of(wide)
    sides = (
        (first_halo_ref, jnp.where(even, wide, -HALF), either(even, above, below)),
        (second_halo_ref, jnp.where(even, -HALF, wide), either(even, below, above)),
    )
    for voxels_ref, at_x, turn in sides:
        total_ref[...] += block_modes(
            voxels_ref[...], at_x.astype(jnp.float32), turn, start_x,
            depth_ref, high_ref, part_ref, plane_ref,
        )
    rows = rotate(total_ref[...], start_x, where_ref[1:2])
    width = own_ref.shape[1]
    first_out_ref[...] = rows[:, :width].astype(jnp.bfloat16)
    own_ref[...] = rows[:, width : 2 * width]
    second_out_ref[...] = rows[:, 2 * width :].astype(jnp.bfloat16)


def join_kernel(own_ref, left_ref, right_ref, multiplicity_ref, *refs):
    outs, wide_ref = refs[:-1], refs[-1]
    total = own_ref[...] + left_ref[...].astype(jnp.float32) + right_ref[...].astype(jnp.float32)
    total = total.astype(jnp.bfloat16)
    rows, lanes = total.shape
    slots, group = lanes // L, rows // L

    def grid_of(shape, axis):
        return lax.broadcasted_iota(jnp.int32, shape, axis)

    def ones_where(flag):
        return jnp.where(flag, 1.0, 0.0).astype(jnp.bfloat16)

    square = (slots * group, lanes)
    mine = ones_where(grid_of(square, 0) // group == grid_of(square, 1) // L)
    square = (lanes, L * L)
    tiled = ones_where(lax.rem(grid_of(square, 0), L) == lax.rem(grid_of(square, 1), L))
    square = (slots * group, L * L)
    place = lax.rem(grid_of(square, 0), group) + 1
    place = jnp.where(place == group, 0, place)
    keep = ones_where(place == grid_of(square, 1) // L)
    square = (slots, slots * group)
    sums = ones_where(grid_of(square, 1) // group == grid_of(square, 0))
    copies = jnp.concatenate(
        [
            jnp.concatenate([total[a * group : (a + 1) * group]] * slots, axis=0) * mine
            for a in range(L)
        ],
        axis=0,
    )
    placed = jnp.dot(copies, tiled, preferred_element_type=jnp.float32).astype(jnp.bfloat16)
    flat = jnp.concatenate(
        [placed[a * rows : (a + 1) * rows] * keep for a in range(L)], axis=1
    )
    wide_ref[...] = jnp.dot(sums, flat, preferred_element_type=jnp.float32)
    wide = wide_ref[...]
    norm = jnp.sqrt(jnp.mean(wide * wide, axis=1, keepdims=True) + EPSILON)
    high = norm.astype(jnp.bfloat16).astype(jnp.float32)
    tail = lax.broadcasted_iota(jnp.int32, (slots, 128), 1)
    tail = jnp.where(tail == 0, high, jnp.where(tail == 1, norm - high, 0.0))
    row = jnp.concatenate(
        [wide.astype(jnp.bfloat16), multiplicity_ref[...], tail.astype(jnp.bfloat16)], axis=1
    )
    for k, out_ref in enumerate(outs):
        count = out_ref.shape[0]
        out_ref[...] = row[k * count : (k + 1) * count]


def block_copies(blocks, rows_ref, tail_ref, sems):
    copies, at = [], 0
    for k, block in enumerate(blocks):
        count = block.shape[0]
        place = pl.ds(at, count)
        copies.append(
            pltpu.make_async_copy(block.at[:, pl.ds(0, F)], rows_ref.at[place], sems.at[2 * k])
        )
        if tail_ref is not None:
            copies.append(
                pltpu.make_async_copy(
                    block.at[:, pl.ds(F, block.shape[1] - F)], tail_ref.at[place], sems.at[2 * k + 1]
                )
            )
        at += count
    return copies


def read_tail(bank_ref, tail, tail_ref, multiplicity_ref, orients):
    tail_ref[...] = tail.astype(jnp.float32).T
    start = pl.multiple_of(bank_ref[0] * orients, orients)
    norm = tail_ref[R : R + 1, :] + tail_ref[R + 1 : R + 2, :]
    multiplicity_ref[...] = tail_ref[pl.ds(start, orients), :] / (F * norm)


def inverse_norms(bank_rows):
    wide = bank_rows.astype(jnp.float32)
    return 1.0 / jnp.sqrt(jnp.mean(wide * wide, axis=1, keepdims=True) + EPSILON)


def weigh(bank_rows, inverse, rows, multiplicity, count):
    scores = lax.dot_general(
        bank_rows, rows, (((1,), (1,)), ((), ())), preferred_element_type=jnp.float32
    )
    multiplicity = jnp.concatenate([multiplicity] * count, axis=0)
    return (multiplicity * jnp.maximum(scores * inverse, 0.0)).astype(jnp.bfloat16)


def weigh_kernel(index_ref, *refs, blocks, known):
    sources, bank_ref = refs[:blocks], refs[blocks]
    if known:
        norms_ref, out_ref = refs[blocks + 1 : blocks + 3]
    else:
        out_ref, norms_ref = refs[blocks + 1 : blocks + 3]
    rows_ref, tail_ref, turned_ref, multiplicity_ref, sems = refs[blocks + 3 :]
    count, orients, width = bank_ref.shape

    @pl.when(pl.program_id(0) == 0)
    def _():
        copies = block_copies(sources, rows_ref, tail_ref, sems)
        for copy in copies:
            copy.start()
        for copy in copies:
            copy.wait()
        read_tail(index_ref, tail_ref[...], turned_ref, multiplicity_ref, orients)

    bank = bank_ref[...].reshape(count * orients, width)
    if known:
        inverse = norms_ref[...].reshape(count * orients, norms_ref.shape[2])[:, :1]
    else:
        inverse = inverse_norms(bank)
        norms_ref[...] = jnp.broadcast_to(inverse, (count * orients, norms_ref.shape[2])).reshape(
            norms_ref.shape
        )
    weights = weigh(bank, inverse, rows_ref[...], multiplicity_ref[...], count)
    out_ref[...] = weights.reshape(out_ref.shape)


def sum_kernel(index_ref, *refs, early, blocks, late, group):
    parts, sources = refs[:early], refs[early : early + blocks]
    norms_ref, bank_ref, out_ref, sums_ref = refs[early + blocks : early + blocks + 4]
    rows_ref, last_ref, tail_ref, turned_ref, multiplicity_ref, weights_ref, sems, last_sems = refs[
        early + blocks + 4 :
    ]
    count, orients, width = out_ref.shape
    boxes, last = rows_ref.shape[0], last_ref.shape[0]
    step = pl.program_id(0)

    @pl.when(step == 0)
    def _():
        copies = block_copies(sources, rows_ref, None, sems)
        urgent = block_copies(sources[blocks - late :], last_ref, tail_ref, last_sems)
        for copy in urgent + copies:
            copy.start()
        for copy in urgent:
            copy.wait()
        read_tail(index_ref, tail_ref[...], turned_ref, multiplicity_ref, orients)
        for c in range(0, bank_ref.shape[0], group):
            bank = bank_ref[c : c + group].reshape(group * orients, width)
            inverse = norms_ref[c : c + group].reshape(group * orients, norms_ref.shape[2])[:, :1]
            weights = weigh(bank, inverse, last_ref[...], multiplicity_ref[...], group)
            weights_ref[c : c + group] = weights.reshape(group, orients, last)
        for copy in copies:
            copy.wait()

    known = [part[...].reshape(count * orients, part.shape[2]) for part in parts]
    at = pl.multiple_of(step * count, count)
    known.append(weights_ref[pl.ds(at, count)].reshape(count * orients, last))
    weights = jnp.concatenate(known, axis=1)
    total = jnp.dot(weights, rows_ref[...], preferred_element_type=jnp.float32)
    out_ref[...] = total.reshape(out_ref.shape)
    ones = jnp.ones((8, boxes), jnp.bfloat16)
    sums = lax.dot_general(
        ones, weights, (((1,), (1,)), ((), ())), preferred_element_type=jnp.float32
    )
    for c in range(count):
        sums_ref[pl.ds(step * count + c, 1), :] = sums[:1, c * orients : (c + 1) * orients]


def score_plain(rows, bank):
    local_rows = bank.shape[0]
    start = F + lax.axis_index("bank") * local_rows
    multiplicity = lax.dynamic_slice_in_dim(rows, start, local_rows, 1).astype(jnp.float32)
    norm = rows[:, F + R].astype(jnp.float32) + rows[:, F + R + 1].astype(jnp.float32)
    features = rows[:, :F]
    scores = jnp.einsum("if,rcf->irc", features, bank, preferred_element_type=jnp.float32)
    wide = bank.astype(jnp.float32)
    bank_norm = jnp.sqrt(jnp.mean(wide * wide, axis=2) + EPSILON)
    correl = scores / (F * norm[:, None, None] * bank_norm[None])
    weights = (multiplicity[:, :, None] * jnp.maximum(correl, 0.0)).astype(jnp.bfloat16)
    class_sums = jnp.einsum("irc,if->rcf", weights, features, preferred_element_type=jnp.float32)
    return class_sums, jnp.sum(weights.astype(jnp.float32), axis=0)


def exchange(value, axis, first):
    count = lax.axis_size(axis)
    pairs = []
    for i in range(0 if first else 1, count - 1, 2):
        pairs += [(i, i + 1), (i + 1, i)]
    return lax.ppermute(value, axis, pairs)


def gather_score(mine, reference_bank):
    tiles, banks = lax.axis_size("tile"), lax.axis_size("bank")
    local_rows, classes, width = reference_bank.shape
    boxes = tiles * banks * sum(part.shape[0] for part in mine)
    if banks != 4 or tiles & (tiles - 1) or tiles < 4 or boxes > 1024 or classes % 5:
        rows = jnp.concatenate(mine, axis=0)
        for axis in ("bank", "tile"):
            rows = lax.all_gather(rows, axis, axis=0, tiled=True)
        return score_plain(rows, reference_bank)
    bank = jnp.transpose(reference_bank, (1, 0, 2))
    early, late = mine

    def along_x(value):
        return lax.ppermute(value, "bank", [(0, 1), (1, 0), (2, 3), (3, 2)])

    def along_y(value):
        return lax.ppermute(value, "bank", [(0, 2), (2, 0), (1, 3), (3, 1)])

    def swap(*values):
        return [lax.ppermute(value, "tile", [(i, i ^ 1) for i in range(tiles)]) for value in values]

    def line_of(part):
        others = [
            lax.ppermute(part, "tile", [(i, i ^ by) for i in range(tiles)])
            for by in range(2, tiles, 2)
        ]
        return jnp.concatenate([part] + others, axis=0)

    def with_swap(*values):
        joined = jnp.concatenate(values, axis=0) if len(values) > 1 else values[0]
        return [*values, *swap(joined)]

    early_line = line_of(early)
    late, early_line = lax.optimization_barrier((late, early_line))
    from_x, from_y = along_x(early_line), along_y(early_line)
    late_line = line_of(late)
    half = early_line.shape[0] // 2
    to_x = jnp.concatenate([from_y[half:], late_line], axis=0)
    to_y = jnp.concatenate([from_x[:half], late_line], axis=0)
    known = with_swap(early_line, from_x, from_y)
    to_x, to_y = lax.optimization_barrier((to_x, to_y))
    next_x, next_y = along_x(to_x), along_y(to_y)
    known += with_swap(to_x[half:])
    first, norms = weigh_blocks(known, bank)
    first, next_x, next_y = lax.optimization_barrier((first, next_x, next_y))
    last_x, last_y = along_x(next_y[half + half :]), along_y(next_x[half : half + half])
    late = with_swap(next_x, next_y) + with_swap(last_x, last_y)
    out, sums = sum_blocks([first], known, late, norms, bank)
    return jnp.transpose(out, (1, 0, 2)), jnp.transpose(sums, (1, 0))


CLASSES = 5


def bank_index():
    return lax.axis_index("bank").astype(jnp.int32)[None]


def weigh_blocks(blocks, bank, norms=None):
    classes, orients, width = bank.shape
    boxes = sum(block.shape[0] for block in blocks)
    tail = blocks[0].shape[1] - F
    known = norms is not None
    norm_spec = pl.BlockSpec((CLASSES, orients, 128), lambda i: (i, 0, 0))
    out_spec = pl.BlockSpec((CLASSES, orients, boxes), lambda i: (i, 0, 0))
    out_shape = jax.ShapeDtypeStruct((classes, orients, boxes), jnp.bfloat16)
    norm_shape = jax.ShapeDtypeStruct((classes, orients, 128), jnp.float32)
    return pl.pallas_call(
        functools.partial(weigh_kernel, blocks=len(blocks), known=known),
        grid=(classes // CLASSES,),
        in_specs=[pl.BlockSpec(memory_space=pltpu.SMEM)]
        + [pl.BlockSpec(memory_space=pl.ANY)] * len(blocks)
        + [pl.BlockSpec((CLASSES, orients, width), lambda i: (i, 0, 0))]
        + ([norm_spec] if known else []),
        out_specs=out_spec if known else [out_spec, norm_spec],
        out_shape=out_shape if known else [out_shape, norm_shape],
        scratch_shapes=[
            pltpu.VMEM((boxes, F), jnp.bfloat16),
            pltpu.VMEM((boxes, tail), jnp.bfloat16),
            pltpu.VMEM((tail, boxes), jnp.float32),
            pltpu.VMEM((orients, boxes), jnp.float32),
            pltpu.SemaphoreType.DMA((2 * len(blocks),)),
        ],
        compiler_params=pltpu.CompilerParams(vmem_limit_bytes=18 * MIB),
        cost_estimate=pl.CostEstimate(
            flops=boxes * classes * orients * width // 8,
            bytes_accessed=classes * orients * width // 8,
            transcendentals=0,
        ),
        name="weigh",
    )(bank_index(), *blocks, bank, *([norms] if known else []))


def sum_blocks(parts, blocks, late, norms, bank):
    classes, orients, width = bank.shape
    blocks = blocks + late
    boxes = sum(block.shape[0] for block in blocks)
    last = sum(block.shape[0] for block in late)
    tail = blocks[0].shape[1] - F
    vmem = pl.BlockSpec(memory_space=pltpu.VMEM)
    return pl.pallas_call(
        functools.partial(
            sum_kernel, early=len(parts), blocks=len(blocks), late=len(late), group=CLASSES
        ),
        grid=(classes // CLASSES,),
        in_specs=[pl.BlockSpec(memory_space=pltpu.SMEM)]
        + [pl.BlockSpec((CLASSES, orients, part.shape[2]), lambda i: (i, 0, 0)) for part in parts]
        + [pl.BlockSpec(memory_space=pl.ANY)] * len(blocks)
        + [vmem, vmem],
        out_specs=[
            pl.BlockSpec((CLASSES, orients, width), lambda i: (i, 0, 0)),
            pl.BlockSpec((classes, orients), lambda i: (0, 0)),
        ],
        out_shape=[
            jax.ShapeDtypeStruct((classes, orients, width), jnp.float32),
            jax.ShapeDtypeStruct((classes, orients), jnp.float32),
        ],
        scratch_shapes=[
            pltpu.VMEM((boxes, F), jnp.bfloat16),
            pltpu.VMEM((last, F), jnp.bfloat16),
            pltpu.VMEM((last, tail), jnp.bfloat16),
            pltpu.VMEM((tail, last), jnp.float32),
            pltpu.VMEM((orients, last), jnp.float32),
            pltpu.VMEM((classes, orients, last), jnp.bfloat16),
            pltpu.SemaphoreType.DMA((2 * len(blocks),)),
            pltpu.SemaphoreType.DMA((2 * len(late),)),
        ],
        compiler_params=pltpu.CompilerParams(vmem_limit_bytes=34 * MIB),
        cost_estimate=pl.CostEstimate(
            flops=2 * boxes * classes * orients * width,
            bytes_accessed=4 * classes * orients * width,
            transcendentals=0,
        ),
        name="class_sums",
    )(bank_index(), *parts, *blocks, norms, bank)


def body(volume, pick_list, box_counts, orientations, orient_weight, reference_bank):
    wide, high, depth = volume.shape
    slots = pick_list.shape[3]
    tile, bank = lax.axis_index("tile"), lax.axis_index("bank")
    side = lax.rem(tile, 2).astype(jnp.int32)
    rest = wide - HALF
    to_first = lax.dynamic_slice_in_dim(volume, jnp.where(side == 0, rest, 0), HALF, 0)
    to_second = lax.dynamic_slice_in_dim(volume, jnp.where(side == 0, 0, rest), HALF, 0)
    first_halo = exchange(to_first, "tile", True)
    second_halo = exchange(to_second, "tile", False)
    picks, first_halo = lax.optimization_barrier((pick_list, first_halo))
    first_picks, second_picks = exchange(picks, "bank", True), exchange(picks, "bank", False)
    origin = jnp.stack([tile * wide + HALF, bank * high + HALF]).astype(jnp.int32)

    first, second = depth_tables(depth)
    plane = jnp.asarray(plane_table(HALF, high), jnp.bfloat16)
    modes, lanes = plane.shape[0], 3 * slots * L
    unit = 32

    params = pltpu.CompilerParams(vmem_limit_bytes=32 * MIB)
    vmem = pl.BlockSpec(memory_space=pltpu.VMEM)
    smem = pl.BlockSpec(memory_space=pltpu.SMEM)
    near, *tables = pl.pallas_call(
        near_kernel,
        in_specs=[smem] + [vmem] * 7,
        out_specs=[vmem] * 4,
        out_shape=[
            jax.ShapeDtypeStruct((modes, lanes), jnp.float32),
            jax.ShapeDtypeStruct((depth, lanes), jnp.bfloat16),
            jax.ShapeDtypeStruct((high, lanes), jnp.float32),
            jax.ShapeDtypeStruct((8, lanes), jnp.float32),
        ],
        scratch_shapes=[pltpu.VMEM((unit * high, lanes), jnp.bfloat16)],
        compiler_params=params,
        cost_estimate=pl.CostEstimate(
            flops=2 * wide * high * lanes * (depth + modes), bytes_accessed=8000000, transcendentals=0
        ),
        name="near_rows",
    )(origin, first_picks, picks, second_picks, first, second, volume, plane)
    for_first, mid, for_second = pl.pallas_call(
        functools.partial(far_kernel, wide=wide),
        in_specs=[smem] + [vmem] * 7,
        out_specs=[vmem] * 3,
        out_shape=[
            jax.ShapeDtypeStruct((L * L, slots * L), jnp.bfloat16),
            jax.ShapeDtypeStruct((L * L, slots * L), jnp.float32),
            jax.ShapeDtypeStruct((L * L, slots * L), jnp.bfloat16),
        ],
        scratch_shapes=[
            pltpu.VMEM((HALF * high, lanes), jnp.bfloat16),
            pltpu.VMEM((modes, lanes), jnp.float32),
        ],
        compiler_params=params,
        name="far_rows",
    )(side[None], *tables, first_halo, second_halo, plane, near)
    from_first, from_second = exchange(for_first, "bank", True), exchange(for_second, "bank", False)

    mid, orientations, orient_weight = lax.optimization_barrier((mid, orientations, orient_weight))
    live_slots = jnp.arange(slots) < box_counts[0, 0]
    matches = orientations[0, 0][:, :, None] == jnp.arange(R)[None, None, :]
    multiplicity = jnp.sum(
        jnp.where(matches, orient_weight[0, 0][:, :, None].astype(jnp.float32), 0.0), axis=1
    )
    multiplicity = jnp.where(live_slots[:, None], multiplicity, 0.0).astype(jnp.bfloat16)
    parts = 2
    mine = pl.pallas_call(
        join_kernel,
        out_shape=[jax.ShapeDtypeStruct((slots // parts, F + R + 128), jnp.bfloat16)] * parts,
        scratch_shapes=[pltpu.VMEM((slots, F), jnp.float32)],
        compiler_params=params,
        name="join",
    )(mid, from_first, from_second, multiplicity)
    return gather_score(mine, reference_bank)


def solution(mesh):
    in_specs = (
        P("tile", "bank", None),
        P(None, "tile", "bank", None),
        P("tile", "bank"),
        P("tile", "bank", None, None),
        P("tile", "bank", None, None),
        P("bank", None, None),
    )
    out_specs = (P("bank", None, None), P("bank", None))
    return jax.shard_map(body, mesh=mesh, in_specs=in_specs, out_specs=out_specs, check_vma=False)
```

```python
import functools

import jax
import jax.numpy as jnp
import numpy as np
from jax import lax
from jax.experimental import pallas as pl
from jax.experimental.pallas import tpu as pltpu
from jax.sharding import PartitionSpec as P

B = 96
L = 16
R = 256
F = L * L * L
HALF = B // 2
TERMS = L // 2
EPSILON = 1e-06
MIB = 1024 * 1024


def waves(count):
    steps = 2.0 * np.pi * np.outer(np.arange(TERMS + 1), np.arange(count)) / B
    return np.cos(steps) / np.sqrt(B), np.sin(steps) / np.sqrt(B)


def depth_tables(depth):
    cos, sin = waves(depth)
    first = np.concatenate([cos, sin[1:TERMS]], axis=0)
    second = np.concatenate([sin, -cos[1:TERMS]], axis=0)
    repeat = 128 // L
    return (
        np.tile(first.T, (1, repeat)).astype(np.float32),
        np.tile(second.T, (1, repeat)).astype(np.float32),
    )


def plane_table(wide, high):
    cos_x, sin_x = waves(wide)
    cos_y, sin_y = waves(high)
    along_x = np.concatenate([cos_x, sin_x[1:]], axis=0)
    along_y = np.concatenate([cos_y[1:], sin_y[1:]], axis=0)
    main = np.einsum("ax,by->abxy", along_x, along_y).reshape(-1, wide * high)
    order = np.concatenate([along_x[1:], along_x[:1]], axis=0)
    flat = np.einsum("ax,y->axy", order, cos_y[0]).reshape(-1, wide * high)
    rows = np.concatenate([main, flat], axis=0)
    pad = -rows.shape[0] % 16
    return np.concatenate([rows, np.zeros((pad, rows.shape[1]))], axis=0).astype(np.float32)


def spread(origin_ref, corner_refs, lanes):
    slots = corner_refs[0].shape[3]
    box = lax.broadcasted_iota(jnp.int32, (slots, lanes), 0)
    lane = lax.broadcasted_iota(jnp.int32, (slots, lanes), 1)
    row = lax.broadcasted_iota(jnp.int32, (8, slots), 0)
    origin = jnp.where(row == 0, origin_ref[0], jnp.where(row == 1, origin_ref[1], 0))
    total = jnp.zeros((8, lanes), jnp.float32)
    for k, corner_ref in enumerate(corner_refs):
        corners = jnp.zeros((8, slots), jnp.int32)
        for axis in range(3):
            corners = jnp.where(row == axis, corner_ref[axis, 0], corners)
        corners = (corners - origin).astype(jnp.float32).astype(jnp.bfloat16)
        pick = jnp.where(lane // L == box + k * slots, 1.0, 0.0).astype(jnp.bfloat16)
        total += jnp.dot(corners, pick, preferred_element_type=jnp.float32)
    return total


def turns(terms, shift):
    turn = (terms * shift).astype(jnp.int32)
    turn = lax.rem(turn, B)
    angle = turn.astype(jnp.float32) * (2.0 * np.pi / B)
    return jnp.cos(angle), jnp.sin(angle)


def prepare(origin_ref, corner_refs, first_ref, second_ref, depth_ref, high_ref, where_ref):
    depth, lanes = depth_ref.shape
    where = spread(origin_ref, corner_refs, lanes)
    where_ref[...] = where
    start_y, start_z = where[1:2], where[2:3]
    lane = lax.rem(lax.broadcasted_iota(jnp.int32, (1, lanes), 1), L)
    term = jnp.where(lane <= TERMS, lane, lane - TERMS).astype(jnp.float32)
    cos, sin = turns(term, start_z)
    copies = lanes // first_ref.shape[1]
    first = jnp.concatenate([first_ref[...]] * copies, axis=1)
    second = jnp.concatenate([second_ref[...]] * copies, axis=1)
    z = lax.broadcasted_iota(jnp.int32, (depth, lanes), 0).astype(jnp.float32) - start_z
    table = jnp.where((z >= 0) & (z < B), first * cos + second * sin, 0.0)
    depth_ref[...] = table.astype(jnp.bfloat16)
    y = lax.broadcasted_iota(jnp.int32, high_ref.shape, 0).astype(jnp.float32) - start_y
    high_ref[...] = jnp.where((y >= 0) & (y < B), 1.0, 0.0)


def block_modes(voxels, at_x, turn, start_x, depth_ref, high_ref, part_ref, plane_ref):
    count, high, depth = voxels.shape
    offset = at_x - start_x
    rows = voxels.reshape(count * high, depth)
    first = jnp.dot(rows, depth_ref[...], preferred_element_type=jnp.float32)
    for x in range(count):
        at = offset + float(x)
        live = high_ref[...] * jnp.where((at >= 0) & (at < B), 1.0, 0.0)
        kept = first[x * high : (x + 1) * high] * live
        part_ref[pl.ds(x * high, high), :] = kept.astype(jnp.bfloat16)
    length = count * high
    total = jnp.dot(
        plane_ref[:, :length], part_ref[:length], preferred_element_type=jnp.float32
    )
    return total if turn is None else moved(total, turn)


def turn_of(at_x):
    angles = 2.0 * np.pi * np.arange(1, TERMS + 1) * at_x / B
    return [float(c) for c in np.cos(angles)], [float(s) for s in np.sin(angles)]


def either(flag, one, other):
    return tuple([jnp.where(flag, a, b) for a, b in zip(u, v)] for u, v in zip(one, other))


def moved(total, turn):
    group, blocks = 2 * TERMS, 2 * TERMS + 1
    rows = [total[a * group : (a + 1) * group] for a in range(blocks)]
    main = blocks * group
    flat_cos, flat_sin = total[main : main + TERMS], total[main + TERMS : main + group]
    out = list(rows)
    term = lax.broadcasted_iota(jnp.int32, flat_cos.shape, 0)
    flat_c, flat_s = jnp.zeros_like(flat_cos), jnp.zeros_like(flat_cos)
    for j, (c, s) in enumerate(zip(*turn)):
        out[1 + j] = rows[1 + j] * c - rows[1 + TERMS + j] * s
        out[1 + TERMS + j] = rows[1 + j] * s + rows[1 + TERMS + j] * c
        flat_c = jnp.where(term == j, c, flat_c)
        flat_s = jnp.where(term == j, s, flat_s)
    out += [
        flat_cos * flat_c - flat_sin * flat_s,
        flat_cos * flat_s + flat_sin * flat_c,
        total[main + group :],
    ]
    return jnp.concatenate(out, axis=0)


def near_kernel(
    origin_ref, first_pick_ref, pick_ref, second_pick_ref, first_ref, second_ref, volume_ref, plane_ref,
    total_ref, depth_ref, high_ref, where_ref, part_ref,
):
    corner_refs = (first_pick_ref, pick_ref, second_pick_ref)
    prepare(origin_ref, corner_refs, first_ref, second_ref, depth_ref, high_ref, where_ref)
    start_x = where_ref[0:1]
    unit = part_ref.shape[0] // volume_ref.shape[1]
    for x in range(0, volume_ref.shape[0], unit):
        added = block_modes(
            volume_ref[x : x + unit], float(x), turn_of(x) if x else None, start_x,
            depth_ref, high_ref, part_ref, plane_ref,
        )
        total_ref[...] = added if x == 0 else total_ref[...] + added


def rotate(total, start_x, start_y):
    lanes = total.shape[1]
    term = (lax.broadcasted_iota(jnp.int32, (TERMS, lanes), 0) + 1).astype(jnp.float32)
    cos_x, sin_x = turns(term, start_x)
    cos_y, sin_y = turns(term, start_y)
    blocks = 2 * TERMS + 1
    main = blocks * 2 * TERMS
    flat_cos = total[main : main + TERMS]
    flat_sin = total[main + TERMS : main + 2 * TERMS]
    flat_zero = total[main + 2 * TERMS : main + 2 * TERMS + 1]
    flats = (
        [flat_zero]
        + [flat_cos[j : j + 1] for j in range(TERMS)]
        + [flat_sin[j : j + 1] for j in range(TERMS)]
    )
    last = lax.broadcasted_iota(jnp.int32, (TERMS, lanes), 0) == TERMS - 1
    turned = []
    for a in range(blocks):
        cos = total[a * 2 * TERMS : a * 2 * TERMS + TERMS]
        sin = total[a * 2 * TERMS + TERMS : (a + 1) * 2 * TERMS]
        low = cos * cos_y + sin * sin_y
        high = sin * cos_y - cos * sin_y
        turned.append((low, jnp.where(last, flats[a], high)))
    rows = [None] * (2 * TERMS)
    rows[0] = turned[0]
    for j in range(1, TERMS + 1):
        c, s = cos_x[j - 1 : j], sin_x[j - 1 : j]
        cos, sin = turned[j], turned[TERMS + j]
        rows[j] = tuple(u * c + v * s for u, v in zip(cos, sin))
        if j < TERMS:
            rows[TERMS + j] = tuple(v * c - u * s for u, v in zip(cos, sin))
    return jnp.concatenate([half for pair in rows for half in pair], axis=0)


def far_kernel(
    side_ref, depth_ref, high_ref, where_ref, first_halo_ref, second_halo_ref, plane_ref, near_ref,
    first_out_ref, own_ref, second_out_ref, part_ref, total_ref, *, wide,
):
    start_x = where_ref[0:1]
    total_ref[...] = near_ref[...]
    even = side_ref[0] == 0
    below, above = turn_of(-HALF), turn_of(wide)
    sides = (
        (first_halo_ref, jnp.where(even, wide, -HALF), either(even, above, below)),
        (second_halo_ref, jnp.where(even, -HALF, wide), either(even, below, above)),
    )
    for voxels_ref, at_x, turn in sides:
        total_ref[...] += block_modes(
            voxels_ref[...], at_x.astype(jnp.float32), turn, start_x,
            depth_ref, high_ref, part_ref, plane_ref,
        )
    rows = rotate(total_ref[...], start_x, where_ref[1:2])
    width = own_ref.shape[1]
    first_out_ref[...] = rows[:, :width].astype(jnp.bfloat16)
    own_ref[...] = rows[:, width : 2 * width]
    second_out_ref[...] = rows[:, 2 * width :].astype(jnp.bfloat16)


def join_kernel(own_ref, left_ref, right_ref, multiplicity_ref, *refs):
    outs, wide_ref = refs[:-1], refs[-1]
    total = own_ref[...] + left_ref[...].astype(jnp.float32) + right_ref[...].astype(jnp.float32)
    total = total.astype(jnp.bfloat16)
    rows, lanes = total.shape
    slots, group = lanes // L, rows // L

    def grid_of(shape, axis):
        return lax.broadcasted_iota(jnp.int32, shape, axis)

    def ones_where(flag):
        return jnp.where(flag, 1.0, 0.0).astype(jnp.bfloat16)

    square = (slots * group, lanes)
    mine = ones_where(grid_of(square, 0) // group == grid_of(square, 1) // L)
    square = (lanes, L * L)
    tiled = ones_where(lax.rem(grid_of(square, 0), L) == lax.rem(grid_of(square, 1), L))
    square = (slots * group, L * L)
    place = lax.rem(grid_of(square, 0), group) + 1
    place = jnp.where(place == group, 0, place)
    keep = ones_where(place == grid_of(square, 1) // L)
    square = (slots, slots * group)
    sums = ones_where(grid_of(square, 1) // group == grid_of(square, 0))
    copies = jnp.concatenate(
        [
            jnp.concatenate([total[a * group : (a + 1) * group]] * slots, axis=0) * mine
            for a in range(L)
        ],
        axis=0,
    )
    placed = jnp.dot(copies, tiled, preferred_element_type=jnp.float32).astype(jnp.bfloat16)
    flat = jnp.concatenate(
        [placed[a * rows : (a + 1) * rows] * keep for a in range(L)], axis=1
    )
    wide_ref[...] = jnp.dot(sums, flat, preferred_element_type=jnp.float32)
    wide = wide_ref[...]
    norm = jnp.sqrt(jnp.mean(wide * wide, axis=1, keepdims=True) + EPSILON)
    high = norm.astype(jnp.bfloat16).astype(jnp.float32)
    tail = lax.broadcasted_iota(jnp.int32, (slots, 128), 1)
    tail = jnp.where(tail == 0, high, jnp.where(tail == 1, norm - high, 0.0))
    row = jnp.concatenate([wide, multiplicity_ref[...].astype(jnp.float32), tail], axis=1)
    for k, out_ref in enumerate(outs):
        count = out_ref.shape[0]
        out_ref[...] = row[k * count : (k + 1) * count].astype(jnp.bfloat16)


def block_copies(blocks, rows_ref, tail_ref, sems):
    copies, at = [], 0
    for k, block in enumerate(blocks):
        count = block.shape[0]
        place = pl.ds(at, count)
        copies.append(
            pltpu.make_async_copy(block.at[:, pl.ds(0, F)], rows_ref.at[place], sems.at[2 * k])
        )
        if tail_ref is not None:
            copies.append(
                pltpu.make_async_copy(
                    block.at[:, pl.ds(F, block.shape[1] - F)], tail_ref.at[place], sems.at[2 * k + 1]
                )
            )
        at += count
    return copies


def read_tail(bank_ref, tail, tail_ref, multiplicity_ref, orients):
    tail_ref[...] = tail.astype(jnp.float32).T
    start = pl.multiple_of(bank_ref[0] * orients, orients)
    norm = tail_ref[R : R + 1, :] + tail_ref[R + 1 : R + 2, :]
    multiplicity_ref[...] = tail_ref[pl.ds(start, orients), :] / (F * norm)


def inverse_norms(bank_rows):
    wide = bank_rows.astype(jnp.float32)
    return 1.0 / jnp.sqrt(jnp.mean(wide * wide, axis=1, keepdims=True) + EPSILON)


def weigh(bank_rows, inverse, rows, multiplicity, count):
    scores = lax.dot_general(
        bank_rows, rows, (((1,), (1,)), ((), ())), preferred_element_type=jnp.float32
    )
    multiplicity = jnp.concatenate([multiplicity] * count, axis=0)
    return (multiplicity * jnp.maximum(scores * inverse, 0.0)).astype(jnp.bfloat16)


def weigh_kernel(index_ref, *refs, blocks, known):
    sources, bank_ref = refs[:blocks], refs[blocks]
    if known:
        norms_ref, out_ref = refs[blocks + 1 : blocks + 3]
    else:
        out_ref, norms_ref = refs[blocks + 1 : blocks + 3]
    rows_ref, tail_ref, turned_ref, multiplicity_ref, sems = refs[blocks + 3 :]
    count, orients, width = bank_ref.shape

    @pl.when(pl.program_id(0) == 0)
    def _():
        copies = block_copies(sources, rows_ref, tail_ref, sems)
        for copy in copies:
            copy.start()
        for copy in copies:
            copy.wait()
        read_tail(index_ref, tail_ref[...], turned_ref, multiplicity_ref, orients)

    bank = bank_ref[...].reshape(count * orients, width)
    if known:
        inverse = norms_ref[...].reshape(count * orients, norms_ref.shape[2])[:, :1]
    else:
        inverse = inverse_norms(bank)
        norms_ref[...] = jnp.broadcast_to(inverse, (count * orients, norms_ref.shape[2])).reshape(
            norms_ref.shape
        )
    weights = weigh(bank, inverse, rows_ref[...], multiplicity_ref[...], count)
    out_ref[...] = weights.reshape(out_ref.shape)


def sum_kernel(index_ref, *refs, early, blocks, late, group):
    parts, sources = refs[:early], refs[early : early + blocks]
    norms_ref, bank_ref, out_ref, sums_ref = refs[early + blocks : early + blocks + 4]
    rows_ref, last_ref, tail_ref, turned_ref, multiplicity_ref, weights_ref, sems, last_sems = refs[
        early + blocks + 4 :
    ]
    count, orients, width = out_ref.shape
    boxes, last = rows_ref.shape[0], last_ref.shape[0]
    step = pl.program_id(0)

    @pl.when(step == 0)
    def _():
        copies = block_copies(sources, rows_ref, None, sems)
        urgent = block_copies(sources[blocks - late :], last_ref, tail_ref, last_sems)
        for copy in urgent + copies:
            copy.start()
        for copy in urgent:
            copy.wait()
        read_tail(index_ref, tail_ref[...], turned_ref, multiplicity_ref, orients)
        for c in range(0, bank_ref.shape[0], group):
            bank = bank_ref[c : c + group].reshape(group * orients, width)
            inverse = norms_ref[c : c + group].reshape(group * orients, norms_ref.shape[2])[:, :1]
            weights = weigh(bank, inverse, last_ref[...], multiplicity_ref[...], group)
            weights_ref[c : c + group] = weights.reshape(group, orients, last)
        for copy in copies:
            copy.wait()

    known = [part[...].reshape(count * orients, part.shape[2]) for part in parts]
    at = pl.multiple_of(step * count, count)
    known.append(weights_ref[pl.ds(at, count)].reshape(count * orients, last))
    weights = jnp.concatenate(known, axis=1)
    total = jnp.dot(weights, rows_ref[...], preferred_element_type=jnp.float32)
    out_ref[...] = total.reshape(out_ref.shape)
    ones = jnp.ones((8, boxes), jnp.bfloat16)
    sums = lax.dot_general(
        ones, weights, (((1,), (1,)), ((), ())), preferred_element_type=jnp.float32
    )
    for c in range(count):
        sums_ref[pl.ds(step * count + c, 1), :] = sums[:1, c * orients : (c + 1) * orients]


def score_plain(rows, bank):
    local_rows = bank.shape[0]
    start = F + lax.axis_index("bank") * local_rows
    multiplicity = lax.dynamic_slice_in_dim(rows, start, local_rows, 1).astype(jnp.float32)
    norm = rows[:, F + R].astype(jnp.float32) + rows[:, F + R + 1].astype(jnp.float32)
    features = rows[:, :F]
    scores = jnp.einsum("if,rcf->irc", features, bank, preferred_element_type=jnp.float32)
    wide = bank.astype(jnp.float32)
    bank_norm = jnp.sqrt(jnp.mean(wide * wide, axis=2) + EPSILON)
    correl = scores / (F * norm[:, None, None] * bank_norm[None])
    weights = (multiplicity[:, :, None] * jnp.maximum(correl, 0.0)).astype(jnp.bfloat16)
    class_sums = jnp.einsum("irc,if->rcf", weights, features, preferred_element_type=jnp.float32)
    return class_sums, jnp.sum(weights.astype(jnp.float32), axis=0)


def exchange(value, axis, first):
    count = lax.axis_size(axis)
    pairs = []
    for i in range(0 if first else 1, count - 1, 2):
        pairs += [(i, i + 1), (i + 1, i)]
    return lax.ppermute(value, axis, pairs)


def gather_score(mine, reference_bank):
    tiles, banks = lax.axis_size("tile"), lax.axis_size("bank")
    local_rows, classes, width = reference_bank.shape
    boxes = tiles * banks * sum(part.shape[0] for part in mine)
    if banks != 4 or tiles & (tiles - 1) or tiles < 4 or boxes > 1024 or classes % 5:
        rows = jnp.concatenate(mine, axis=0)
        for axis in ("bank", "tile"):
            rows = lax.all_gather(rows, axis, axis=0, tiled=True)
        return score_plain(rows, reference_bank)
    bank = jnp.transpose(reference_bank, (1, 0, 2))
    early, late = mine

    def along_x(value):
        return lax.ppermute(value, "bank", [(0, 1), (1, 0), (2, 3), (3, 2)])

    def along_y(value):
        return lax.ppermute(value, "bank", [(0, 2), (2, 0), (1, 3), (3, 1)])

    def swap(*values):
        return [lax.ppermute(value, "tile", [(i, i ^ 1) for i in range(tiles)]) for value in values]

    def line_of(part):
        others = [
            lax.ppermute(part, "tile", [(i, i ^ by) for i in range(tiles)])
            for by in range(2, tiles, 2)
        ]
        return jnp.concatenate([part] + others, axis=0)

    def with_swap(*values):
        joined = jnp.concatenate(values, axis=0) if len(values) > 1 else values[0]
        return [*values, *swap(joined)]

    early_line = line_of(early)
    late, early_line = lax.optimization_barrier((late, early_line))
    from_x, from_y = along_x(early_line), along_y(early_line)
    late_line = line_of(late)
    half = early_line.shape[0] // 2
    to_x = jnp.concatenate([from_y[half:], late_line], axis=0)
    to_y = jnp.concatenate([from_x[:half], late_line], axis=0)
    known = with_swap(early_line, from_x, from_y)
    to_x, to_y = lax.optimization_barrier((to_x, to_y))
    next_x, next_y = along_x(to_x), along_y(to_y)
    known += with_swap(to_x[half:])
    first, norms = weigh_blocks(known, bank)
    first, next_x, next_y = lax.optimization_barrier((first, next_x, next_y))
    last_x, last_y = along_x(next_y[half + half :]), along_y(next_x[half : half + half])
    late = with_swap(next_x, next_y) + with_swap(last_x, last_y)
    out, sums = sum_blocks([first], known, late, norms, bank)
    return jnp.transpose(out, (1, 0, 2)), jnp.transpose(sums, (1, 0))


CLASSES = 5


def bank_index():
    return lax.axis_index("bank").astype(jnp.int32)[None]


def weigh_blocks(blocks, bank, norms=None):
    classes, orients, width = bank.shape
    boxes = sum(block.shape[0] for block in blocks)
    tail = blocks[0].shape[1] - F
    known = norms is not None
    norm_spec = pl.BlockSpec((CLASSES, orients, 128), lambda i: (i, 0, 0))
    out_spec = pl.BlockSpec((CLASSES, orients, boxes), lambda i: (i, 0, 0))
    out_shape = jax.ShapeDtypeStruct((classes, orients, boxes), jnp.bfloat16)
    norm_shape = jax.ShapeDtypeStruct((classes, orients, 128), jnp.float32)
    return pl.pallas_call(
        functools.partial(weigh_kernel, blocks=len(blocks), known=known),
        grid=(classes // CLASSES,),
        in_specs=[pl.BlockSpec(memory_space=pltpu.SMEM)]
        + [pl.BlockSpec(memory_space=pl.ANY)] * len(blocks)
        + [pl.BlockSpec((CLASSES, orients, width), lambda i: (i, 0, 0))]
        + ([norm_spec] if known else []),
        out_specs=out_spec if known else [out_spec, norm_spec],
        out_shape=out_shape if known else [out_shape, norm_shape],
        scratch_shapes=[
            pltpu.VMEM((boxes, F), jnp.bfloat16),
            pltpu.VMEM((boxes, tail), jnp.bfloat16),
            pltpu.VMEM((tail, boxes), jnp.float32),
            pltpu.VMEM((orients, boxes), jnp.float32),
            pltpu.SemaphoreType.DMA((2 * len(blocks),)),
        ],
        compiler_params=pltpu.CompilerParams(vmem_limit_bytes=18 * MIB),
        cost_estimate=pl.CostEstimate(
            flops=boxes * classes * orients * width // 8,
            bytes_accessed=classes * orients * width // 8,
            transcendentals=0,
        ),
        name="weigh",
    )(bank_index(), *blocks, bank, *([norms] if known else []))


def sum_blocks(parts, blocks, late, norms, bank):
    classes, orients, width = bank.shape
    blocks = blocks + late
    boxes = sum(block.shape[0] for block in blocks)
    last = sum(block.shape[0] for block in late)
    tail = blocks[0].shape[1] - F
    vmem = pl.BlockSpec(memory_space=pltpu.VMEM)
    return pl.pallas_call(
        functools.partial(
            sum_kernel, early=len(parts), blocks=len(blocks), late=len(late), group=CLASSES
        ),
        grid=(classes // CLASSES,),
        in_specs=[pl.BlockSpec(memory_space=pltpu.SMEM)]
        + [pl.BlockSpec((CLASSES, orients, part.shape[2]), lambda i: (i, 0, 0)) for part in parts]
        + [pl.BlockSpec(memory_space=pl.ANY)] * len(blocks)
        + [vmem, vmem],
        out_specs=[
            pl.BlockSpec((CLASSES, orients, width), lambda i: (i, 0, 0)),
            pl.BlockSpec((classes, orients), lambda i: (0, 0)),
        ],
        out_shape=[
            jax.ShapeDtypeStruct((classes, orients, width), jnp.float32),
            jax.ShapeDtypeStruct((classes, orients), jnp.float32),
        ],
        scratch_shapes=[
            pltpu.VMEM((boxes, F), jnp.bfloat16),
            pltpu.VMEM((last, F), jnp.bfloat16),
            pltpu.VMEM((last, tail), jnp.bfloat16),
            pltpu.VMEM((tail, last), jnp.float32),
            pltpu.VMEM((orients, last), jnp.float32),
            pltpu.VMEM((classes, orients, last), jnp.bfloat16),
            pltpu.SemaphoreType.DMA((2 * len(blocks),)),
            pltpu.SemaphoreType.DMA((2 * len(late),)),
        ],
        compiler_params=pltpu.CompilerParams(vmem_limit_bytes=34 * MIB),
        cost_estimate=pl.CostEstimate(
            flops=2 * boxes * classes * orients * width,
            bytes_accessed=4 * classes * orients * width,
            transcendentals=0,
        ),
        name="class_sums",
    )(bank_index(), *parts, *blocks, norms, bank)


def body(volume, pick_list, box_counts, orientations, orient_weight, reference_bank):
    wide, high, depth = volume.shape
    slots = pick_list.shape[3]
    tile, bank = lax.axis_index("tile"), lax.axis_index("bank")
    side = lax.rem(tile, 2).astype(jnp.int32)
    rest = wide - HALF
    to_first = lax.dynamic_slice_in_dim(volume, jnp.where(side == 0, rest, 0), HALF, 0)
    to_second = lax.dynamic_slice_in_dim(volume, jnp.where(side == 0, 0, rest), HALF, 0)
    first_halo = exchange(to_first, "tile", True)
    second_halo = exchange(to_second, "tile", False)
    picks, first_halo = lax.optimization_barrier((pick_list, first_halo))
    first_picks, second_picks = exchange(picks, "bank", True), exchange(picks, "bank", False)
    origin = jnp.stack([tile * wide + HALF, bank * high + HALF]).astype(jnp.int32)

    first, second = depth_tables(depth)
    plane = jnp.asarray(plane_table(HALF, high), jnp.bfloat16)
    modes, lanes = plane.shape[0], 3 * slots * L
    unit = 32

    params = pltpu.CompilerParams(vmem_limit_bytes=32 * MIB)
    vmem = pl.BlockSpec(memory_space=pltpu.VMEM)
    smem = pl.BlockSpec(memory_space=pltpu.SMEM)
    near, *tables = pl.pallas_call(
        near_kernel,
        in_specs=[smem] + [vmem] * 7,
        out_specs=[vmem] * 4,
        out_shape=[
            jax.ShapeDtypeStruct((modes, lanes), jnp.float32),
            jax.ShapeDtypeStruct((depth, lanes), jnp.bfloat16),
            jax.ShapeDtypeStruct((high, lanes), jnp.float32),
            jax.ShapeDtypeStruct((8, lanes), jnp.float32),
        ],
        scratch_shapes=[pltpu.VMEM((unit * high, lanes), jnp.bfloat16)],
        compiler_params=params,
        cost_estimate=pl.CostEstimate(
            flops=2 * wide * high * lanes * (depth + modes), bytes_accessed=8000000, transcendentals=0
        ),
        name="near_rows",
    )(origin, first_picks, picks, second_picks, first, second, volume, plane)
    for_first, mid, for_second = pl.pallas_call(
        functools.partial(far_kernel, wide=wide),
        in_specs=[smem] + [vmem] * 7,
        out_specs=[vmem] * 3,
        out_shape=[
            jax.ShapeDtypeStruct((L * L, slots * L), jnp.bfloat16),
            jax.ShapeDtypeStruct((L * L, slots * L), jnp.float32),
            jax.ShapeDtypeStruct((L * L, slots * L), jnp.bfloat16),
        ],
        scratch_shapes=[
            pltpu.VMEM((HALF * high, lanes), jnp.bfloat16),
            pltpu.VMEM((modes, lanes), jnp.float32),
        ],
        compiler_params=params,
        name="far_rows",
    )(side[None], *tables, first_halo, second_halo, plane, near)
    from_first, from_second = exchange(for_first, "bank", True), exchange(for_second, "bank", False)

    mid, orientations, orient_weight = lax.optimization_barrier((mid, orientations, orient_weight))
    live_slots = jnp.arange(slots) < box_counts[0, 0]
    matches = orientations[0, 0][:, :, None] == jnp.arange(R)[None, None, :]
    multiplicity = jnp.sum(
        jnp.where(matches, orient_weight[0, 0][:, :, None].astype(jnp.float32), 0.0), axis=1
    )
    multiplicity = jnp.where(live_slots[:, None], multiplicity, 0.0).astype(jnp.bfloat16)
    parts = 2
    mine = pl.pallas_call(
        join_kernel,
        out_shape=[jax.ShapeDtypeStruct((slots // parts, F + R + 128), jnp.bfloat16)] * parts,
        scratch_shapes=[pltpu.VMEM((slots, F), jnp.float32)],
        compiler_params=params,
        name="join",
    )(mid, from_first, from_second, multiplicity)
    return gather_score(mine, reference_bank)


def solution(mesh):
    in_specs = (
        P("tile", "bank", None),
        P(None, "tile", "bank", None),
        P("tile", "bank"),
        P("tile", "bank", None, None),
        P("tile", "bank", None, None),
        P("bank", None, None),
    )
    out_specs = (P("bank", None, None), P("bank", None))
    return jax.shard_map(body, mesh=mesh, in_specs=in_specs, out_specs=out_specs, check_vma=False)
```

```python
import functools

import jax
import jax.numpy as jnp
import numpy as np
from jax import lax
from jax.experimental import pallas as pl
from jax.experimental.pallas import tpu as pltpu
from jax.sharding import PartitionSpec as P

B = 96
L = 16
R = 256
F = L * L * L
HALF = B // 2
TERMS = L // 2
EPSILON = 1e-06
MIB = 1024 * 1024


def waves(count):
    steps = 2.0 * np.pi * np.outer(np.arange(TERMS + 1), np.arange(count)) / B
    return np.cos(steps) / np.sqrt(B), np.sin(steps) / np.sqrt(B)


def depth_tables(depth):
    cos, sin = waves(depth)
    first = np.concatenate([cos, sin[1:TERMS]], axis=0)
    second = np.concatenate([sin, -cos[1:TERMS]], axis=0)
    repeat = 128 // L
    return (
        np.tile(first.T, (1, repeat)).astype(np.float32),
        np.tile(second.T, (1, repeat)).astype(np.float32),
    )


def plane_table(wide, high):
    cos_x, sin_x = waves(wide)
    cos_y, sin_y = waves(high)
    along_x = np.concatenate([cos_x, sin_x[1:]], axis=0)
    along_y = np.concatenate([cos_y[1:], sin_y[1:]], axis=0)
    main = np.einsum("ax,by->abxy", along_x, along_y).reshape(-1, wide * high)
    order = np.concatenate([along_x[1:], along_x[:1]], axis=0)
    flat = np.einsum("ax,y->axy", order, cos_y[0]).reshape(-1, wide * high)
    rows = np.concatenate([main, flat], axis=0)
    pad = -rows.shape[0] % 16
    return np.concatenate([rows, np.zeros((pad, rows.shape[1]))], axis=0).astype(np.float32)


def spread(origin_ref, corner_refs, lanes):
    slots = corner_refs[0].shape[3]
    box = lax.broadcasted_iota(jnp.int32, (slots, lanes), 0)
    lane = lax.broadcasted_iota(jnp.int32, (slots, lanes), 1)
    row = lax.broadcasted_iota(jnp.int32, (8, slots), 0)
    origin = jnp.where(row == 0, origin_ref[0], jnp.where(row == 1, origin_ref[1], 0))
    total = jnp.zeros((8, lanes), jnp.float32)
    for k, corner_ref in enumerate(corner_refs):
        corners = jnp.zeros((8, slots), jnp.int32)
        for axis in range(3):
            corners = jnp.where(row == axis, corner_ref[axis, 0], corners)
        corners = (corners - origin).astype(jnp.float32).astype(jnp.bfloat16)
        pick = jnp.where(lane // L == box + k * slots, 1.0, 0.0).astype(jnp.bfloat16)
        total += jnp.dot(corners, pick, preferred_element_type=jnp.float32)
    return total


def turns(terms, shift):
    turn = (terms * shift).astype(jnp.int32)
    turn = lax.rem(turn, B)
    angle = turn.astype(jnp.float32) * (2.0 * np.pi / B)
    return jnp.cos(angle), jnp.sin(angle)


def prepare(origin_ref, corner_refs, first_ref, second_ref, depth_ref, high_ref, where_ref):
    depth, lanes = depth_ref.shape
    where = spread(origin_ref, corner_refs, lanes)
    where_ref[...] = where
    start_y, start_z = where[1:2], where[2:3]
    lane = lax.rem(lax.broadcasted_iota(jnp.int32, (1, lanes), 1), L)
    term = jnp.where(lane <= TERMS, lane, lane - TERMS).astype(jnp.float32)
    cos, sin = turns(term, start_z)
    copies = lanes // first_ref.shape[1]
    first = jnp.concatenate([first_ref[...]] * copies, axis=1)
    second = jnp.concatenate([second_ref[...]] * copies, axis=1)
    z = lax.broadcasted_iota(jnp.int32, (depth, lanes), 0).astype(jnp.float32) - start_z
    table = jnp.where((z >= 0) & (z < B), first * cos + second * sin, 0.0)
    depth_ref[...] = table.astype(jnp.bfloat16)
    y = lax.broadcasted_iota(jnp.int32, high_ref.shape, 0).astype(jnp.float32) - start_y
    high_ref[...] = jnp.where((y >= 0) & (y < B), 1.0, 0.0)


def block_modes(voxels, at_x, turn, start_x, depth_ref, high_ref, part_ref, plane_ref):
    count, high, depth = voxels.shape
    offset = at_x - start_x
    rows = voxels.reshape(count * high, depth)
    first = jnp.dot(rows, depth_ref[...], preferred_element_type=jnp.float32)
    for x in range(count):
        at = offset + float(x)
        live = high_ref[...] * jnp.where((at >= 0) & (at < B), 1.0, 0.0)
        kept = first[x * high : (x + 1) * high] * live
        part_ref[pl.ds(x * high, high), :] = kept.astype(jnp.bfloat16)
    length = count * high
    total = jnp.dot(
        plane_ref[:, :length], part_ref[:length], preferred_element_type=jnp.float32
    )
    return total if turn is None else moved(total, turn)


def turn_of(at_x):
    angles = 2.0 * np.pi * np.arange(1, TERMS + 1) * at_x / B
    return [float(c) for c in np.cos(angles)], [float(s) for s in np.sin(angles)]


def either(flag, one, other):
    return tuple([jnp.where(flag, a, b) for a, b in zip(u, v)] for u, v in zip(one, other))


def moved(total, turn):
    group, blocks = 2 * TERMS, 2 * TERMS + 1
    rows = [total[a * group : (a + 1) * group] for a in range(blocks)]
    main = blocks * group
    flat_cos, flat_sin = total[main : main + TERMS], total[main + TERMS : main + group]
    out = list(rows)
    term = lax.broadcasted_iota(jnp.int32, flat_cos.shape, 0)
    flat_c, flat_s = jnp.zeros_like(flat_cos), jnp.zeros_like(flat_cos)
    for j, (c, s) in enumerate(zip(*turn)):
        out[1 + j] = rows[1 + j] * c - rows[1 + TERMS + j] * s
        out[1 + TERMS + j] = rows[1 + j] * s + rows[1 + TERMS + j] * c
        flat_c = jnp.where(term == j, c, flat_c)
        flat_s = jnp.where(term == j, s, flat_s)
    out += [
        flat_cos * flat_c - flat_sin * flat_s,
        flat_cos * flat_s + flat_sin * flat_c,
        total[main + group :],
    ]
    return jnp.concatenate(out, axis=0)


def near_kernel(
    origin_ref, first_pick_ref, pick_ref, second_pick_ref, first_ref, second_ref, volume_ref, plane_ref,
    total_ref, depth_ref, high_ref, where_ref, part_ref,
):
    corner_refs = (first_pick_ref, pick_ref, second_pick_ref)
    prepare(origin_ref, corner_refs, first_ref, second_ref, depth_ref, high_ref, where_ref)
    start_x = where_ref[0:1]
    unit = part_ref.shape[0] // volume_ref.shape[1]
    for x in range(0, volume_ref.shape[0], unit):
        added = block_modes(
            volume_ref[x : x + unit], float(x), turn_of(x) if x else None, start_x,
            depth_ref, high_ref, part_ref, plane_ref,
        )
        total_ref[...] = added if x == 0 else total_ref[...] + added


def rotate(total, start_x, start_y):
    lanes = total.shape[1]
    term = (lax.broadcasted_iota(jnp.int32, (TERMS, lanes), 0) + 1).astype(jnp.float32)
    cos_x, sin_x = turns(term, start_x)
    cos_y, sin_y = turns(term, start_y)
    blocks = 2 * TERMS + 1
    main = blocks * 2 * TERMS
    flat_cos = total[main : main + TERMS]
    flat_sin = total[main + TERMS : main + 2 * TERMS]
    flat_zero = total[main + 2 * TERMS : main + 2 * TERMS + 1]
    flats = (
        [flat_zero]
        + [flat_cos[j : j + 1] for j in range(TERMS)]
        + [flat_sin[j : j + 1] for j in range(TERMS)]
    )
    last = lax.broadcasted_iota(jnp.int32, (TERMS, lanes), 0) == TERMS - 1
    turned = []
    for a in range(blocks):
        cos = total[a * 2 * TERMS : a * 2 * TERMS + TERMS]
        sin = total[a * 2 * TERMS + TERMS : (a + 1) * 2 * TERMS]
        low = cos * cos_y + sin * sin_y
        high = sin * cos_y - cos * sin_y
        turned.append((low, jnp.where(last, flats[a], high)))
    rows = [None] * (2 * TERMS)
    rows[0] = turned[0]
    for j in range(1, TERMS + 1):
        c, s = cos_x[j - 1 : j], sin_x[j - 1 : j]
        cos, sin = turned[j], turned[TERMS + j]
        rows[j] = tuple(u * c + v * s for u, v in zip(cos, sin))
        if j < TERMS:
            rows[TERMS + j] = tuple(v * c - u * s for u, v in zip(cos, sin))
    return jnp.concatenate([half for pair in rows for half in pair], axis=0)


def far_kernel(
    side_ref, depth_ref, high_ref, where_ref, first_halo_ref, second_halo_ref, plane_ref, near_ref,
    first_out_ref, own_ref, second_out_ref, part_ref, total_ref, *, wide,
):
    start_x = where_ref[0:1]
    total_ref[...] = near_ref[...]
    even = side_ref[0] == 0
    below, above = turn_of(-HALF), turn_of(wide)
    sides = (
        (first_halo_ref, jnp.where(even, wide, -HALF), either(even, above, below)),
        (second_halo_ref, jnp.where(even, -HALF, wide), either(even, below, above)),
    )
    for voxels_ref, at_x, turn in sides:
        total_ref[...] += block_modes(
            voxels_ref[...], at_x.astype(jnp.float32), turn, start_x,
            depth_ref, high_ref, part_ref, plane_ref,
        )
    rows = rotate(total_ref[...], start_x, where_ref[1:2])
    width = own_ref.shape[1]
    first_out_ref[...] = rows[:, :width].astype(jnp.bfloat16)
    own_ref[...] = rows[:, width : 2 * width]
    second_out_ref[...] = rows[:, 2 * width :].astype(jnp.bfloat16)


def join_kernel(own_ref, left_ref, right_ref, multiplicity_ref, *refs):
    outs, wide_ref = refs[:-1], refs[-1]
    total = own_ref[...] + left_ref[...].astype(jnp.float32) + right_ref[...].astype(jnp.float32)
    total = total.astype(jnp.bfloat16)
    rows, lanes = total.shape
    slots, group = lanes // L, rows // L

    def grid_of(shape, axis):
        return lax.broadcasted_iota(jnp.int32, shape, axis)

    def ones_where(flag):
        return jnp.where(flag, 1.0, 0.0).astype(jnp.bfloat16)

    square = (slots * group, lanes)
    mine = ones_where(grid_of(square, 0) // group == grid_of(square, 1) // L)
    square = (lanes, L * L)
    tiled = ones_where(lax.rem(grid_of(square, 0), L) == lax.rem(grid_of(square, 1), L))
    square = (slots * group, L * L)
    place = lax.rem(grid_of(square, 0), group) + 1
    place = jnp.where(place == group, 0, place)
    keep = ones_where(place == grid_of(square, 1) // L)
    square = (slots, slots * group)
    sums = ones_where(grid_of(square, 1) // group == grid_of(square, 0))
    copies = jnp.concatenate(
        [
            jnp.concatenate([total[a * group : (a + 1) * group]] * slots, axis=0) * mine
            for a in range(L)
        ],
        axis=0,
    )
    placed = jnp.dot(copies, tiled, preferred_element_type=jnp.float32).astype(jnp.bfloat16)
    flat = jnp.concatenate(
        [placed[a * rows : (a + 1) * rows] * keep for a in range(L)], axis=1
    )
    wide_ref[...] = jnp.dot(sums, flat, preferred_element_type=jnp.float32)
    wide = wide_ref[...]
    norm = jnp.sqrt(jnp.mean(wide * wide, axis=1, keepdims=True) + EPSILON)
    high = norm.astype(jnp.bfloat16).astype(jnp.float32)
    tail = lax.broadcasted_iota(jnp.int32, (slots, 128), 1)
    tail = jnp.where(tail == 0, high, jnp.where(tail == 1, norm - high, 0.0))
    row = jnp.concatenate([wide, multiplicity_ref[...].astype(jnp.float32), tail], axis=1)
    for k, out_ref in enumerate(outs):
        count = out_ref.shape[0]
        out_ref[...] = row[k * count : (k + 1) * count].astype(jnp.bfloat16)


def block_copies(blocks, rows_ref, tail_ref, sems):
    copies, at = [], 0
    for k, block in enumerate(blocks):
        count = block.shape[0]
        place = pl.ds(at, count)
        copies.append(
            pltpu.make_async_copy(block.at[:, pl.ds(0, F)], rows_ref.at[place], sems.at[2 * k])
        )
        if tail_ref is not None:
            copies.append(
                pltpu.make_async_copy(
                    block.at[:, pl.ds(F, block.shape[1] - F)], tail_ref.at[place], sems.at[2 * k + 1]
                )
            )
        at += count
    return copies


def read_tail(bank_ref, tail, tail_ref, multiplicity_ref, orients):
    tail_ref[...] = tail.astype(jnp.float32).T
    start = pl.multiple_of(bank_ref[0] * orients, orients)
    norm = tail_ref[R : R + 1, :] + tail_ref[R + 1 : R + 2, :]
    multiplicity_ref[...] = tail_ref[pl.ds(start, orients), :] / (F * norm)


def inverse_norms(bank_rows):
    wide = bank_rows.astype(jnp.float32)
    return 1.0 / jnp.sqrt(jnp.mean(wide * wide, axis=1, keepdims=True) + EPSILON)


def weigh(bank_rows, inverse, rows, multiplicity, count):
    scores = lax.dot_general(
        bank_rows, rows, (((1,), (1,)), ((), ())), preferred_element_type=jnp.float32
    )
    multiplicity = jnp.concatenate([multiplicity] * count, axis=0)
    return (multiplicity * jnp.maximum(scores * inverse, 0.0)).astype(jnp.bfloat16)


def weigh_kernel(index_ref, *refs, blocks, known):
    sources, bank_ref = refs[:blocks], refs[blocks]
    if known:
        norms_ref, out_ref = refs[blocks + 1 : blocks + 3]
    else:
        out_ref, norms_ref = refs[blocks + 1 : blocks + 3]
    rows_ref, tail_ref, turned_ref, multiplicity_ref, sems = refs[blocks + 3 :]
    count, orients, width = bank_ref.shape

    @pl.when(pl.program_id(0) == 0)
    def _():
        copies = block_copies(sources, rows_ref, tail_ref, sems)
        for copy in copies:
            copy.start()
        for copy in copies:
            copy.wait()
        read_tail(index_ref, tail_ref[...], turned_ref, multiplicity_ref, orients)

    bank = bank_ref[...].reshape(count * orients, width)
    if known:
        inverse = norms_ref[...].reshape(count * orients, norms_ref.shape[2])[:, :1]
    else:
        inverse = inverse_norms(bank)
        norms_ref[...] = jnp.broadcast_to(inverse, (count * orients, norms_ref.shape[2])).reshape(
            norms_ref.shape
        )
    weights = weigh(bank, inverse, rows_ref[...], multiplicity_ref[...], count)
    out_ref[...] = weights.reshape(out_ref.shape)


def sum_kernel(index_ref, *refs, early, blocks, late, group):
    parts, sources = refs[:early], refs[early : early + blocks]
    norms_ref, bank_ref, out_ref, sums_ref = refs[early + blocks : early + blocks + 4]
    rows_ref, last_ref, tail_ref, turned_ref, multiplicity_ref, weights_ref, sems, last_sems = refs[
        early + blocks + 4 :
    ]
    count, orients, width = out_ref.shape
    boxes, last = rows_ref.shape[0], last_ref.shape[0]
    step = pl.program_id(0)

    @pl.when(step == 0)
    def _():
        copies = block_copies(sources, rows_ref, None, sems)
        urgent = block_copies(sources[blocks - late :], last_ref, tail_ref, last_sems)
        for copy in urgent + copies:
            copy.start()
        for copy in urgent:
            copy.wait()
        read_tail(index_ref, tail_ref[...], turned_ref, multiplicity_ref, orients)
        for c in range(0, bank_ref.shape[0], group):
            bank = bank_ref[c : c + group].reshape(group * orients, width)
            inverse = norms_ref[c : c + group].reshape(group * orients, norms_ref.shape[2])[:, :1]
            weights = weigh(bank, inverse, last_ref[...], multiplicity_ref[...], group)
            weights_ref[c : c + group] = weights.reshape(group, orients, last)
        for copy in copies:
            copy.wait()

    known = [part[...].reshape(count * orients, part.shape[2]) for part in parts]
    at = pl.multiple_of(step * count, count)
    known.append(weights_ref[pl.ds(at, count)].reshape(count * orients, last))
    weights = jnp.concatenate(known, axis=1)
    total = jnp.dot(weights, rows_ref[...], preferred_element_type=jnp.float32)
    out_ref[...] = total.reshape(out_ref.shape)
    ones = jnp.ones((8, boxes), jnp.bfloat16)
    sums = lax.dot_general(
        ones, weights, (((1,), (1,)), ((), ())), preferred_element_type=jnp.float32
    )
    for c in range(count):
        sums_ref[pl.ds(step * count + c, 1), :] = sums[:1, c * orients : (c + 1) * orients]


def score_plain(rows, bank):
    local_rows = bank.shape[0]
    start = F + lax.axis_index("bank") * local_rows
    multiplicity = lax.dynamic_slice_in_dim(rows, start, local_rows, 1).astype(jnp.float32)
    norm = rows[:, F + R].astype(jnp.float32) + rows[:, F + R + 1].astype(jnp.float32)
    features = rows[:, :F]
    scores = jnp.einsum("if,rcf->irc", features, bank, preferred_element_type=jnp.float32)
    wide = bank.astype(jnp.float32)
    bank_norm = jnp.sqrt(jnp.mean(wide * wide, axis=2) + EPSILON)
    correl = scores / (F * norm[:, None, None] * bank_norm[None])
    weights = (multiplicity[:, :, None] * jnp.maximum(correl, 0.0)).astype(jnp.bfloat16)
    class_sums = jnp.einsum("irc,if->rcf", weights, features, preferred_element_type=jnp.float32)
    return class_sums, jnp.sum(weights.astype(jnp.float32), axis=0)


def exchange(value, axis, first):
    count = lax.axis_size(axis)
    pairs = []
    for i in range(0 if first else 1, count - 1, 2):
        pairs += [(i, i + 1), (i + 1, i)]
    return lax.ppermute(value, axis, pairs)


def gather_score(mine, reference_bank):
    tiles, banks = lax.axis_size("tile"), lax.axis_size("bank")
    local_rows, classes, width = reference_bank.shape
    boxes = tiles * banks * sum(part.shape[0] for part in mine)
    if banks != 4 or tiles & (tiles - 1) or tiles < 4 or boxes > 1024 or classes % 5:
        rows = jnp.concatenate(mine, axis=0)
        for axis in ("bank", "tile"):
            rows = lax.all_gather(rows, axis, axis=0, tiled=True)
        return score_plain(rows, reference_bank)
    bank = jnp.transpose(reference_bank, (1, 0, 2))
    early, late = mine

    def along_x(value):
        return lax.ppermute(value, "bank", [(0, 1), (1, 0), (2, 3), (3, 2)])

    def along_y(value):
        return lax.ppermute(value, "bank", [(0, 2), (2, 0), (1, 3), (3, 1)])

    def swap(*values):
        return [lax.ppermute(value, "tile", [(i, i ^ 1) for i in range(tiles)]) for value in values]

    def line_of(part):
        others = [
            lax.ppermute(part, "tile", [(i, i ^ by) for i in range(tiles)])
            for by in range(2, tiles, 2)
        ]
        return jnp.concatenate([part] + others, axis=0)

    def with_swap(*values):
        joined = jnp.concatenate(values, axis=0) if len(values) > 1 else values[0]
        return [*values, *swap(joined)]

    early_line = line_of(early)
    late, early_line = lax.optimization_barrier((late, early_line))
    from_x, from_y = along_x(early_line), along_y(early_line)
    late_line = line_of(late)
    half = early_line.shape[0] // 2
    to_x = jnp.concatenate([from_y[half:], late_line], axis=0)
    to_y = jnp.concatenate([from_x[:half], late_line], axis=0)
    known = with_swap(early_line, from_x, from_y)
    to_x, to_y = lax.optimization_barrier((to_x, to_y))
    next_x, next_y = along_x(to_x), along_y(to_y)
    known += with_swap(to_x[half:])
    first, norms = weigh_blocks(known, bank)
    first, next_x, next_y = lax.optimization_barrier((first, next_x, next_y))
    last_x, last_y = along_x(next_y[half + half :]), along_y(next_x[half : half + half])
    late = with_swap(next_x, next_y) + with_swap(last_x, last_y)
    out, sums = sum_blocks([first], known, late, norms, bank)
    return jnp.transpose(out, (1, 0, 2)), jnp.transpose(sums, (1, 0))


CLASSES = 5


def bank_index():
    return lax.axis_index("bank").astype(jnp.int32)[None]


def weigh_blocks(blocks, bank, norms=None):
    classes, orients, width = bank.shape
    boxes = sum(block.shape[0] for block in blocks)
    tail = blocks[0].shape[1] - F
    known = norms is not None
    norm_spec = pl.BlockSpec((CLASSES, orients, 128), lambda i: (i, 0, 0))
    out_spec = pl.BlockSpec((CLASSES, orients, boxes), lambda i: (i, 0, 0))
    out_shape = jax.ShapeDtypeStruct((classes, orients, boxes), jnp.bfloat16)
    norm_shape = jax.ShapeDtypeStruct((classes, orients, 128), jnp.float32)
    return pl.pallas_call(
        functools.partial(weigh_kernel, blocks=len(blocks), known=known),
        grid=(classes // CLASSES,),
        in_specs=[pl.BlockSpec(memory_space=pltpu.SMEM)]
        + [pl.BlockSpec(memory_space=pl.ANY)] * len(blocks)
        + [pl.BlockSpec((CLASSES, orients, width), lambda i: (i, 0, 0))]
        + ([norm_spec] if known else []),
        out_specs=out_spec if known else [out_spec, norm_spec],
        out_shape=out_shape if known else [out_shape, norm_shape],
        scratch_shapes=[
            pltpu.VMEM((boxes, F), jnp.bfloat16),
            pltpu.VMEM((boxes, tail), jnp.bfloat16),
            pltpu.VMEM((tail, boxes), jnp.float32),
            pltpu.VMEM((orients, boxes), jnp.float32),
            pltpu.SemaphoreType.DMA((2 * len(blocks),)),
        ],
        compiler_params=pltpu.CompilerParams(vmem_limit_bytes=18 * MIB),
        cost_estimate=pl.CostEstimate(
            flops=boxes * classes * orients * width // 8,
            bytes_accessed=classes * orients * width // 8,
            transcendentals=0,
        ),
        name="weigh",
    )(bank_index(), *blocks, bank, *([norms] if known else []))


def sum_blocks(parts, blocks, late, norms, bank):
    classes, orients, width = bank.shape
    blocks = blocks + late
    boxes = sum(block.shape[0] for block in blocks)
    last = sum(block.shape[0] for block in late)
    tail = blocks[0].shape[1] - F
    vmem = pl.BlockSpec(memory_space=pltpu.VMEM)
    return pl.pallas_call(
        functools.partial(
            sum_kernel, early=len(parts), blocks=len(blocks), late=len(late), group=CLASSES
        ),
        grid=(classes // CLASSES,),
        in_specs=[pl.BlockSpec(memory_space=pltpu.SMEM)]
        + [pl.BlockSpec((CLASSES, orients, part.shape[2]), lambda i: (i, 0, 0)) for part in parts]
        + [pl.BlockSpec(memory_space=pl.ANY)] * len(blocks)
        + [vmem, vmem],
        out_specs=[
            pl.BlockSpec((CLASSES, orients, width), lambda i: (i, 0, 0)),
            pl.BlockSpec((classes, orients), lambda i: (0, 0)),
        ],
        out_shape=[
            jax.ShapeDtypeStruct((classes, orients, width), jnp.float32),
            jax.ShapeDtypeStruct((classes, orients), jnp.float32),
        ],
        scratch_shapes=[
            pltpu.VMEM((boxes, F), jnp.bfloat16),
            pltpu.VMEM((last, F), jnp.bfloat16),
            pltpu.VMEM((last, tail), jnp.bfloat16),
            pltpu.VMEM((tail, last), jnp.float32),
            pltpu.VMEM((orients, last), jnp.float32),
            pltpu.VMEM((classes, orients, last), jnp.bfloat16),
            pltpu.SemaphoreType.DMA((2 * len(blocks),)),
            pltpu.SemaphoreType.DMA((2 * len(late),)),
        ],
        compiler_params=pltpu.CompilerParams(vmem_limit_bytes=34 * MIB),
        cost_estimate=pl.CostEstimate(
            flops=2 * boxes * classes * orients * width,
            bytes_accessed=4 * classes * orients * width,
            transcendentals=0,
        ),
        name="class_sums",
    )(bank_index(), *parts, *blocks, norms, bank)


def body(volume, pick_list, box_counts, orientations, orient_weight, reference_bank):
    wide, high, depth = volume.shape
    slots = pick_list.shape[3]
    tile, bank = lax.axis_index("tile"), lax.axis_index("bank")
    side = lax.rem(tile, 2).astype(jnp.int32)
    rest = wide - HALF
    to_first = lax.dynamic_slice_in_dim(volume, jnp.where(side == 0, rest, 0), HALF, 0)
    to_second = lax.dynamic_slice_in_dim(volume, jnp.where(side == 0, 0, rest), HALF, 0)
    first_halo = exchange(to_first, "tile", True)
    second_halo = exchange(to_second, "tile", False)
    picks, first_halo = lax.optimization_barrier((pick_list, first_halo))
    first_picks, second_picks = exchange(picks, "bank", True), exchange(picks, "bank", False)
    origin = jnp.stack([tile * wide + HALF, bank * high + HALF]).astype(jnp.int32)

    first, second = depth_tables(depth)
    plane = jnp.asarray(plane_table(HALF, high), jnp.bfloat16)
    modes, lanes = plane.shape[0], 3 * slots * L
    unit = 32

    params = pltpu.CompilerParams(vmem_limit_bytes=20 * MIB)
    vmem = pl.BlockSpec(memory_space=pltpu.VMEM)
    smem = pl.BlockSpec(memory_space=pltpu.SMEM)
    near, *tables = pl.pallas_call(
        near_kernel,
        in_specs=[smem] + [vmem] * 7,
        out_specs=[vmem] * 4,
        out_shape=[
            jax.ShapeDtypeStruct((modes, lanes), jnp.float32),
            jax.ShapeDtypeStruct((depth, lanes), jnp.bfloat16),
            jax.ShapeDtypeStruct((high, lanes), jnp.float32),
            jax.ShapeDtypeStruct((8, lanes), jnp.float32),
        ],
        scratch_shapes=[pltpu.VMEM((unit * high, lanes), jnp.bfloat16)],
        compiler_params=params,
        cost_estimate=pl.CostEstimate(
            flops=2 * wide * high * lanes * (depth + modes), bytes_accessed=8000000, transcendentals=0
        ),
        name="near_rows",
    )(origin, first_picks, picks, second_picks, first, second, volume, plane)
    for_first, mid, for_second = pl.pallas_call(
        functools.partial(far_kernel, wide=wide),
        in_specs=[smem] + [vmem] * 7,
        out_specs=[vmem] * 3,
        out_shape=[
            jax.ShapeDtypeStruct((L * L, slots * L), jnp.bfloat16),
            jax.ShapeDtypeStruct((L * L, slots * L), jnp.float32),
            jax.ShapeDtypeStruct((L * L, slots * L), jnp.bfloat16),
        ],
        scratch_shapes=[
            pltpu.VMEM((HALF * high, lanes), jnp.bfloat16),
            pltpu.VMEM((modes, lanes), jnp.float32),
        ],
        compiler_params=params,
        name="far_rows",
    )(side[None], *tables, first_halo, second_halo, plane, near)
    from_first, from_second = exchange(for_first, "bank", True), exchange(for_second, "bank", False)

    mid, orientations, orient_weight = lax.optimization_barrier((mid, orientations, orient_weight))
    live_slots = jnp.arange(slots) < box_counts[0, 0]
    matches = orientations[0, 0][:, :, None] == jnp.arange(R)[None, None, :]
    multiplicity = jnp.sum(
        jnp.where(matches, orient_weight[0, 0][:, :, None].astype(jnp.float32), 0.0), axis=1
    )
    multiplicity = jnp.where(live_slots[:, None], multiplicity, 0.0).astype(jnp.bfloat16)
    parts = 2
    mine = pl.pallas_call(
        join_kernel,
        out_shape=[jax.ShapeDtypeStruct((slots // parts, F + R + 128), jnp.bfloat16)] * parts,
        scratch_shapes=[pltpu.VMEM((slots, F), jnp.float32)],
        compiler_params=params,
        name="join",
    )(mid, from_first, from_second, multiplicity)
    return gather_score(mine, reference_bank)


def solution(mesh):
    in_specs = (
        P("tile", "bank", None),
        P(None, "tile", "bank", None),
        P("tile", "bank"),
        P("tile", "bank", None, None),
        P("tile", "bank", None, None),
        P("bank", None, None),
    )
    out_specs = (P("bank", None, None), P("bank", None))
    return jax.shard_map(body, mesh=mesh, in_specs=in_specs, out_specs=out_specs, check_vma=False)
```
